32 devices in a mesh: dp: 8 (over z, x), expert: 4 (over y, core).
Axes of the slice: x: 2, y: 2, z: 4, core: 2. Of those that a mesh axis runs over, the one named last changes fastest.
Arguments:
- grads: bfloat16 [8, 4096, 3072], P('dp', None, 'expert'), parts along dimension 2, may hold values from -16 to 16
- error: bfloat16 [8, 4096, 3072], P('dp', None, 'expert'), parts along dimension 2, may hold values from -6 to 6
- q_start: float32 [3072, 32], P('expert'), parts along dimension 0, may hold values from -6 to 6
- bucket: float32 [8, 262144], P('dp', 'expert'), parts along dimension 1, may hold values from -6 to 6
Outputs:
- update: float32 [4096, 3072], P(None, 'expert'), parts along dimension 1
- new_error: bfloat16 [8, 4096, 3072], P('dp', None, 'expert'), parts along dimension 2
- bucket_mean: float32 [262144], P(('expert', 'dp')), parts along dimension 0
The draws below stay inside these ranges and needn't reach their ends.
There are 4 independent parts, one for each index of `expert`. The reference program is written for one: setup_inputs(seed, part) draws one part's arguments, and reference() takes and returns one part's arrays. A program takes and returns all parts, laid end to end along the dimension named above; each array names one. Nothing has to cross between parts.
All inputs are finite; a program needn't handle non-finite values.
Results may differ from the reference program's by a relative error of at most 0.02.
Values may be sent and summed in bfloat16 or wider, within the bound.
No kernel may reach another device: no remote copies, remote signals or barrier semaphores. Data moves between devices by JAX's collectives and lax.ppermute only.
A program may use at most 128 MiB of HBM per device.

```python
import jax
import jax.numpy as jnp
from jax import lax

D = 4096
H = 768
R = 32
ITERS = 2
BUCKET = 65536
REPLICAS = 8
N_DP = 8


def raised(values, key, source, target, parts, factor):
    owner, partner = [(jnp.arange(values.shape[axis_at]) // (values.shape[axis_at] // parts)).reshape([-1 if axis == axis_at else 1 for axis in range(values.ndim)]) for axis_at in (source, target)]
    chosen = jax.random.permutation(key, parts)[partner]
    strong = (owner == chosen) | (owner == (partner + parts // 2) % parts)
    return jnp.where(strong, factor * values, values)


def block_scale(stream_key, dims, split, low, top_value):
    factor_of, own = 1.0, jax.random.fold_in(stream_key, 6)
    for position, shards_of in split:
        heights = jnp.exp(jax.random.uniform(jax.random.fold_in(own, position), (shards_of,), jnp.float32, low / len(split), top_value / len(split)))
        factor_of = factor_of * jnp.repeat(heights, dims[position] // shards_of).reshape([-1 if axis == position else 1 for axis in range(len(dims))])
    return factor_of


def gaussian(rng, extent, scale, bound, cuts=(), held_as=jnp.bfloat16):
    values = scale * jax.random.normal(rng, extent, jnp.float32)
    if cuts:
        values = values * block_scale(rng, extent, cuts, -0.22, 0.18)
    return jnp.clip(values, -bound, bound).astype(held_as)


def heavy_noise(key, extent, scale, most, cuts, heavy, kind=jnp.bfloat16):
    drawn = scale * jax.random.normal(key, extent, jnp.float32)
    if cuts:
        drawn = drawn * block_scale(key, extent, cuts, -0.22, 0.18)
    return jnp.clip(raised(drawn, jax.random.fold_in(key, 3), *heavy), -most, most).astype(kind)


def setup_inputs(seed: int = 0, part: int = 0) -> dict:
    key_list = jax.random.split(jax.random.key(seed), 5)
    own_keys = jax.random.split(jax.random.fold_in(key_list[4], part), 5)
    return {
        "grads": gaussian(own_keys[0], (REPLICAS, D, H), 4.0, 16.0, ((0, 8),)),
        "error": gaussian(own_keys[1], (REPLICAS, D, H), 1.0, 6.0, ((0, 8),)),
        "q_start": gaussian(own_keys[2], (H, R), 1.0, 6.0, (), jnp.float32),
        "bucket": heavy_noise(own_keys[3], (REPLICAS, BUCKET), 1.0, 6.0, ((0, 8),), (0, 1, 8, 2.0), jnp.float32),
    }


def reference(grads, error, q_start, bucket):
    compensated = (grads.astype(jnp.float32) + error.astype(jnp.float32)).astype(jnp.bfloat16)
    whole = compensated.astype(jnp.float32)
    factor_q = q_start
    p_half = None
    for step in range(ITERS):
        q_half = factor_q.astype(jnp.bfloat16).astype(jnp.float32)
        factor_p = jnp.einsum('rdh,hk->dk', whole, q_half) / N_DP
        gram = jnp.dot(factor_p.T, factor_p, precision=lax.Precision.HIGHEST)
        lower = jnp.linalg.cholesky(gram)
        p_hat = jax.scipy.linalg.solve_triangular(lower, factor_p.T, lower=True).T
        p_half = p_hat.astype(jnp.bfloat16).astype(jnp.float32)
        factor_q = jnp.einsum('rdh,dk->hk', whole, p_half) / N_DP
        if step + 1 < ITERS:
            factor_q = factor_q / jnp.sqrt(lax.optimization_barrier(jnp.sum(factor_q * factor_q, axis=0, keepdims=True)) + 1e-06)
    update = jnp.dot(p_half, factor_q.T, precision=lax.Precision.HIGHEST)
    new_error = (whole - update[None]).astype(jnp.bfloat16)
    bucket_mean = lax.optimization_barrier(jnp.sum(bucket, axis=0)) / N_DP
    return (update, new_error, bucket_mean)
```

```python
import jax
import jax.numpy as jnp
from jax import lax
from jax.sharding import PartitionSpec as P

ITERS = 2


def shift(value, by, size):
    return lax.ppermute(value, "dp", [(i, (i + by) % size) for i in range(size)])


def reduce_scatter(chunks, size):
    me = lax.axis_index("dp")
    pieces = [
        lax.dynamic_index_in_dim(chunks, (me + by) % size, 0, keepdims=False) for by in range(size)
    ]
    arrived = [shift(pieces[by].astype(jnp.bfloat16), by, size) for by in range(1, size)]
    total = pieces[0].astype(jnp.float32)
    for piece in arrived:
        total = total + piece.astype(jnp.float32)
    return total


def all_gather(share, size):
    me = lax.axis_index("dp")
    arrived = [share] + [shift(share, by, size) for by in range(1, size)]
    stacked = jnp.stack(arrived[::-1])
    return jnp.roll(stacked, me + 1, axis=0)


def on_device(grads, error, q_start, bucket):
    replicas = lax.axis_size("dp")
    compensated = (grads[0].astype(jnp.float32) + error[0].astype(jnp.float32)).astype(jnp.bfloat16)
    rows, hidden = compensated.shape
    rank = q_start.shape[1]
    bucket_share = reduce_scatter(bucket[0].reshape(replicas, -1), replicas) / replicas
    factor_q = q_start.T
    p_half = None
    for step in range(ITERS):
        q_half = factor_q.astype(jnp.bfloat16)
        local_p = lax.dot_general(
            q_half, compensated, (((1,), (1,)), ((), ())), preferred_element_type=jnp.float32
        )
        chunks = local_p.reshape(rank, replicas, rows // replicas).transpose(1, 0, 2)
        share = (reduce_scatter(chunks, replicas) / replicas).astype(jnp.bfloat16)
        factor_p = all_gather(share, replicas).transpose(1, 0, 2).reshape(rank, rows)
        gram = lax.dot_general(
            factor_p, factor_p, (((1,), (1,)), ((), ())), preferred_element_type=jnp.float32
        )
        lower = jnp.linalg.cholesky(gram)
        p_half = jax.scipy.linalg.solve_triangular(
            lower, factor_p.astype(jnp.float32), lower=True
        ).astype(jnp.bfloat16)
        local_q = jnp.dot(p_half, compensated, preferred_element_type=jnp.float32)
        chunks = local_q.reshape(rank, replicas, hidden // replicas).transpose(1, 0, 2)
        share = reduce_scatter(chunks, replicas) / replicas
        share = share.astype(jnp.bfloat16)
        factor_q = all_gather(share, replicas).transpose(1, 0, 2).reshape(rank, hidden)
        factor_q = factor_q.astype(jnp.float32)
        if step + 1 < ITERS:
            factor_q = factor_q / jnp.sqrt(
                jnp.sum(factor_q * factor_q, axis=1, keepdims=True) + 1e-06
            )
    update = lax.dot_general(
        p_half.astype(jnp.float32),
        factor_q,
        (((0,), (0,)), ((), ())),
        precision=lax.Precision.HIGHEST,
    )
    new_error = (compensated.astype(jnp.float32) - update).astype(jnp.bfloat16)[None]
    return (update, new_error, bucket_share)


def solution(mesh):
    return jax.shard_map(
        on_device,
        mesh=mesh,
        in_specs=(
            P("dp", None, "expert"),
            P("dp", None, "expert"),
            P("expert", None),
            P("dp", "expert"),
        ),
        out_specs=(P(None, "expert"), P("dp", None, "expert"), P(("expert", "dp"))),
        check_vma=False,
    )
```

```python
import jax
import jax.numpy as jnp
from jax import lax
from jax.sharding import PartitionSpec as P

ITERS = 2


def exchange(chunks):
    return lax.all_to_all(chunks, "dp", split_axis=0, concat_axis=0, tiled=True)


def reduce_scatter(chunks):
    return jnp.sum(exchange(chunks.astype(jnp.bfloat16)).astype(jnp.float32), axis=0)


def all_gather(share, size):
    return exchange(jnp.broadcast_to(share, (size,) + share.shape))


def on_device(grads, error, q_start, bucket):
    replicas = lax.axis_size("dp")
    compensated = (grads[0].astype(jnp.float32) + error[0].astype(jnp.float32)).astype(jnp.bfloat16)
    rows, hidden = compensated.shape
    rank = q_start.shape[1]
    bucket_share = (
        lax.psum_scatter(
            bucket[0].astype(jnp.bfloat16), "dp", scatter_dimension=0, tiled=True
        ).astype(jnp.float32)
        / replicas
    )
    factor_q = q_start.T
    p_half = None
    for step in range(ITERS):
        q_half = factor_q.astype(jnp.bfloat16)
        local_p = lax.dot_general(
            q_half, compensated, (((1,), (1,)), ((), ())), preferred_element_type=jnp.float32
        )
        chunks = local_p.reshape(rank, replicas, rows // replicas).transpose(1, 0, 2)
        share = (reduce_scatter(chunks) / replicas).astype(jnp.bfloat16)
        factor_p = all_gather(share, replicas).transpose(1, 0, 2).reshape(rank, rows)
        gram = lax.dot_general(
            factor_p, factor_p, (((1,), (1,)), ((), ())), preferred_element_type=jnp.float32
        )
        lower = jnp.linalg.cholesky(gram)
        p_half = jax.scipy.linalg.solve_triangular(
            lower, factor_p.astype(jnp.float32), lower=True
        ).astype(jnp.bfloat16)
        local_q = jnp.dot(p_half, compensated, preferred_element_type=jnp.float32)
        chunks = local_q.reshape(rank, replicas, hidden // replicas).transpose(1, 0, 2)
        share = reduce_scatter(chunks) / replicas
        share = share.astype(jnp.bfloat16)
        factor_q = all_gather(share, replicas).transpose(1, 0, 2).reshape(rank, hidden)
        factor_q = factor_q.astype(jnp.float32)
        if step + 1 < ITERS:
            factor_q = factor_q / jnp.sqrt(
                jnp.sum(factor_q * factor_q, axis=1, keepdims=True) + 1e-06
            )
    update = lax.dot_general(
        p_half.astype(jnp.float32),
        factor_q,
        (((0,), (0,)), ((), ())),
        precision=lax.Precision.HIGHEST,
    )
    new_error = (compensated.astype(jnp.float32) - update).astype(jnp.bfloat16)[None]
    return (update, new_error, bucket_share)


def solution(mesh):
    return jax.shard_map(
        on_device,
        mesh=mesh,
        in_specs=(
            P("dp", None, "expert"),
            P("dp", None, "expert"),
            P("expert", None),
            P("dp", "expert"),
        ),
        out_specs=(P(None, "expert"), P("dp", None, "expert"), P(("expert", "dp"))),
        check_vma=False,
    )
```

```python
import functools

import jax
import jax.numpy as jnp
from jax import lax
from jax.experimental import pallas as pl
from jax.experimental.pallas import tpu as pltpu
from jax.sharding import PartitionSpec as P

ITERS = 2
LANES = 128
MIB = 1024 * 1024
CONTRACT_LAST = (((1,), (1,)), ((), ()))
CONTRACT_FIRST = (((0,), (0,)), ((), ()))


def exchange(chunks):
    return lax.all_to_all(chunks, "dp", split_axis=0, concat_axis=0, tiled=True)


def everywhere(share, size):
    return exchange(jnp.broadcast_to(share, (size,) + share.shape))


def store_columns(out_ref, value):
    rank, columns = value.shape
    for tile in range(columns // LANES):
        out_ref[tile * rank : (tile + 1) * rank, :] = value[:, tile * LANES : (tile + 1) * LANES]


def three_parts(value):
    high = value.astype(jnp.bfloat16)
    rest = value - high.astype(jnp.float32)
    middle = rest.astype(jnp.bfloat16)
    low = (rest - middle.astype(jnp.float32)).astype(jnp.bfloat16)
    return high, middle, low


def first_kernel(grads, error, q_start, bucket, compensated, outgoing, q_half):
    @pl.when(pl.program_id(0) == 0)
    def _():
        q_half[...] = q_start[...].T.astype(jnp.bfloat16)

    block = (grads[...].astype(jnp.float32) + error[...].astype(jnp.float32)).astype(jnp.bfloat16)
    compensated[...] = block
    local_p = lax.dot_general(
        q_half[...], block, CONTRACT_LAST, preferred_element_type=jnp.float32
    ).astype(jnp.bfloat16)
    store_columns(outgoing.at[0], local_p)
    outgoing[0, -bucket.shape[1] :, :] = bucket[0].astype(jnp.bfloat16)


def first(grads, error, q_start, bucket, replicas):
    rows, hidden = grads.shape
    rank = q_start.shape[1]
    block = rows // replicas
    tall = block * rank // LANES + bucket.shape[1]
    return pl.pallas_call(
        first_kernel,
        grid=(replicas,),
        in_specs=[
            pl.BlockSpec((block, hidden), lambda s: (s, 0)),
            pl.BlockSpec((block, hidden), lambda s: (s, 0)),
            pl.BlockSpec((hidden, rank), lambda s: (0, 0)),
            pl.BlockSpec((1,) + bucket.shape[1:], lambda s: (s, 0, 0)),
        ],
        out_specs=[
            pl.BlockSpec((block, hidden), lambda s: (s, 0)),
            pl.BlockSpec((1, tall, LANES), lambda s: (s, 0, 0)),
        ],
        out_shape=[
            jax.ShapeDtypeStruct((rows, hidden), jnp.bfloat16),
            jax.ShapeDtypeStruct((replicas, tall, LANES), jnp.bfloat16),
        ],
        scratch_shapes=[pltpu.VMEM((rank, hidden), jnp.bfloat16)],
        compiler_params=pltpu.CompilerParams(vmem_limit_bytes=24 * MIB),
        name="compensate_and_left",
    )(grads, error, q_start, bucket)


def inverse_lower(gram):
    rank = gram.shape[0]
    row = lax.broadcasted_iota(jnp.int32, (rank, 1), 0)
    across = lax.broadcasted_iota(jnp.int32, (rank, 2 * rank), 1)
    down = lax.broadcasted_iota(jnp.int32, (rank, 2 * rank), 0)
    both = jnp.concatenate([jnp.zeros((rank, rank), jnp.float32), gram], axis=1)
    both = jnp.where(across == down, 1.0, both)
    for k in range(rank):
        column = both[:, rank + k : rank + k + 1]
        pivot = both[k : k + 1, rank + k : rank + k + 1]
        factor = jnp.where(row > k, column / pivot, 0.0)
        both = both - factor * both[k : k + 1, :]
    pivots = jnp.sum(jnp.where(across == down + rank, both, 0.0), axis=1, keepdims=True)
    return both[:, :rank] * lax.rsqrt(pivots)


def right_kernel(tiles, parts, arrived, compensated, p_half_out, term, held, sems):
    replicas, tall, _ = arrived.shape
    rank = tall // tiles
    block = tiles * LANES
    size = compensated.shape[0] // parts
    copies = []
    for part in range(parts):
        where = pl.ds(part * size, size)
        copies.append(
            pltpu.make_async_copy(compensated.at[where], held.at[where], sems.at[part])
        )
        copies[-1].start()
    factor_p = jnp.concatenate(
        [
            arrived[s, t * rank : (t + 1) * rank, :]
            for s in range(replicas)
            for t in range(tiles)
        ],
        axis=1,
    )
    gram = lax.dot_general(
        factor_p, factor_p, CONTRACT_LAST, preferred_element_type=jnp.float32
    )
    inverse = inverse_lower(gram)
    stacked = jnp.concatenate(three_parts(inverse), axis=0)
    p_parts = jnp.dot(stacked, factor_p, preferred_element_type=jnp.float32)
    p_hat = p_parts[:rank] + (p_parts[rank : 2 * rank] + p_parts[2 * rank :])
    p_half = p_hat.astype(jnp.bfloat16)
    p_half_out[...] = p_half
    total = None
    for part in range(parts):
        copies[part].wait()
        product = jnp.dot(
            p_half[:, part * size : (part + 1) * size],
            held[part * size : (part + 1) * size, :],
            preferred_element_type=jnp.float32,
        )
        total = product if total is None else total + product
    term[...] = total.astype(jnp.bfloat16)


def right(arrived, compensated, rank):
    rows, hidden = compensated.shape
    tiles = arrived.shape[1] // rank
    parts = 8
    return pl.pallas_call(
        functools.partial(right_kernel, tiles, parts),
        in_specs=[
            pl.BlockSpec(memory_space=pltpu.VMEM),
            pl.BlockSpec(memory_space=pl.ANY),
        ],
        out_specs=[pl.BlockSpec(memory_space=pltpu.VMEM)] * 2,
        out_shape=[
            jax.ShapeDtypeStruct((rank, rows), jnp.bfloat16),
            jax.ShapeDtypeStruct((rank, hidden), jnp.bfloat16),
        ],
        scratch_shapes=[
            pltpu.VMEM((rows, hidden), jnp.bfloat16),
            pltpu.SemaphoreType.DMA((parts,)),
        ],
        compiler_params=pltpu.CompilerParams(vmem_limit_bytes=24 * MIB),
        name="orthogonalize_and_right",
    )(arrived, compensated)


def sum_of_terms(arrived):
    total = arrived[0].astype(jnp.float32)
    for s in range(1, arrived.shape[0]):
        total = total + arrived[s].astype(jnp.float32)
    return total / arrived.shape[0]


def left_kernel(arrived, compensated, outgoing, held, sems):
    replicas = arrived.shape[0]
    block = compensated.shape[0] // replicas
    copies = []
    for s in range(replicas):
        where = pl.ds(s * block, block)
        copies.append(pltpu.make_async_copy(compensated.at[where], held.at[where], sems.at[s]))
        copies[-1].start()
    factor_q = sum_of_terms(arrived)
    factor_q = factor_q / jnp.sqrt(jnp.sum(factor_q * factor_q, axis=1, keepdims=True) + 1e-06)
    q_half = factor_q.astype(jnp.bfloat16)
    for s in range(replicas):
        copies[s].wait()
        local_p = lax.dot_general(
            q_half,
            held[s * block : (s + 1) * block, :],
            CONTRACT_LAST,
            preferred_element_type=jnp.float32,
        )
        store_columns(outgoing.at[s], local_p.astype(jnp.bfloat16))


def left(arrived, compensated):
    replicas, rank, _ = arrived.shape
    rows, hidden = compensated.shape
    tall = rows // replicas * rank // LANES
    return pl.pallas_call(
        left_kernel,
        in_specs=[
            pl.BlockSpec(memory_space=pltpu.VMEM),
            pl.BlockSpec(memory_space=pl.ANY),
        ],
        out_specs=pl.BlockSpec(memory_space=pltpu.VMEM),
        out_shape=jax.ShapeDtypeStruct((replicas, tall, LANES), jnp.bfloat16),
        scratch_shapes=[
            pltpu.VMEM((rows, hidden), jnp.bfloat16),
            pltpu.SemaphoreType.DMA((replicas,)),
        ],
        compiler_params=pltpu.CompilerParams(vmem_limit_bytes=24 * MIB),
        name="normalize_and_left",
    )(arrived, compensated)


def last_kernel(arrived, p_half, compensated, update, new_error, q_parts):
    @pl.when(pl.program_id(0) == 0)
    def _():
        factor_q = sum_of_terms(arrived)
        q_parts[...] = jnp.concatenate(three_parts(factor_q), axis=0)

    p_block = p_half[...]
    block = lax.dot_general(
        jnp.concatenate([p_block] * 3, axis=0),
        q_parts[...],
        CONTRACT_FIRST,
        preferred_element_type=jnp.float32,
    )
    update[...] = block
    new_error[...] = (compensated[...].astype(jnp.float32) - block).astype(jnp.bfloat16)


def last(arrived, p_half, compensated, block):
    replicas, rank, hidden = arrived.shape
    rows = compensated.shape[0]
    return pl.pallas_call(
        last_kernel,
        grid=(rows // block,),
        in_specs=[
            pl.BlockSpec(arrived.shape, lambda i: (0, 0, 0)),
            pl.BlockSpec((rank, block), lambda i: (0, i)),
            pl.BlockSpec((block, hidden), lambda i: (i, 0)),
        ],
        out_specs=[
            pl.BlockSpec((block, hidden), lambda i: (i, 0)),
            pl.BlockSpec((block, hidden), lambda i: (i, 0)),
        ],
        out_shape=[
            jax.ShapeDtypeStruct((rows, hidden), jnp.float32),
            jax.ShapeDtypeStruct((rows, hidden), jnp.bfloat16),
        ],
        scratch_shapes=[pltpu.VMEM((3 * rank, hidden), jnp.bfloat16)],
        compiler_params=pltpu.CompilerParams(vmem_limit_bytes=24 * MIB),
        name="update_and_error",
    )(arrived, p_half, compensated)


def on_device(grads, error, q_start, bucket):
    replicas = lax.axis_size("dp")
    rows = grads.shape[1]
    rank = q_start.shape[1]
    bucket = bucket.reshape(replicas, -1, LANES)
    tall = rows // replicas * rank // LANES
    compensated, outgoing = first(grads[0], error[0], q_start, bucket, replicas)
    bucket_share = p_half = term = None
    for step in range(ITERS):
        if step > 0:
            outgoing = left(everywhere(term, replicas), compensated)
        share = jnp.sum(exchange(outgoing).astype(jnp.float32), axis=0) / replicas
        if step == 0:
            bucket_share = share[tall:].reshape(-1)
        factor_p = everywhere(share[:tall].astype(jnp.bfloat16), replicas)
        p_half, term = right(factor_p, compensated, rank)
    update, new_error = last(everywhere(term, replicas), p_half, compensated, 256)
    return (update, new_error[None], bucket_share)


def solution(mesh):
    return jax.shard_map(
        on_device,
        mesh=mesh,
        in_specs=(
            P("dp", None, "expert"),
            P("dp", None, "expert"),
            P("expert", None),
            P("dp", "expert"),
        ),
        out_specs=(P(None, "expert"), P("dp", None, "expert"), P(("expert", "dp"))),
        check_vma=False,
    )
```

```python
import functools

import jax
import jax.numpy as jnp
from jax import lax
from jax.experimental import pallas as pl
from jax.experimental.pallas import tpu as pltpu
from jax.sharding import PartitionSpec as P

ITERS = 2
LANES = 128
MIB = 1024 * 1024
CONTRACT_LAST = (((1,), (1,)), ((), ()))


def exchange(chunks):
    return lax.all_to_all(chunks, "dp", split_axis=0, concat_axis=0, tiled=True)


def everywhere(share, size):
    return exchange(jnp.broadcast_to(share, (size,) + share.shape))


def three_parts(value):
    high = value.astype(jnp.bfloat16)
    rest = value - high.astype(jnp.float32)
    middle = rest.astype(jnp.bfloat16)
    low = (rest - middle.astype(jnp.float32)).astype(jnp.bfloat16)
    return high, middle, low


def store_tiles(outgoing, first_tile, tiles, value):
    rank, columns = value.shape
    for at in range(columns // LANES):
        chunk, tile = divmod(first_tile + at, tiles)
        outgoing[chunk, tile * rank : (tile + 1) * rank, :] = value[:, at * LANES : (at + 1) * LANES]


def first_kernel(
    tiles, piece, ahead, grads, error, q_start, bucket, compensated, outgoing, landed, sems
):
    rows = grads.shape[0]
    pieces = rows // piece
    copies = []
    for i in range(pieces):
        where = pl.ds(i * piece, piece)
        copies.append(
            [
                pltpu.make_async_copy(array.at[where], landed.at[j, where], sems.at[j, i])
                for j, array in enumerate((grads, error))
            ]
        )

    def start(i):
        for copy in copies[i]:
            copy.start()

    for i in range(min(ahead, pieces)):
        start(i)
    q_half = q_start[...].astype(jnp.bfloat16)
    outgoing[:, -bucket.shape[1] :, :] = bucket[...].astype(jnp.bfloat16)
    for i in range(pieces):
        for copy in copies[i]:
            copy.wait()
        if i + ahead < pieces:
            start(i + ahead)
        where = slice(i * piece, (i + 1) * piece)
        block = (
            landed[0, where, :].astype(jnp.float32) + landed[1, where, :].astype(jnp.float32)
        ).astype(jnp.bfloat16)
        compensated[where, :] = block
        local_p = lax.dot_general(q_half, block, CONTRACT_LAST, preferred_element_type=jnp.float32)
        store_tiles(outgoing, i * piece // LANES, tiles, local_p.astype(jnp.bfloat16))


def first(grads, error, q_start, bucket):
    rows, hidden = grads.shape
    rank = q_start.shape[0]
    replicas = bucket.shape[0]
    tiles = rows // replicas // LANES
    piece = 2 * LANES
    tall = tiles * rank + bucket.shape[1]
    in_vmem = pl.BlockSpec(memory_space=pltpu.VMEM)
    in_place = pl.BlockSpec(memory_space=pl.ANY)
    return pl.pallas_call(
        functools.partial(first_kernel, tiles, piece, 4),
        in_specs=[in_place, in_place, in_vmem, in_vmem],
        out_specs=[in_vmem, in_vmem],
        out_shape=[
            jax.ShapeDtypeStruct((rows, hidden), jnp.bfloat16),
            jax.ShapeDtypeStruct((replicas, tall, LANES), jnp.bfloat16),
        ],
        scratch_shapes=[
            pltpu.VMEM((2, rows, hidden), jnp.bfloat16),
            pltpu.SemaphoreType.DMA((2, rows // piece)),
        ],
        compiler_params=pltpu.CompilerParams(vmem_limit_bytes=44 * MIB),
        name="compensate_and_left",
    )(grads, error, q_start, bucket)


def inverse_lower(gram):
    rank = gram.shape[0]
    row = lax.broadcasted_iota(jnp.int32, (rank, 1), 0)
    across = lax.broadcasted_iota(jnp.int32, (rank, 2 * rank), 1)
    down = lax.broadcasted_iota(jnp.int32, (rank, 2 * rank), 0)
    both = jnp.concatenate([jnp.zeros((rank, rank), jnp.float32), gram], axis=1)
    both = jnp.where(across == down, 1.0, both)
    for k in range(rank):
        column = both[:, rank + k : rank + k + 1]
        pivot = both[k : k + 1, rank + k : rank + k + 1]
        factor = jnp.where(row > k, column / pivot, 0.0)
        both = both - factor * both[k : k + 1, :]
    pivots = jnp.sum(jnp.where(across == down + rank, both, 0.0), axis=1, keepdims=True)
    return both[:, :rank] * lax.rsqrt(pivots)


def right_kernel(tiles, arrived, compensated, p_half_out, term):
    replicas, tall, _ = arrived.shape
    rank = tall // tiles
    factor_p = jnp.concatenate(
        [
            arrived[s, t * rank : (t + 1) * rank, :]
            for s in range(replicas)
            for t in range(tiles)
        ],
        axis=1,
    )
    gram = lax.dot_general(
        factor_p, factor_p, CONTRACT_LAST, preferred_element_type=jnp.float32
    )
    inverse = inverse_lower(gram)
    stacked = jnp.concatenate(three_parts(inverse), axis=0)
    p_parts = jnp.dot(stacked, factor_p, preferred_element_type=jnp.float32)
    p_hat = p_parts[:rank] + (p_parts[rank : 2 * rank] + p_parts[2 * rank :])
    p_half = p_hat.astype(jnp.bfloat16)
    p_half_out[...] = p_half
    term[...] = jnp.dot(
        p_half, compensated[...], preferred_element_type=jnp.float32
    ).astype(jnp.bfloat16)


def right(arrived, compensated, rank):
    rows, hidden = compensated.shape
    return pl.pallas_call(
        functools.partial(right_kernel, arrived.shape[1] // rank),
        in_specs=[pl.BlockSpec(memory_space=pltpu.VMEM)] * 2,
        out_specs=[pl.BlockSpec(memory_space=pltpu.VMEM)] * 2,
        out_shape=[
            jax.ShapeDtypeStruct((rank, rows), jnp.bfloat16),
            jax.ShapeDtypeStruct((rank, hidden), jnp.bfloat16),
        ],
        compiler_params=pltpu.CompilerParams(vmem_limit_bytes=24 * MIB),
        name="orthogonalize_and_right",
    )(arrived, compensated)


def sum_of_terms(arrived):
    total = arrived[0].astype(jnp.float32)
    for s in range(1, arrived.shape[0]):
        total = total + arrived[s].astype(jnp.float32)
    return total / arrived.shape[0]


def left_kernel(arrived, compensated, outgoing):
    replicas = arrived.shape[0]
    block = compensated.shape[0] // replicas
    factor_q = sum_of_terms(arrived)
    factor_q = factor_q / jnp.sqrt(jnp.sum(factor_q * factor_q, axis=1, keepdims=True) + 1e-06)
    q_half = factor_q.astype(jnp.bfloat16)
    for s in range(replicas):
        local_p = lax.dot_general(
            q_half,
            compensated[s * block : (s + 1) * block, :],
            CONTRACT_LAST,
            preferred_element_type=jnp.float32,
        )
        store_tiles(outgoing, s * block // LANES, block // LANES, local_p.astype(jnp.bfloat16))


def left(arrived, compensated):
    replicas, rank, _ = arrived.shape
    tall = compensated.shape[0] // replicas * rank // LANES
    return pl.pallas_call(
        left_kernel,
        in_specs=[pl.BlockSpec(memory_space=pltpu.VMEM)] * 2,
        out_specs=pl.BlockSpec(memory_space=pltpu.VMEM),
        out_shape=jax.ShapeDtypeStruct((replicas, tall, LANES), jnp.bfloat16),
        compiler_params=pltpu.CompilerParams(vmem_limit_bytes=24 * MIB),
        name="normalize_and_left",
    )(arrived, compensated)


def last_kernel(
    piece, arrived, p_half, compensated, bucket_sum,
    update, new_error, bucket_mean, update_held, error_held, sems,
):
    bucket_mean[...] = bucket_sum[...] / arrived.shape[0]
    q_parts = jnp.concatenate(three_parts(sum_of_terms(arrived)), axis=0)
    copies = []
    for i in range(compensated.shape[0] // piece):
        where = slice(i * piece, (i + 1) * piece)
        p_block = p_half[:, where].T
        block = jnp.dot(
            jnp.concatenate([p_block] * 3, axis=1), q_parts, preferred_element_type=jnp.float32
        )
        update_held[where, :] = block
        error_held[where, :] = (compensated[where, :].astype(jnp.float32) - block).astype(
            jnp.bfloat16
        )
        there = pl.ds(i * piece, piece)
        for j, (held, out) in enumerate(((update_held, update), (error_held, new_error))):
            copies.append(pltpu.make_async_copy(held.at[there], out.at[there], sems.at[j, i]))
            copies[-1].start()
    for copy in copies:
        copy.wait()


def last(arrived, p_half, compensated, bucket_sum):
    rows, hidden = compensated.shape
    piece = 2 * LANES
    in_vmem = pl.BlockSpec(memory_space=pltpu.VMEM)
    in_place = pl.BlockSpec(memory_space=pl.ANY)
    return pl.pallas_call(
        functools.partial(last_kernel, piece),
        in_specs=[in_vmem] * 4,
        out_specs=[in_place, in_place, in_vmem],
        out_shape=[
            jax.ShapeDtypeStruct((rows, hidden), jnp.float32),
            jax.ShapeDtypeStruct((rows, hidden), jnp.bfloat16),
            jax.ShapeDtypeStruct(bucket_sum.shape, jnp.float32),
        ],
        scratch_shapes=[
            pltpu.VMEM((rows, hidden), jnp.float32),
            pltpu.VMEM((rows, hidden), jnp.bfloat16),
            pltpu.SemaphoreType.DMA((2, rows // piece)),
        ],
        compiler_params=pltpu.CompilerParams(vmem_limit_bytes=40 * MIB),
        name="update_and_error",
    )(arrived, p_half, compensated, bucket_sum)


def on_device(grads, error, q_start, bucket):
    replicas = lax.axis_size("dp")
    rows = grads.shape[1]
    rank = q_start.shape[1]
    bucket = bucket.reshape(replicas, -1, LANES)
    tall = rows // replicas * rank // LANES
    compensated, outgoing = first(grads[0], error[0], q_start.T, bucket)
    bucket_sum = p_half = term = None
    for step in range(ITERS):
        if step > 0:
            outgoing = left(everywhere(term, replicas), compensated)
        share = jnp.sum(exchange(outgoing).astype(jnp.float32), axis=0)
        if step == 0:
            bucket_sum = share[tall:]
        factor_p = everywhere((share[:tall] / replicas).astype(jnp.bfloat16), replicas)
        p_half, term = right(factor_p, compensated, rank)
    update, new_error, bucket_mean = last(
        everywhere(term, replicas), p_half, compensated, bucket_sum
    )
    return (update, new_error[None], bucket_mean.reshape(-1))


def solution(mesh):
    return jax.shard_map(
        on_device,
        mesh=mesh,
        in_specs=(
            P("dp", None, "expert"),
            P("dp", None, "expert"),
            P("expert", None),
            P("dp", "expert"),
        ),
        out_specs=(P(None, "expert"), P("dp", None, "expert"), P(("expert", "dp"))),
        check_vma=False,
    )
```

```python
import functools

import jax
import jax.numpy as jnp
from jax import lax
from jax.experimental import pallas as pl
from jax.experimental.pallas import tpu as pltpu
from jax.sharding import PartitionSpec as P

ITERS = 2
LANES = 128
MIB = 1024 * 1024
CONTRACT_LAST = (((1,), (1,)), ((), ()))


def exchange(chunks):
    return lax.all_to_all(chunks, "dp", split_axis=0, concat_axis=0, tiled=True)


def everywhere(share, size):
    return exchange(jnp.broadcast_to(share, (size,) + share.shape))


def three_parts(value):
    high = value.astype(jnp.bfloat16)
    rest = value - high.astype(jnp.float32)
    middle = rest.astype(jnp.bfloat16)
    low = (rest - middle.astype(jnp.float32)).astype(jnp.bfloat16)
    return high, middle, low


def store_tiles(outgoing, first_tile, tiles, value):
    rank, columns = value.shape
    for at in range(columns // LANES):
        chunk, tile = divmod(first_tile + at, tiles)
        outgoing[chunk, tile * rank : (tile + 1) * rank, :] = value[:, at * LANES : (at + 1) * LANES]


def first_kernel(
    tiles, piece, ahead, grads, error, q_start, bucket, compensated, outgoing,
    landed, q_landed, bucket_landed, sems, small_sems,
):
    rows = grads.shape[0]
    pieces = rows // piece
    copies = []
    for i in range(pieces):
        where = pl.ds(i * piece, piece)
        copies.append(
            [
                pltpu.make_async_copy(array.at[where], landed.at[j, where], sems.at[j, i])
                for j, array in enumerate((grads, error))
            ]
        )

    def start(i):
        for copy in copies[i]:
            copy.start()

    fetch_q = pltpu.make_async_copy(q_start, q_landed, small_sems.at[0])
    fetch_bucket = pltpu.make_async_copy(bucket, bucket_landed, small_sems.at[1])
    fetch_q.start()
    for i in range(min(ahead, pieces)):
        start(i)
    fetch_bucket.start()
    fetch_q.wait()
    q_half = q_landed[...].astype(jnp.bfloat16)
    for i in range(pieces):
        for copy in copies[i]:
            copy.wait()
        if i + ahead < pieces:
            start(i + ahead)
        where = slice(i * piece, (i + 1) * piece)
        block = (
            landed[0, where, :].astype(jnp.float32) + landed[1, where, :].astype(jnp.float32)
        ).astype(jnp.bfloat16)
        compensated[where, :] = block
        local_p = lax.dot_general(q_half, block, CONTRACT_LAST, preferred_element_type=jnp.float32)
        store_tiles(outgoing, i * piece // LANES, tiles, local_p.astype(jnp.bfloat16))
    fetch_bucket.wait()
    outgoing[:, -bucket.shape[1] :, :] = bucket_landed[...].astype(jnp.bfloat16)


def first(grads, error, q_start, bucket):
    rows, hidden = grads.shape
    rank = q_start.shape[0]
    replicas = bucket.shape[0]
    tiles = rows // replicas // LANES
    piece = 2 * LANES
    tall = tiles * rank + bucket.shape[1]
    in_vmem = pl.BlockSpec(memory_space=pltpu.VMEM)
    in_place = pl.BlockSpec(memory_space=pl.ANY)
    return pl.pallas_call(
        functools.partial(first_kernel, tiles, piece, 8),
        in_specs=[in_place] * 4,
        out_specs=[in_vmem, in_vmem],
        out_shape=[
            pltpu.VMEM((rows, hidden), jnp.bfloat16),
            pltpu.VMEM((replicas, tall, LANES), jnp.bfloat16),
        ],
        scratch_shapes=[
            pltpu.VMEM((2, rows, hidden), jnp.bfloat16),
            pltpu.VMEM(q_start.shape, jnp.float32),
            pltpu.VMEM(bucket.shape, jnp.float32),
            pltpu.SemaphoreType.DMA((2, rows // piece)),
            pltpu.SemaphoreType.DMA((2,)),
        ],
        compiler_params=pltpu.CompilerParams(vmem_limit_bytes=50 * MIB),
        name="compensate_and_left",
    )(grads, error, q_start, bucket)


def inverse_lower(gram, width):
    rank = gram.shape[0]
    row = lax.broadcasted_iota(jnp.int32, (rank, 2 * rank), 0)
    across = lax.broadcasted_iota(jnp.int32, (rank, 2 * rank), 1)
    both = jnp.concatenate([jnp.zeros((rank, rank), jnp.float32), gram], axis=1)
    both = jnp.where(across == row, 1.0, both)
    for base in range(0, rank, width):
        columns = [
            jnp.broadcast_to(both[:, rank + k : rank + k + 1], both.shape)
            for k in range(base, base + width)
        ]
        for j, column in enumerate(columns):
            k = base + j
            factor = jnp.where(row > k, column * (1.0 / column[k : k + 1, :]), 0.0)
            for i in range(j + 1, width):
                columns[i] = columns[i] - factor * column[base + i : base + i + 1, :]
            both = both - factor * both[k : k + 1, :]
    pivots = jnp.sum(jnp.where(across == row + rank, both, 0.0), axis=1, keepdims=True)
    return both[:, :rank] * lax.rsqrt(pivots)


def right_kernel(tiles, arrived, compensated, term, p_half_out=None):
    replicas, tall, _ = arrived.shape
    rank = tall // tiles
    factor_p = jnp.concatenate(
        [
            arrived[s, t * rank : (t + 1) * rank, :]
            for s in range(replicas)
            for t in range(tiles)
        ],
        axis=1,
    )
    gram = lax.dot_general(
        factor_p, factor_p, CONTRACT_LAST, preferred_element_type=jnp.float32
    )
    inverse = inverse_lower(gram, 4)
    stacked = jnp.concatenate(three_parts(inverse), axis=0)
    p_parts = jnp.dot(stacked, factor_p, preferred_element_type=jnp.float32)
    p_hat = p_parts[:rank] + (p_parts[rank : 2 * rank] + p_parts[2 * rank :])
    p_half = p_hat.astype(jnp.bfloat16)
    if p_half_out is not None:
        p_half_out[...] = p_half
    term[...] = jnp.dot(
        p_half, compensated[...], preferred_element_type=jnp.float32
    ).astype(jnp.bfloat16)


def right(arrived, compensated, rank, keep):
    rows, hidden = compensated.shape
    widths = [hidden, rows] if keep else [hidden]
    return pl.pallas_call(
        functools.partial(right_kernel, arrived.shape[1] // rank),
        in_specs=[pl.BlockSpec(memory_space=pltpu.VMEM)] * 2,
        out_specs=[pl.BlockSpec(memory_space=pltpu.VMEM)] * len(widths),
        out_shape=[jax.ShapeDtypeStruct((rank, width), jnp.bfloat16) for width in widths],
        compiler_params=pltpu.CompilerParams(vmem_limit_bytes=24 * MIB),
        name="orthogonalize_and_right",
    )(arrived, compensated)


def sum_of_terms(arrived):
    total = arrived[0].astype(jnp.float32)
    for s in range(1, arrived.shape[0]):
        total = total + arrived[s].astype(jnp.float32)
    return total / arrived.shape[0]


def left_kernel(arrived, compensated, outgoing):
    replicas = arrived.shape[0]
    block = compensated.shape[0] // replicas
    factor_q = sum_of_terms(arrived)
    factor_q = factor_q / jnp.sqrt(jnp.sum(factor_q * factor_q, axis=1, keepdims=True) + 1e-06)
    q_half = factor_q.astype(jnp.bfloat16)
    for s in range(replicas):
        local_p = lax.dot_general(
            q_half,
            compensated[s * block : (s + 1) * block, :],
            CONTRACT_LAST,
            preferred_element_type=jnp.float32,
        )
        store_tiles(outgoing, s * block // LANES, block // LANES, local_p.astype(jnp.bfloat16))


def left(arrived, compensated):
    replicas, rank, _ = arrived.shape
    tall = compensated.shape[0] // replicas * rank // LANES
    return pl.pallas_call(
        left_kernel,
        in_specs=[pl.BlockSpec(memory_space=pltpu.VMEM)] * 2,
        out_specs=pl.BlockSpec(memory_space=pltpu.VMEM),
        out_shape=jax.ShapeDtypeStruct((replicas, tall, LANES), jnp.bfloat16),
        compiler_params=pltpu.CompilerParams(vmem_limit_bytes=24 * MIB),
        name="normalize_and_left",
    )(arrived, compensated)


def last_kernel(
    piece, arrived, p_half, compensated, share,
    update, new_error, bucket_mean, update_held, error_held, sems,
):
    bucket_mean[...] = share[-bucket_mean.shape[0] :, :] / arrived.shape[0]
    q_parts = jnp.concatenate(three_parts(sum_of_terms(arrived)), axis=0)
    copies = []
    for i in range(compensated.shape[0] // piece):
        where = slice(i * piece, (i + 1) * piece)
        p_block = p_half[:, where].T
        block = jnp.dot(
            jnp.concatenate([p_block] * 3, axis=1), q_parts, preferred_element_type=jnp.float32
        )
        update_held[where, :] = block
        error_held[where, :] = (compensated[where, :].astype(jnp.float32) - block).astype(
            jnp.bfloat16
        )
        there = pl.ds(i * piece, piece)
        for j, (held, out) in enumerate(((update_held, update), (error_held, new_error))):
            copies.append(pltpu.make_async_copy(held.at[there], out.at[there], sems.at[j, i]))
            copies[-1].start()
    for copy in copies:
        copy.wait()


def last(arrived, p_half, compensated, share, bucket_tall):
    rows, hidden = compensated.shape
    piece = 2 * LANES
    in_vmem = pl.BlockSpec(memory_space=pltpu.VMEM)
    in_place = pl.BlockSpec(memory_space=pl.ANY)
    return pl.pallas_call(
        functools.partial(last_kernel, piece),
        in_specs=[in_vmem] * 4,
        out_specs=[in_place, in_place, in_vmem],
        out_shape=[
            jax.ShapeDtypeStruct((rows, hidden), jnp.float32),
            jax.ShapeDtypeStruct((rows, hidden), jnp.bfloat16),
            jax.ShapeDtypeStruct((bucket_tall, LANES), jnp.float32),
        ],
        scratch_shapes=[
            pltpu.VMEM((rows, hidden), jnp.float32),
            pltpu.VMEM((rows, hidden), jnp.bfloat16),
            pltpu.SemaphoreType.DMA((2, rows // piece)),
        ],
        compiler_params=pltpu.CompilerParams(vmem_limit_bytes=40 * MIB),
        name="update_and_error",
    )(arrived, p_half, compensated, share)


def on_device(grads, error, q_start, bucket):
    replicas = lax.axis_size("dp")
    rows = grads.shape[1]
    rank = q_start.shape[1]
    bucket = bucket.reshape(replicas, -1, LANES)
    tall = rows // replicas * rank // LANES
    compensated, outgoing = first(grads[0], error[0], q_start.T, bucket)
    first_share = p_half = term = None
    for step in range(ITERS):
        if step > 0:
            outgoing = left(everywhere(term, replicas), compensated)
        share = jnp.sum(exchange(outgoing).astype(jnp.float32), axis=0)
        if step == 0:
            first_share = share
        factor_p = everywhere((share[:tall] / replicas).astype(jnp.bfloat16), replicas)
        term, *p_half = right(factor_p, compensated, rank, step + 1 == ITERS)
    update, new_error, bucket_mean = last(
        everywhere(term, replicas), p_half[0], compensated, first_share, bucket.shape[1]
    )
    return (update, new_error[None], bucket_mean.reshape(-1))


def solution(mesh):
    return jax.shard_map(
        on_device,
        mesh=mesh,
        in_specs=(
            P("dp", None, "expert"),
            P("dp", None, "expert"),
            P("expert", None),
            P("dp", "expert"),
        ),
        out_specs=(P(None, "expert"), P("dp", None, "expert"), P(("expert", "dp"))),
        check_vma=False,
    )
```

```python
import functools

import jax
import jax.numpy as jnp
from jax import lax
from jax.experimental import pallas as pl
from jax.experimental.pallas import tpu as pltpu
from jax.sharding import PartitionSpec as P

ITERS = 2
LANES = 128
MIB = 1024 * 1024
CONTRACT_LAST = (((1,), (1,)), ((), ()))


def exchange(chunks):
    return lax.all_to_all(chunks, "dp", split_axis=0, concat_axis=0, tiled=True)


def everywhere(share, size):
    return exchange(jnp.broadcast_to(share, (size,) + share.shape))


def three_parts(value):
    high = value.astype(jnp.bfloat16)
    rest = value - high.astype(jnp.float32)
    middle = rest.astype(jnp.bfloat16)
    low = (rest - middle.astype(jnp.float32)).astype(jnp.bfloat16)
    return high, middle, low


def store_tiles(outgoing, first_tile, tiles, value):
    rank, columns = value.shape
    for at in range(columns // LANES):
        chunk, tile = divmod(first_tile + at, tiles)
        outgoing[chunk, tile * rank : (tile + 1) * rank, :] = value[:, at * LANES : (at + 1) * LANES]


def first_kernel(
    tiles, piece, grads, error, q_start, compensated, outgoing, landed, q_landed, sems, q_sem
):
    fetch_q = pltpu.make_async_copy(q_start, q_landed, q_sem)
    fetch_q.start()
    copies = []
    for i in range(grads.shape[0] // piece):
        where = pl.ds(i * piece, piece)
        for j, array in enumerate((grads, error)):
            copies.append(
                pltpu.make_async_copy(array.at[where], landed.at[j, where], sems.at[j, i])
            )
            copies[-1].start(priority=j)
    fetch_q.wait()
    q_half = q_landed[...].astype(jnp.bfloat16)
    for i in range(grads.shape[0] // piece):
        copies[2 * i].wait()
        copies[2 * i + 1].wait()
        where = slice(i * piece, (i + 1) * piece)
        block = (
            landed[0, where, :].astype(jnp.float32) + landed[1, where, :].astype(jnp.float32)
        ).astype(jnp.bfloat16)
        compensated[where, :] = block
        local_p = lax.dot_general(q_half, block, CONTRACT_LAST, preferred_element_type=jnp.float32)
        store_tiles(outgoing, i * piece // LANES, tiles, local_p.astype(jnp.bfloat16))


def first(grads, error, q_start, replicas):
    rows, hidden = grads.shape
    rank = q_start.shape[0]
    tiles = rows // replicas // LANES
    piece = 4 * LANES
    return pl.pallas_call(
        functools.partial(first_kernel, tiles, piece),
        in_specs=[pl.BlockSpec(memory_space=pl.ANY)] * 3,
        out_specs=[pl.BlockSpec(memory_space=pltpu.VMEM)] * 2,
        out_shape=[
            pltpu.VMEM((rows, hidden), jnp.bfloat16),
            pltpu.VMEM((replicas, tiles * rank, LANES), jnp.bfloat16),
        ],
        scratch_shapes=[
            pltpu.VMEM((2, rows, hidden), jnp.bfloat16),
            pltpu.VMEM(q_start.shape, jnp.float32),
            pltpu.SemaphoreType.DMA((2, rows // piece)),
            pltpu.SemaphoreType.DMA(()),
        ],
        compiler_params=pltpu.CompilerParams(vmem_limit_bytes=50 * MIB),
        name="compensate_and_left",
    )(grads, error, q_start)


def inverse_lower(gram, width):
    rank = gram.shape[0]
    row = lax.broadcasted_iota(jnp.int32, (rank, 2 * rank), 0)
    across = lax.broadcasted_iota(jnp.int32, (rank, 2 * rank), 1)
    both = jnp.concatenate([jnp.zeros((rank, rank), jnp.float32), gram], axis=1)
    both = jnp.where(across == row, 1.0, both)
    for base in range(0, rank, width):
        columns = [
            jnp.broadcast_to(both[:, rank + k : rank + k + 1], both.shape)
            for k in range(base, base + width)
        ]
        for j, column in enumerate(columns):
            k = base + j
            factor = jnp.where(row > k, column * (1.0 / column[k : k + 1, :]), 0.0)
            for i in range(j + 1, width):
                columns[i] = columns[i] - factor * column[base + i : base + i + 1, :]
            both = both - factor * both[k : k + 1, :]
    pivots = jnp.sum(jnp.where(across == row + rank, both, 0.0), axis=1, keepdims=True)
    return both[:, :rank] * lax.rsqrt(pivots)


def right_kernel(tiles, arrived, compensated, term, p_half_out=None):
    replicas, tall, _ = arrived.shape
    rank = tall // tiles
    factor_p = jnp.concatenate(
        [
            arrived[s, t * rank : (t + 1) * rank, :]
            for s in range(replicas)
            for t in range(tiles)
        ],
        axis=1,
    )
    gram = lax.dot_general(
        factor_p, factor_p, CONTRACT_LAST, preferred_element_type=jnp.float32
    )
    inverse = inverse_lower(gram, 8)
    stacked = jnp.concatenate(three_parts(inverse), axis=0)
    p_parts = jnp.dot(stacked, factor_p, preferred_element_type=jnp.float32)
    p_hat = p_parts[:rank] + (p_parts[rank : 2 * rank] + p_parts[2 * rank :])
    p_half = p_hat.astype(jnp.bfloat16)
    if p_half_out is not None:
        p_half_out[...] = p_half
    term[...] = jnp.dot(
        p_half, compensated[...], preferred_element_type=jnp.float32
    ).astype(jnp.bfloat16)


def right(arrived, compensated, rank, keep):
    rows, hidden = compensated.shape
    widths = [hidden, rows] if keep else [hidden]
    return pl.pallas_call(
        functools.partial(right_kernel, arrived.shape[1] // rank),
        in_specs=[pl.BlockSpec(memory_space=pltpu.VMEM)] * 2,
        out_specs=[pl.BlockSpec(memory_space=pltpu.VMEM)] * len(widths),
        out_shape=[jax.ShapeDtypeStruct((rank, width), jnp.bfloat16) for width in widths],
        compiler_params=pltpu.CompilerParams(vmem_limit_bytes=24 * MIB),
        name="orthogonalize_and_right",
    )(arrived, compensated)


def sum_of_terms(arrived):
    total = arrived[0].astype(jnp.float32)
    for s in range(1, arrived.shape[0]):
        total = total + arrived[s].astype(jnp.float32)
    return total / arrived.shape[0]


def left_kernel(arrived, compensated, outgoing):
    replicas = arrived.shape[0]
    block = compensated.shape[0] // replicas
    factor_q = sum_of_terms(arrived)
    factor_q = factor_q / jnp.sqrt(jnp.sum(factor_q * factor_q, axis=1, keepdims=True) + 1e-06)
    q_half = factor_q.astype(jnp.bfloat16)
    for s in range(replicas):
        local_p = lax.dot_general(
            q_half,
            compensated[s * block : (s + 1) * block, :],
            CONTRACT_LAST,
            preferred_element_type=jnp.float32,
        )
        store_tiles(outgoing, s * block // LANES, block // LANES, local_p.astype(jnp.bfloat16))


def left(arrived, compensated):
    replicas, rank, _ = arrived.shape
    tall = compensated.shape[0] // replicas * rank // LANES
    return pl.pallas_call(
        left_kernel,
        in_specs=[pl.BlockSpec(memory_space=pltpu.VMEM)] * 2,
        out_specs=pl.BlockSpec(memory_space=pltpu.VMEM),
        out_shape=jax.ShapeDtypeStruct((replicas, tall, LANES), jnp.bfloat16),
        compiler_params=pltpu.CompilerParams(vmem_limit_bytes=24 * MIB),
        name="normalize_and_left",
    )(arrived, compensated)


def last_kernel(
    piece, arrived, p_half, compensated, update, new_error, update_held, error_held, sems
):
    q_parts = jnp.concatenate(three_parts(sum_of_terms(arrived)), axis=0)
    copies = []
    for i in range(compensated.shape[0] // piece):
        where = slice(i * piece, (i + 1) * piece)
        p_block = p_half[:, where].T
        block = jnp.dot(
            jnp.concatenate([p_block] * 3, axis=1), q_parts, preferred_element_type=jnp.float32
        )
        update_held[where, :] = block
        error_held[where, :] = (compensated[where, :].astype(jnp.float32) - block).astype(
            jnp.bfloat16
        )
        there = pl.ds(i * piece, piece)
        for j, (held, out) in enumerate(((update_held, update), (error_held, new_error))):
            copies.append(pltpu.make_async_copy(held.at[there], out.at[there], sems.at[j, i]))
            copies[-1].start()
    for copy in copies:
        copy.wait()


def last(arrived, p_half, compensated):
    rows, hidden = compensated.shape
    piece = 2 * LANES
    in_vmem = pl.BlockSpec(memory_space=pltpu.VMEM)
    in_place = pl.BlockSpec(memory_space=pl.ANY)
    return pl.pallas_call(
        functools.partial(last_kernel, piece),
        in_specs=[in_vmem] * 3,
        out_specs=[in_place, in_place],
        out_shape=[
            jax.ShapeDtypeStruct((rows, hidden), jnp.float32),
            jax.ShapeDtypeStruct((rows, hidden), jnp.bfloat16),
        ],
        scratch_shapes=[
            pltpu.VMEM((rows, hidden), jnp.float32),
            pltpu.VMEM((rows, hidden), jnp.bfloat16),
            pltpu.SemaphoreType.DMA((2, rows // piece)),
        ],
        compiler_params=pltpu.CompilerParams(vmem_limit_bytes=40 * MIB),
        name="update_and_error",
    )(arrived, p_half, compensated)


def on_device(grads, error, q_start, bucket):
    replicas = lax.axis_size("dp")
    rank = q_start.shape[1]
    bucket = lax.psum(bucket.reshape(-1, LANES), "dp")
    compensated, outgoing = first(grads[0], error[0], q_start.T, replicas)
    p_half = term = None
    for step in range(ITERS):
        if step > 0:
            outgoing = left(everywhere(term, replicas), compensated)
        share = jnp.sum(exchange(outgoing).astype(jnp.float32), axis=0) / replicas
        factor_p = everywhere(share.astype(jnp.bfloat16), replicas)
        term, *p_half = right(factor_p, compensated, rank, step + 1 == ITERS)
    update, new_error = last(everywhere(term, replicas), p_half[0], compensated)
    tall = bucket.shape[0] // replicas
    bucket_share = lax.dynamic_slice_in_dim(bucket, lax.axis_index("dp") * tall, tall) / replicas
    return (update, new_error[None], bucket_share.reshape(-1))


def solution(mesh):
    return jax.shard_map(
        on_device,
        mesh=mesh,
        in_specs=(
            P("dp", None, "expert"),
            P("dp", None, "expert"),
            P("expert", None),
            P("dp", "expert"),
        ),
        out_specs=(P(None, "expert"), P("dp", None, "expert"), P(("expert", "dp"))),
        check_vma=False,
    )
```

```python
import functools

import jax
import jax.numpy as jnp
from jax import lax
from jax.experimental import pallas as pl
from jax.experimental.pallas import tpu as pltpu
from jax.sharding import PartitionSpec as P

ITERS = 2
LANES = 128
MIB = 1024 * 1024
CONTRACT_LAST = (((1,), (1,)), ((), ()))


def exchange(chunks):
    return lax.all_to_all(chunks, "dp", split_axis=0, concat_axis=0, tiled=True)


def everywhere(share, size):
    return exchange(jnp.broadcast_to(share, (size,) + share.shape))


def three_parts(value):
    high = value.astype(jnp.bfloat16)
    rest = value - high.astype(jnp.float32)
    middle = rest.astype(jnp.bfloat16)
    low = (rest - middle.astype(jnp.float32)).astype(jnp.bfloat16)
    return high, middle, low


def store_tiles(outgoing, first_tile, tiles, value):
    rank, columns = value.shape
    for at in range(columns // LANES):
        chunk, tile = divmod(first_tile + at, tiles)
        outgoing[chunk, tile * rank : (tile + 1) * rank, :] = value[:, at * LANES : (at + 1) * LANES]


def first_kernel(
    tiles, piece, grads, error, q_start, bucket, compensated, outgoing,
    landed, q_landed, bucket_landed, sems, small_sems,
):
    fetch_q = pltpu.make_async_copy(q_start, q_landed, small_sems.at[0])
    fetch_bucket = pltpu.make_async_copy(bucket, bucket_landed, small_sems.at[1])
    fetch_q.start()
    copies = []
    for i in range(grads.shape[0] // piece):
        where = pl.ds(i * piece, piece)
        for j, array in enumerate((grads, error)):
            copies.append(
                pltpu.make_async_copy(array.at[where], landed.at[j, where], sems.at[j, i])
            )
            copies[-1].start(priority=j)
    fetch_bucket.start()
    fetch_q.wait()
    q_half = q_landed[...].astype(jnp.bfloat16)
    for i in range(grads.shape[0] // piece):
        copies[2 * i].wait()
        copies[2 * i + 1].wait()
        where = slice(i * piece, (i + 1) * piece)
        block = (
            landed[0, where, :].astype(jnp.float32) + landed[1, where, :].astype(jnp.float32)
        ).astype(jnp.bfloat16)
        compensated[where, :] = block
        local_p = lax.dot_general(q_half, block, CONTRACT_LAST, preferred_element_type=jnp.float32)
        store_tiles(outgoing, i * piece // LANES, tiles, local_p.astype(jnp.bfloat16))
    fetch_bucket.wait()
    outgoing[:, -bucket.shape[1] :, :] = bucket_landed[...].astype(jnp.bfloat16)


def first(grads, error, q_start, bucket):
    rows, hidden = grads.shape
    rank = q_start.shape[0]
    replicas = bucket.shape[0]
    tiles = rows // replicas // LANES
    tall = tiles * rank + bucket.shape[1]
    piece = 4 * LANES
    return pl.pallas_call(
        functools.partial(first_kernel, tiles, piece),
        in_specs=[pl.BlockSpec(memory_space=pl.ANY)] * 4,
        out_specs=[pl.BlockSpec(memory_space=pltpu.VMEM)] * 2,
        out_shape=[
            pltpu.VMEM((rows, hidden), jnp.bfloat16),
            pltpu.VMEM((replicas, tall, LANES), jnp.bfloat16),
        ],
        scratch_shapes=[
            pltpu.VMEM((2, rows, hidden), jnp.bfloat16),
            pltpu.VMEM(q_start.shape, jnp.float32),
            pltpu.VMEM(bucket.shape, jnp.float32),
            pltpu.SemaphoreType.DMA((2, rows // piece)),
            pltpu.SemaphoreType.DMA((2,)),
        ],
        compiler_params=pltpu.CompilerParams(vmem_limit_bytes=50 * MIB),
        name="compensate_and_left",
    )(grads, error, q_start, bucket)


def inverse_lower(gram, width):
    rank = gram.shape[0]
    row = lax.broadcasted_iota(jnp.int32, (rank, 2 * rank), 0)
    across = lax.broadcasted_iota(jnp.int32, (rank, 2 * rank), 1)
    both = jnp.concatenate([jnp.zeros((rank, rank), jnp.float32), gram], axis=1)
    both = jnp.where(across == row, 1.0, both)
    for base in range(0, rank, width):
        columns = [
            jnp.broadcast_to(both[:, rank + k : rank + k + 1], both.shape)
            for k in range(base, base + width)
        ]
        for j, column in enumerate(columns):
            k = base + j
            factor = jnp.where(row > k, column * (1.0 / column[k : k + 1, :]), 0.0)
            for i in range(j + 1, width):
                columns[i] = columns[i] - factor * column[base + i : base + i + 1, :]
            both = both - factor * both[k : k + 1, :]
    pivots = jnp.sum(jnp.where(across == row + rank, both, 0.0), axis=1, keepdims=True)
    return both[:, :rank] * lax.rsqrt(pivots)


def right_kernel(tiles, arrived, compensated, term, p_half_out=None):
    replicas, tall, _ = arrived.shape
    rank = tall // tiles
    factor_p = jnp.concatenate(
        [
            arrived[s, t * rank : (t + 1) * rank, :]
            for s in range(replicas)
            for t in range(tiles)
        ],
        axis=1,
    )
    gram = lax.dot_general(
        factor_p, factor_p, CONTRACT_LAST, preferred_element_type=jnp.float32
    )
    inverse = inverse_lower(gram, 8)
    stacked = jnp.concatenate(three_parts(inverse), axis=0)
    p_parts = jnp.dot(stacked, factor_p, preferred_element_type=jnp.float32)
    p_hat = p_parts[:rank] + (p_parts[rank : 2 * rank] + p_parts[2 * rank :])
    p_half = p_hat.astype(jnp.bfloat16)
    if p_half_out is not None:
        p_half_out[...] = p_half
    product = jnp.dot(p_half, compensated[...], preferred_element_type=jnp.float32)
    for tile in range(term.shape[0] // rank):
        term[tile * rank : (tile + 1) * rank, :] = product[
            :, tile * LANES : (tile + 1) * LANES
        ].astype(jnp.bfloat16)


def right(arrived, compensated, rank, keep):
    rows, hidden = compensated.shape
    shapes = [(hidden // LANES * rank, LANES)] + [(rank, rows)] * keep
    return pl.pallas_call(
        functools.partial(right_kernel, arrived.shape[1] // rank),
        in_specs=[pl.BlockSpec(memory_space=pltpu.VMEM)] * 2,
        out_specs=[pl.BlockSpec(memory_space=pltpu.VMEM)] * len(shapes),
        out_shape=[jax.ShapeDtypeStruct(shape, jnp.bfloat16) for shape in shapes],
        compiler_params=pltpu.CompilerParams(vmem_limit_bytes=24 * MIB),
        name="orthogonalize_and_right",
    )(arrived, compensated)


def untile(tiles, rank):
    return jnp.concatenate(
        [tiles[at : at + rank, :] for at in range(0, tiles.shape[0], rank)], axis=1
    )


def left_kernel(rank, arrived, compensated, outgoing):
    replicas = outgoing.shape[0]
    block = compensated.shape[0] // replicas
    factor_q = untile(arrived, rank).astype(jnp.float32)
    factor_q = factor_q / jnp.sqrt(jnp.sum(factor_q * factor_q, axis=1, keepdims=True) + 1e-06)
    q_half = factor_q.astype(jnp.bfloat16)
    for s in range(replicas):
        local_p = lax.dot_general(
            q_half,
            compensated[s * block : (s + 1) * block, :],
            CONTRACT_LAST,
            preferred_element_type=jnp.float32,
        )
        store_tiles(outgoing, s * block // LANES, block // LANES, local_p.astype(jnp.bfloat16))


def left(arrived, compensated, rank, replicas):
    tall = compensated.shape[0] // replicas * rank // LANES
    return pl.pallas_call(
        functools.partial(left_kernel, rank),
        in_specs=[pl.BlockSpec(memory_space=pltpu.VMEM)] * 2,
        out_specs=pl.BlockSpec(memory_space=pltpu.VMEM),
        out_shape=jax.ShapeDtypeStruct((replicas, tall, LANES), jnp.bfloat16),
        compiler_params=pltpu.CompilerParams(vmem_limit_bytes=24 * MIB),
        name="normalize_and_left",
    )(arrived, compensated)


def last_kernel(
    piece, arrived, p_half, compensated, share,
    update, new_error, bucket_mean, update_held, error_held, sems,
):
    rank = p_half.shape[0]
    q_half = untile(arrived, rank)
    copies = []
    for i in range(compensated.shape[0] // piece):
        where = slice(i * piece, (i + 1) * piece)
        block = jnp.dot(p_half[:, where].T, q_half, preferred_element_type=jnp.float32)
        update_held[where, :] = block
        error_held[where, :] = (compensated[where, :].astype(jnp.float32) - block).astype(
            jnp.bfloat16
        )
        there = pl.ds(i * piece, piece)
        for j, (held, out) in enumerate(((update_held, update), (error_held, new_error))):
            copies.append(pltpu.make_async_copy(held.at[there], out.at[there], sems.at[j, i]))
            copies[-1].start(priority=j)
    bucket_mean[...] = share[-bucket_mean.shape[0] :, :]
    for copy in copies:
        copy.wait()


def last(arrived, p_half, compensated, share, bucket_tall):
    rows, hidden = compensated.shape
    piece = 2 * LANES
    in_vmem = pl.BlockSpec(memory_space=pltpu.VMEM)
    in_place = pl.BlockSpec(memory_space=pl.ANY)
    return pl.pallas_call(
        functools.partial(last_kernel, piece),
        in_specs=[in_vmem] * 4,
        out_specs=[in_place, in_place, in_vmem],
        out_shape=[
            jax.ShapeDtypeStruct((rows, hidden), jnp.float32),
            jax.ShapeDtypeStruct((rows, hidden), jnp.bfloat16),
            jax.ShapeDtypeStruct((bucket_tall, LANES), jnp.float32),
        ],
        scratch_shapes=[
            pltpu.VMEM((rows, hidden), jnp.float32),
            pltpu.VMEM((rows, hidden), jnp.bfloat16),
            pltpu.SemaphoreType.DMA((2, rows // piece)),
        ],
        compiler_params=pltpu.CompilerParams(vmem_limit_bytes=40 * MIB),
        name="update_and_error",
    )(arrived, p_half, compensated, share)


def on_device(grads, error, q_start, bucket):
    replicas = lax.axis_size("dp")
    rows = grads.shape[1]
    rank = q_start.shape[1]
    bucket = bucket.reshape(replicas, -1, LANES)
    tall = rows // replicas * rank // LANES

    def mean_of_share(chunks):
        return jnp.sum(exchange(chunks).astype(jnp.float32), axis=0) / replicas

    compensated, outgoing = first(grads[0], error[0], q_start.T, bucket)
    first_share = None
    for step in range(ITERS):
        share = mean_of_share(outgoing)
        if step == 0:
            first_share = share
        factor_p = everywhere(share[:tall].astype(jnp.bfloat16), replicas)
        term, *p_half = right(factor_p, compensated, rank, step + 1 == ITERS)
        share = mean_of_share(term.reshape(replicas, -1, LANES)).astype(jnp.bfloat16)
        factor_q = everywhere(share, replicas).reshape(term.shape)
        if step + 1 < ITERS:
            outgoing = left(factor_q, compensated, rank, replicas)
    update, new_error, bucket_mean = last(
        factor_q, p_half[0], compensated, first_share, bucket.shape[1]
    )
    return (update, new_error[None], bucket_mean.reshape(-1))


def solution(mesh):
    return jax.shard_map(
        on_device,
        mesh=mesh,
        in_specs=(
            P("dp", None, "expert"),
            P("dp", None, "expert"),
            P("expert", None),
            P("dp", "expert"),
        ),
        out_specs=(P(None, "expert"), P("dp", None, "expert"), P(("expert", "dp"))),
        check_vma=False,
    )
```

```python
import functools

import jax
import jax.numpy as jnp
from jax import lax
from jax.experimental import pallas as pl
from jax.experimental.pallas import tpu as pltpu
from jax.sharding import PartitionSpec as P

ITERS = 2
LANES = 128
SUBLANES = 8
MIB = 1024 * 1024
CONTRACT_LAST = (((1,), (1,)), ((), ()))


def exchange(chunks):
    return lax.all_to_all(chunks, "dp", split_axis=0, concat_axis=0, tiled=True)


def everywhere(share, size):
    return exchange(jnp.broadcast_to(share, (size,) + share.shape))


def three_parts(value):
    high = value.astype(jnp.bfloat16)
    rest = value - high.astype(jnp.float32)
    middle = rest.astype(jnp.bfloat16)
    low = (rest - middle.astype(jnp.float32)).astype(jnp.bfloat16)
    return high, middle, low


def store_tiles(outgoing, first_tile, tiles, value):
    rank, columns = value.shape
    for at in range(columns // LANES):
        chunk, tile = divmod(first_tile + at, tiles)
        outgoing[chunk, tile * rank : (tile + 1) * rank, :] = value[:, at * LANES : (at + 1) * LANES]


def first_kernel(
    tiles, piece, grads, error, q_start, bucket, compensated, outgoing,
    landed, q_landed, bucket_landed, sems, small_sems,
):
    fetch_q = pltpu.make_async_copy(q_start, q_landed, small_sems.at[0])
    fetch_bucket = pltpu.make_async_copy(bucket, bucket_landed, small_sems.at[1])
    fetch_q.start()
    copies = []
    for i in range(grads.shape[0] // piece):
        where = pl.ds(i * piece, piece)
        for j, array in enumerate((grads, error)):
            copies.append(
                pltpu.make_async_copy(array.at[where], landed.at[j, where], sems.at[j, i])
            )
            copies[-1].start(priority=j)
    fetch_bucket.start()
    fetch_q.wait()
    q_half = q_landed[...].astype(jnp.bfloat16)
    for i in range(grads.shape[0] // piece):
        copies[2 * i].wait()
        copies[2 * i + 1].wait()
        where = slice(i * piece, (i + 1) * piece)
        block = (
            landed[0, where, :].astype(jnp.float32) + landed[1, where, :].astype(jnp.float32)
        ).astype(jnp.bfloat16)
        compensated[where, :] = block
        local_p = lax.dot_general(q_half, block, CONTRACT_LAST, preferred_element_type=jnp.float32)
        store_tiles(outgoing, i * piece // LANES, tiles, local_p.astype(jnp.bfloat16))
    fetch_bucket.wait()
    outgoing[:, -bucket.shape[1] :, :] = bucket_landed[...].astype(jnp.bfloat16)


def first(grads, error, q_start, bucket):
    rows, hidden = grads.shape
    rank = q_start.shape[0]
    replicas = bucket.shape[0]
    tiles = rows // replicas // LANES
    tall = tiles * rank + bucket.shape[1]
    piece = 4 * LANES
    return pl.pallas_call(
        functools.partial(first_kernel, tiles, piece),
        in_specs=[pl.BlockSpec(memory_space=pl.ANY)] * 4,
        out_specs=[pl.BlockSpec(memory_space=pltpu.VMEM)] * 2,
        out_shape=[
            pltpu.VMEM((rows, hidden), jnp.bfloat16),
            pltpu.VMEM((replicas, tall, LANES), jnp.bfloat16),
        ],
        scratch_shapes=[
            pltpu.VMEM((2, rows, hidden), jnp.bfloat16),
            pltpu.VMEM(q_start.shape, jnp.float32),
            pltpu.VMEM(bucket.shape, jnp.float32),
            pltpu.SemaphoreType.DMA((2, rows // piece)),
            pltpu.SemaphoreType.DMA((2,)),
        ],
        compiler_params=pltpu.CompilerParams(vmem_limit_bytes=50 * MIB),
        name="compensate_and_left",
    )(grads, error, q_start, bucket)


def inverse_lower(gram):
    rank = gram.shape[0]
    row = lax.broadcasted_iota(jnp.int32, (SUBLANES, 2 * rank), 0)
    across = lax.broadcasted_iota(jnp.int32, (SUBLANES, 2 * rank), 1)
    both = jnp.concatenate([jnp.zeros((rank, rank), jnp.float32), gram], axis=1)
    starts = range(0, rank, SUBLANES)
    tiles = [
        jnp.where(across == row + at, 1.0, both[at : at + SUBLANES, :]) for at in starts
    ]
    inverse = []
    for top, base in enumerate(starts):
        columns = [
            [
                jnp.broadcast_to(tile[:, rank + k : rank + k + 1], tile.shape)
                for tile in tiles[top:]
            ]
            for k in range(base, base + SUBLANES)
        ]
        for j in range(SUBLANES):
            head = columns[j][0]
            reciprocal = 1.0 / head[j : j + 1, :]
            pivot_row = tiles[top][j : j + 1, :]
            for at in range(len(columns[j])):
                factor = columns[j][at] * reciprocal
                if at == 0:
                    factor = jnp.where(row > j, factor, 0.0)
                for i in range(j + 1, SUBLANES):
                    columns[i][at] = columns[i][at] - factor * head[i : i + 1, :]
                tiles[top + at] = tiles[top + at] - factor * pivot_row
        done = tiles[top]
        pivots = jnp.sum(
            jnp.where(across == row + (rank + base), done, 0.0), axis=1, keepdims=True
        )
        inverse.append(done[:, :rank] * lax.rsqrt(pivots))
    return jnp.concatenate(inverse, axis=0)


def right_kernel(tiles, arrived, compensated, term, p_half_out=None):
    replicas, tall, _ = arrived.shape
    rank = tall // tiles
    factor_p = jnp.concatenate(
        [
            arrived[s, t * rank : (t + 1) * rank, :]
            for s in range(replicas)
            for t in range(tiles)
        ],
        axis=1,
    )
    gram = lax.dot_general(
        factor_p, factor_p, CONTRACT_LAST, preferred_element_type=jnp.float32
    )
    inverse = inverse_lower(gram)
    stacked = jnp.concatenate(three_parts(inverse), axis=0)
    p_parts = jnp.dot(stacked, factor_p, preferred_element_type=jnp.float32)
    p_hat = p_parts[:rank] + (p_parts[rank : 2 * rank] + p_parts[2 * rank :])
    p_half = p_hat.astype(jnp.bfloat16)
    if p_half_out is not None:
        p_half_out[...] = p_half
    term[...] = jnp.dot(
        p_half, compensated[...], preferred_element_type=jnp.float32
    ).astype(jnp.bfloat16)


def right(arrived, compensated, rank, keep):
    rows, hidden = compensated.shape
    shapes = [(rank, hidden)] + [(rank, rows)] * keep
    return pl.pallas_call(
        functools.partial(right_kernel, arrived.shape[1] // rank),
        in_specs=[pl.BlockSpec(memory_space=pltpu.VMEM)] * 2,
        out_specs=[pl.BlockSpec(memory_space=pltpu.VMEM)] * len(shapes),
        out_shape=[jax.ShapeDtypeStruct(shape, jnp.bfloat16) for shape in shapes],
        compiler_params=pltpu.CompilerParams(vmem_limit_bytes=24 * MIB),
        name="orthogonalize_and_right",
    )(arrived, compensated)


def add(mine, other):
    return mine.astype(jnp.float32) + other.astype(jnp.float32)


def all_but_last_sum(term, size):
    step = 1
    while True:
        other = lax.ppermute(term, "dp", [(i, i ^ step) for i in range(size)])
        step *= 2
        if step >= size:
            return term, other
        term = add(term, other).astype(jnp.bfloat16)


def left_kernel(mine, other, compensated, outgoing):
    replicas = outgoing.shape[0]
    block = compensated.shape[0] // replicas
    factor_q = add(mine[...], other[...]) / replicas
    factor_q = factor_q / jnp.sqrt(jnp.sum(factor_q * factor_q, axis=1, keepdims=True) + 1e-06)
    q_half = factor_q.astype(jnp.bfloat16)
    for s in range(replicas):
        local_p = lax.dot_general(
            q_half,
            compensated[s * block : (s + 1) * block, :],
            CONTRACT_LAST,
            preferred_element_type=jnp.float32,
        )
        store_tiles(outgoing, s * block // LANES, block // LANES, local_p.astype(jnp.bfloat16))


def left(mine, other, compensated, replicas):
    tall = compensated.shape[0] // replicas * mine.shape[0] // LANES
    return pl.pallas_call(
        left_kernel,
        in_specs=[pl.BlockSpec(memory_space=pltpu.VMEM)] * 3,
        out_specs=pl.BlockSpec(memory_space=pltpu.VMEM),
        out_shape=jax.ShapeDtypeStruct((replicas, tall, LANES), jnp.bfloat16),
        compiler_params=pltpu.CompilerParams(vmem_limit_bytes=24 * MIB),
        name="normalize_and_left",
    )(mine, other, compensated)


def last_kernel(
    piece, replicas, mine, other, p_half, compensated, share,
    update, new_error, bucket_mean, update_held, error_held, sems,
):
    q_parts = jnp.concatenate(three_parts(add(mine[...], other[...]) / replicas), axis=0)
    copies = []
    for i in range(compensated.shape[0] // piece):
        where = slice(i * piece, (i + 1) * piece)
        p_block = p_half[:, where].T
        block = jnp.dot(
            jnp.concatenate([p_block] * 3, axis=1), q_parts, preferred_element_type=jnp.float32
        )
        update_held[where, :] = block
        error_held[where, :] = (compensated[where, :].astype(jnp.float32) - block).astype(
            jnp.bfloat16
        )
        there = pl.ds(i * piece, piece)
        for j, (held, out) in enumerate(((update_held, update), (error_held, new_error))):
            copies.append(pltpu.make_async_copy(held.at[there], out.at[there], sems.at[j, i]))
            copies[-1].start(priority=j)
    bucket_mean[...] = share[-bucket_mean.shape[0] :, :]
    for copy in copies:
        copy.wait()


def last(mine, other, p_half, compensated, share, replicas, bucket_tall):
    rows, hidden = compensated.shape
    piece = 2 * LANES
    in_vmem = pl.BlockSpec(memory_space=pltpu.VMEM)
    in_place = pl.BlockSpec(memory_space=pl.ANY)
    return pl.pallas_call(
        functools.partial(last_kernel, piece, replicas),
        in_specs=[in_vmem] * 5,
        out_specs=[in_place, in_place, in_vmem],
        out_shape=[
            jax.ShapeDtypeStruct((rows, hidden), jnp.float32),
            jax.ShapeDtypeStruct((rows, hidden), jnp.bfloat16),
            jax.ShapeDtypeStruct((bucket_tall, LANES), jnp.float32),
        ],
        scratch_shapes=[
            pltpu.VMEM((rows, hidden), jnp.float32),
            pltpu.VMEM((rows, hidden), jnp.bfloat16),
            pltpu.SemaphoreType.DMA((2, rows // piece)),
        ],
        compiler_params=pltpu.CompilerParams(vmem_limit_bytes=40 * MIB),
        name="update_and_error",
    )(mine, other, p_half, compensated, share)


def on_device(grads, error, q_start, bucket):
    replicas = lax.axis_size("dp")
    rows = grads.shape[1]
    rank = q_start.shape[1]
    bucket = bucket.reshape(replicas, -1, LANES)
    tall = rows // replicas * rank // LANES

    compensated, outgoing = first(grads[0], error[0], q_start.T, bucket)
    first_share = None
    for step in range(ITERS):
        share = jnp.sum(exchange(outgoing).astype(jnp.float32), axis=0) / replicas
        if step == 0:
            first_share = share
        factor_p = everywhere(share[:tall].astype(jnp.bfloat16), replicas)
        term, *p_half = right(factor_p, compensated, rank, step + 1 == ITERS)
        mine, other = all_but_last_sum(term, replicas)
        if step + 1 < ITERS:
            outgoing = left(mine, other, compensated, replicas)
    update, new_error, bucket_mean = last(
        mine, other, p_half[0], compensated, first_share, replicas, bucket.shape[1]
    )
    return (update, new_error[None], bucket_mean.reshape(-1))


def solution(mesh):
    return jax.shard_map(
        on_device,
        mesh=mesh,
        in_specs=(
            P("dp", None, "expert"),
            P("dp", None, "expert"),
            P("expert", None),
            P("dp", "expert"),
        ),
        out_specs=(P(None, "expert"), P("dp", None, "expert"), P(("expert", "dp"))),
        check_vma=False,
    )
```

```python
import functools

import jax
import jax.numpy as jnp
from jax import lax
from jax.experimental import pallas as pl
from jax.experimental.pallas import tpu as pltpu
from jax.sharding import PartitionSpec as P

ITERS = 2
LANES = 128
SUBLANES = 8
MIB = 1024 * 1024
CONTRACT_LAST = (((1,), (1,)), ((), ()))


def exchange(chunks):
    return lax.all_to_all(chunks, "dp", split_axis=0, concat_axis=0, tiled=True)


def everywhere(share, size):
    return exchange(jnp.broadcast_to(share, (size,) + share.shape))


def three_parts(value):
    high = value.astype(jnp.bfloat16)
    rest = value - high.astype(jnp.float32)
    middle = rest.astype(jnp.bfloat16)
    low = (rest - middle.astype(jnp.float32)).astype(jnp.bfloat16)
    return high, middle, low


def pieces(rows):
    sizes = [LANES, LANES, 2 * LANES] + [4 * LANES] * (rows // (4 * LANES) - 1)
    return [(sum(sizes[:i]), size) for i, size in enumerate(sizes)]


def store_tiles(outgoing, first_tile, tiles, value):
    rank, columns = value.shape
    for at in range(columns // LANES):
        chunk, tile = divmod(first_tile + at, tiles)
        outgoing[chunk, tile * rank : (tile + 1) * rank, :] = value[:, at * LANES : (at + 1) * LANES]


def first_kernel(
    tiles, grads, error, q_start, bucket, compensated, outgoing,
    landed, q_landed, bucket_landed, sems, small_sems,
):
    fetch_q = pltpu.make_async_copy(q_start, q_landed, small_sems.at[0])
    fetch_bucket = pltpu.make_async_copy(bucket, bucket_landed, small_sems.at[1])
    fetch_q.start()
    copies = []
    rows = grads.shape[0]
    cuts = [(rows - at - size, size) for at, size in reversed(pieces(rows))]
    for i, (at, size) in enumerate(cuts):
        where = pl.ds(at, size)
        for j, array in enumerate((grads, error)):
            copies.append(
                pltpu.make_async_copy(array.at[where], landed.at[j, where], sems.at[j, i])
            )
            copies[-1].start(priority=j)
    fetch_bucket.start()
    fetch_q.wait()
    q_half = q_landed[...].astype(jnp.bfloat16)
    for i, (at, size) in enumerate(cuts):
        copies[2 * i].wait()
        copies[2 * i + 1].wait()
        where = slice(at, at + size)
        block = (
            landed[0, where, :].astype(jnp.float32) + landed[1, where, :].astype(jnp.float32)
        ).astype(jnp.bfloat16)
        compensated[where, :] = block
        local_p = lax.dot_general(q_half, block, CONTRACT_LAST, preferred_element_type=jnp.float32)
        store_tiles(outgoing, at // LANES, tiles, local_p.astype(jnp.bfloat16))
    fetch_bucket.wait()
    outgoing[:, -bucket.shape[1] :, :] = bucket_landed[...].astype(jnp.bfloat16)


def first(grads, error, q_start, bucket):
    rows, hidden = grads.shape
    rank = q_start.shape[0]
    replicas = bucket.shape[0]
    tiles = rows // replicas // LANES
    tall = tiles * rank + bucket.shape[1]
    return pl.pallas_call(
        functools.partial(first_kernel, tiles),
        in_specs=[pl.BlockSpec(memory_space=pl.ANY)] * 4,
        out_specs=[pl.BlockSpec(memory_space=pltpu.VMEM)] * 2,
        out_shape=[
            pltpu.VMEM((rows, hidden), jnp.bfloat16),
            pltpu.VMEM((replicas, tall, LANES), jnp.bfloat16),
        ],
        scratch_shapes=[
            pltpu.VMEM((2, rows, hidden), jnp.bfloat16),
            pltpu.VMEM(q_start.shape, jnp.float32),
            pltpu.VMEM(bucket.shape, jnp.float32),
            pltpu.SemaphoreType.DMA((2, len(pieces(rows)))),
            pltpu.SemaphoreType.DMA((2,)),
        ],
        compiler_params=pltpu.CompilerParams(vmem_limit_bytes=50 * MIB),
        name="compensate_and_left",
    )(grads, error, q_start, bucket)


def inverse_lower(gram):
    rank = gram.shape[0]
    row = lax.broadcasted_iota(jnp.int32, (SUBLANES, 2 * rank), 0)
    across = lax.broadcasted_iota(jnp.int32, (SUBLANES, 2 * rank), 1)
    both = jnp.concatenate([jnp.zeros((rank, rank), jnp.float32), gram], axis=1)
    starts = range(0, rank, SUBLANES)
    tiles = [
        jnp.where(across == row + at, 1.0, both[at : at + SUBLANES, :]) for at in starts
    ]
    inverse = []
    for top, base in enumerate(starts):
        columns = [
            [
                jnp.broadcast_to(tile[:, rank + k : rank + k + 1], tile.shape)
                for tile in tiles[top:]
            ]
            for k in range(base, base + SUBLANES)
        ]
        for j in range(SUBLANES):
            head = columns[j][0]
            reciprocal = 1.0 / head[j : j + 1, :]
            pivot_row = tiles[top][j : j + 1, :]
            for at in range(len(columns[j])):
                factor = columns[j][at] * reciprocal
                if at == 0:
                    factor = jnp.where(row > j, factor, 0.0)
                for i in range(j + 1, SUBLANES):
                    columns[i][at] = columns[i][at] - factor * head[i : i + 1, :]
                tiles[top + at] = tiles[top + at] - factor * pivot_row
        done = tiles[top]
        pivots = jnp.sum(
            jnp.where(across == row + (rank + base), done, 0.0), axis=1, keepdims=True
        )
        inverse.append(done[:, :rank] * lax.rsqrt(pivots))
    return jnp.concatenate(inverse, axis=0)


def right_kernel(tiles, arrived, compensated, term, p_half_out=None):
    replicas, tall, _ = arrived.shape
    rank = tall // tiles
    factor_p = jnp.concatenate(
        [
            arrived[s, t * rank : (t + 1) * rank, :]
            for s in range(replicas)
            for t in range(tiles)
        ],
        axis=1,
    )
    gram = lax.dot_general(
        factor_p, factor_p, CONTRACT_LAST, preferred_element_type=jnp.float32
    )
    product = jnp.dot(factor_p, compensated[...], preferred_element_type=jnp.float32)
    inverse = inverse_lower(gram)
    term[...] = jnp.dot(
        inverse, product, precision=lax.Precision.HIGHEST, preferred_element_type=jnp.float32
    ).astype(jnp.bfloat16)
    if p_half_out is not None:
        stacked = jnp.concatenate(three_parts(inverse), axis=0)
        p_parts = jnp.dot(stacked, factor_p, preferred_element_type=jnp.float32)
        p_hat = p_parts[:rank] + (p_parts[rank : 2 * rank] + p_parts[2 * rank :])
        p_half_out[...] = p_hat.astype(jnp.bfloat16)


def right(arrived, compensated, rank, keep):
    rows, hidden = compensated.shape
    shapes = [(rank, hidden)] + [(rank, rows)] * keep
    return pl.pallas_call(
        functools.partial(right_kernel, arrived.shape[1] // rank),
        in_specs=[pl.BlockSpec(memory_space=pltpu.VMEM)] * 2,
        out_specs=[pl.BlockSpec(memory_space=pltpu.VMEM)] * len(shapes),
        out_shape=[jax.ShapeDtypeStruct(shape, jnp.bfloat16) for shape in shapes],
        compiler_params=pltpu.CompilerParams(vmem_limit_bytes=24 * MIB),
        name="orthogonalize_and_right",
    )(arrived, compensated)


def add(mine, other):
    return mine.astype(jnp.float32) + other.astype(jnp.float32)


def all_but_last_sum(term, size):
    step = 1
    while True:
        other = lax.ppermute(term, "dp", [(i, i ^ step) for i in range(size)])
        step *= 2
        if step >= size:
            return term, other
        term = add(term, other).astype(jnp.bfloat16)


def left_kernel(mine, other, compensated, outgoing):
    replicas = outgoing.shape[0]
    block = compensated.shape[0] // replicas
    factor_q = add(mine[...], other[...]) / replicas
    factor_q = factor_q / jnp.sqrt(jnp.sum(factor_q * factor_q, axis=1, keepdims=True) + 1e-06)
    q_half = factor_q.astype(jnp.bfloat16)
    for s in range(replicas):
        local_p = lax.dot_general(
            q_half,
            compensated[s * block : (s + 1) * block, :],
            CONTRACT_LAST,
            preferred_element_type=jnp.float32,
        )
        store_tiles(outgoing, s * block // LANES, block // LANES, local_p.astype(jnp.bfloat16))


def left(mine, other, compensated, replicas):
    tall = compensated.shape[0] // replicas * mine.shape[0] // LANES
    return pl.pallas_call(
        left_kernel,
        in_specs=[pl.BlockSpec(memory_space=pltpu.VMEM)] * 3,
        out_specs=pl.BlockSpec(memory_space=pltpu.VMEM),
        out_shape=jax.ShapeDtypeStruct((replicas, tall, LANES), jnp.bfloat16),
        compiler_params=pltpu.CompilerParams(vmem_limit_bytes=24 * MIB),
        name="normalize_and_left",
    )(mine, other, compensated)


def last_kernel(
    replicas, mine, other, p_half, compensated, share,
    update, new_error, bucket_mean, update_held, error_held, sems, bucket_sem,
):
    tall = bucket_mean.shape[0]
    there = pl.ds(share.shape[0] - tall, tall)
    copies = [pltpu.make_async_copy(share.at[there], bucket_mean, bucket_sem)]
    copies[0].start()
    q_parts = jnp.concatenate(three_parts(add(mine[...], other[...]) / replicas), axis=0)
    for i, (at, size) in enumerate(pieces(compensated.shape[0])):
        where = slice(at, at + size)
        p_block = p_half[:, where].T
        block = jnp.dot(
            jnp.concatenate([p_block] * 3, axis=1), q_parts, preferred_element_type=jnp.float32
        )
        update_held[where, :] = block
        error_held[where, :] = (compensated[where, :].astype(jnp.float32) - block).astype(
            jnp.bfloat16
        )
        there = pl.ds(at, size)
        for j, (held, out) in enumerate(((update_held, update), (error_held, new_error))):
            copies.append(pltpu.make_async_copy(held.at[there], out.at[there], sems.at[j, i]))
            copies[-1].start(priority=j)
    for copy in copies:
        copy.wait()


def last(mine, other, p_half, compensated, share, replicas, bucket_tall):
    rows, hidden = compensated.shape
    in_vmem = pl.BlockSpec(memory_space=pltpu.VMEM)
    in_place = pl.BlockSpec(memory_space=pl.ANY)
    return pl.pallas_call(
        functools.partial(last_kernel, replicas),
        in_specs=[in_vmem] * 5,
        out_specs=[in_place] * 3,
        out_shape=[
            jax.ShapeDtypeStruct((rows, hidden), jnp.float32),
            jax.ShapeDtypeStruct((rows, hidden), jnp.bfloat16),
            jax.ShapeDtypeStruct((bucket_tall, LANES), jnp.float32),
        ],
        scratch_shapes=[
            pltpu.VMEM((rows, hidden), jnp.float32),
            pltpu.VMEM((rows, hidden), jnp.bfloat16),
            pltpu.SemaphoreType.DMA((2, len(pieces(rows)))),
            pltpu.SemaphoreType.DMA(()),
        ],
        compiler_params=pltpu.CompilerParams(vmem_limit_bytes=40 * MIB),
        name="update_and_error",
    )(mine, other, p_half, compensated, share)


def on_device(grads, error, q_start, bucket):
    replicas = lax.axis_size("dp")
    rows = grads.shape[1]
    rank = q_start.shape[1]
    bucket = bucket.reshape(replicas, -1, LANES)
    tall = rows // replicas * rank // LANES

    compensated, outgoing = first(grads[0], error[0], q_start.T, bucket)
    first_share = None
    for step in range(ITERS):
        share = jnp.sum(exchange(outgoing).astype(jnp.float32), axis=0) / replicas
        if step == 0:
            first_share = share
        factor_p = everywhere(share[:tall].astype(jnp.bfloat16), replicas)
        term, *p_half = right(factor_p, compensated, rank, step + 1 == ITERS)
        mine, other = all_but_last_sum(term, replicas)
        if step + 1 < ITERS:
            outgoing = left(mine, other, compensated, replicas)
    update, new_error, bucket_mean = last(
        mine, other, p_half[0], compensated, first_share, replicas, bucket.shape[1]
    )
    return (update, new_error[None], bucket_mean.reshape(-1))


def solution(mesh):
    return jax.shard_map(
        on_device,
        mesh=mesh,
        in_specs=(
            P("dp", None, "expert"),
            P("dp", None, "expert"),
            P("expert", None),
            P("dp", "expert"),
        ),
        out_specs=(P(None, "expert"), P("dp", None, "expert"), P(("expert", "dp"))),
        check_vma=False,
    )
```

```python
import functools

import jax
import jax.numpy as jnp
from jax import lax
from jax.experimental import pallas as pl
from jax.experimental.pallas import tpu as pltpu
from jax.sharding import PartitionSpec as P

ITERS = 2
LANES = 128
SUBLANES = 8
MIB = 1024 * 1024
CONTRACT_FIRST = (((0,), (0,)), ((), ()))
CONTRACT_LAST = (((1,), (1,)), ((), ()))


def exchange(chunks):
    return lax.all_to_all(chunks, "dp", split_axis=0, concat_axis=0, tiled=True)


def everywhere(share, size):
    return exchange(jnp.broadcast_to(share, (size,) + share.shape))


def three_parts(value):
    high = value.astype(jnp.bfloat16)
    rest = value - high.astype(jnp.float32)
    middle = rest.astype(jnp.bfloat16)
    low = (rest - middle.astype(jnp.float32)).astype(jnp.bfloat16)
    return high, middle, low


def pieces(rows):
    sizes = [LANES, LANES, 2 * LANES] + [4 * LANES] * (rows // (4 * LANES) - 1)
    return [(sum(sizes[:i]), size) for i, size in enumerate(sizes)]


def store_tiles(outgoing, first_tile, tiles, value):
    rank, columns = value.shape
    for at in range(columns // LANES):
        chunk, tile = divmod(first_tile + at, tiles)
        outgoing[chunk, tile * rank : (tile + 1) * rank, :] = value[:, at * LANES : (at + 1) * LANES]


def first_kernel(
    tiles, piece, grads, error, q_start, compensated, outgoing, landed, q_landed, sems, q_sem
):
    fetch_q = pltpu.make_async_copy(q_start, q_landed, q_sem)
    fetch_q.start()
    copies = []
    for i in range(grads.shape[0] // piece):
        where = pl.ds(i * piece, piece)
        for j, array in enumerate((grads, error)):
            copies.append(
                pltpu.make_async_copy(array.at[where], landed.at[j, where], sems.at[j, i])
            )
            copies[-1].start(priority=j)
    fetch_q.wait()
    q_half = q_landed[...].astype(jnp.bfloat16)
    for i in range(grads.shape[0] // piece):
        copies[2 * i].wait()
        copies[2 * i + 1].wait()
        where = slice(i * piece, (i + 1) * piece)
        block = (
            landed[0, where, :].astype(jnp.float32) + landed[1, where, :].astype(jnp.float32)
        ).astype(jnp.bfloat16)
        compensated[where, :] = block
        local_p = lax.dot_general(q_half, block, CONTRACT_LAST, preferred_element_type=jnp.float32)
        store_tiles(outgoing, i * piece // LANES, tiles, local_p.astype(jnp.bfloat16))


def first(grads, error, q_start, replicas):
    rows, hidden = grads.shape
    rank = q_start.shape[0]
    tiles = rows // replicas // LANES
    piece = 4 * LANES
    return pl.pallas_call(
        functools.partial(first_kernel, tiles, piece),
        in_specs=[pl.BlockSpec(memory_space=pl.ANY)] * 3,
        out_specs=[pl.BlockSpec(memory_space=pltpu.VMEM)] * 2,
        out_shape=[
            pltpu.VMEM((rows, hidden), jnp.bfloat16),
            pltpu.VMEM((replicas, tiles * rank, LANES), jnp.bfloat16),
        ],
        scratch_shapes=[
            pltpu.VMEM((2, rows, hidden), jnp.bfloat16),
            pltpu.VMEM(q_start.shape, jnp.float32),
            pltpu.SemaphoreType.DMA((2, rows // piece)),
            pltpu.SemaphoreType.DMA(()),
        ],
        compiler_params=pltpu.CompilerParams(vmem_limit_bytes=50 * MIB),
        name="compensate_and_left",
    )(grads, error, q_start)


def inverse_lower(gram):
    rank = gram.shape[0]
    row = lax.broadcasted_iota(jnp.int32, (SUBLANES, 2 * rank), 0)
    across = lax.broadcasted_iota(jnp.int32, (SUBLANES, 2 * rank), 1)
    both = jnp.concatenate([jnp.zeros((rank, rank), jnp.float32), gram], axis=1)
    starts = range(0, rank, SUBLANES)
    tiles = [
        jnp.where(across == row + at, 1.0, both[at : at + SUBLANES, :]) for at in starts
    ]
    inverse = []
    for top, base in enumerate(starts):
        columns = [
            [
                jnp.broadcast_to(tile[:, rank + k : rank + k + 1], tile.shape)
                for tile in tiles[top:]
            ]
            for k in range(base, base + SUBLANES)
        ]
        for j in range(SUBLANES):
            head = columns[j][0]
            reciprocal = 1.0 / head[j : j + 1, :]
            pivot_row = tiles[top][j : j + 1, :]
            for at in range(len(columns[j])):
                factor = columns[j][at] * reciprocal
                if at == 0:
                    factor = jnp.where(row > j, factor, 0.0)
                for i in range(j + 1, SUBLANES):
                    columns[i][at] = columns[i][at] - factor * head[i : i + 1, :]
                tiles[top + at] = tiles[top + at] - factor * pivot_row
        done = tiles[top]
        pivots = jnp.sum(
            jnp.where(across == row + (rank + base), done, 0.0), axis=1, keepdims=True
        )
        inverse.append(done[:, :rank] * lax.rsqrt(pivots))
    return jnp.concatenate(inverse, axis=0)


def columns_of(arrived, tiles, first_tile, count):
    rank = arrived.shape[1] // tiles
    parts = []
    for at in range(first_tile, first_tile + count):
        chunk, tile = divmod(at, tiles)
        parts.append(arrived[chunk, tile * rank : (tile + 1) * rank, :])
    return jnp.concatenate(parts, axis=1)


def right_kernel(tiles, arrived, compensated, term, inverse_out=None):
    factor_p = columns_of(arrived, tiles, 0, arrived.shape[0] * tiles)
    gram = lax.dot_general(
        factor_p, factor_p, CONTRACT_LAST, preferred_element_type=jnp.float32
    )
    product = jnp.dot(factor_p, compensated[...], preferred_element_type=jnp.float32)
    inverse = inverse_lower(gram)
    if inverse_out is not None:
        inverse_out[...] = inverse
    term[...] = jnp.dot(
        inverse, product, precision=lax.Precision.HIGHEST, preferred_element_type=jnp.float32
    ).astype(jnp.bfloat16)


def right(arrived, compensated, rank, keep):
    out_shape = [pltpu.VMEM((rank, compensated.shape[1]), jnp.bfloat16)]
    if keep:
        out_shape.append(pltpu.VMEM((rank, rank), jnp.float32))
    return pl.pallas_call(
        functools.partial(right_kernel, arrived.shape[1] // rank),
        in_specs=[pl.BlockSpec(memory_space=pltpu.VMEM)] * 2,
        out_specs=[pl.BlockSpec(memory_space=pltpu.VMEM)] * len(out_shape),
        out_shape=out_shape,
        compiler_params=pltpu.CompilerParams(vmem_limit_bytes=24 * MIB),
        name="orthogonalize_and_right",
    )(arrived, compensated)


def addends(term, size):
    def partner(by):
        return lax.ppermute(term, "dp", [(i, i ^ by) for i in range(size)])

    step = 1
    while 4 * step < size:
        term = (term.astype(jnp.float32) + partner(step).astype(jnp.float32)).astype(jnp.bfloat16)
        step *= 2
    return [term] + [partner(by) for by in (step, 2 * step, 3 * step)]


def sum_of(parts):
    one, two, three, four = [part[...].astype(jnp.float32) for part in parts]
    return (one + two) + (three + four)


def left_kernel(parts, compensated, bucket, outgoing, landed, sem):
    replicas = outgoing.shape[0]
    block = compensated.shape[0] // replicas
    fetch = pltpu.make_async_copy(bucket, landed, sem)
    fetch.start()
    factor_q = sum_of(parts) / replicas
    norm = jnp.sqrt(jnp.sum(factor_q * factor_q, axis=1, keepdims=True) + 1e-06)
    q_half = factor_q.astype(jnp.bfloat16)
    for s in range(replicas):
        local_p = lax.dot_general(
            q_half,
            compensated[s * block : (s + 1) * block, :],
            CONTRACT_LAST,
            preferred_element_type=jnp.float32,
        )
        local_p = (local_p / norm).astype(jnp.bfloat16)
        store_tiles(outgoing, s * block // LANES, block // LANES, local_p)
    fetch.wait()
    outgoing[:, -bucket.shape[1] :, :] = landed[...].astype(jnp.bfloat16)


def left(parts, compensated, bucket):
    replicas = bucket.shape[0]
    tall = compensated.shape[0] // replicas * parts[0].shape[0] // LANES + bucket.shape[1]
    in_vmem = pl.BlockSpec(memory_space=pltpu.VMEM)
    return pl.pallas_call(
        left_kernel,
        in_specs=[[in_vmem] * len(parts), in_vmem, pl.BlockSpec(memory_space=pl.ANY)],
        out_specs=in_vmem,
        out_shape=pltpu.VMEM((replicas, tall, LANES), jnp.bfloat16),
        scratch_shapes=[pltpu.VMEM(bucket.shape, jnp.float32), pltpu.SemaphoreType.DMA(())],
        compiler_params=pltpu.CompilerParams(vmem_limit_bytes=24 * MIB),
        name="normalize_and_left",
    )(parts, compensated, bucket)


def last_kernel(
    replicas, parts, inverse, arrived, compensated, share,
    update, new_error, bucket_mean, update_held, error_held, sems, bucket_sem,
):
    tall = bucket_mean.shape[0]
    there = pl.ds(share.shape[0] - tall, tall)
    copies = [pltpu.make_async_copy(share.at[there], bucket_mean, bucket_sem)]
    copies[0].start()
    tiles = compensated.shape[0] // replicas // LANES
    right = lax.dot_general(
        inverse[...],
        sum_of(parts) / replicas,
        CONTRACT_FIRST,
        precision=lax.Precision.HIGHEST,
        preferred_element_type=jnp.float32,
    )
    right = jnp.concatenate(three_parts(right), axis=0)
    for i, (at, size) in enumerate(pieces(compensated.shape[0])):
        where = slice(at, at + size)
        p_block = columns_of(arrived, tiles, at // LANES, size // LANES).T
        block = jnp.dot(
            jnp.concatenate([p_block] * 3, axis=1), right, preferred_element_type=jnp.float32
        )
        update_held[where, :] = block
        error_held[where, :] = (compensated[where, :].astype(jnp.float32) - block).astype(
            jnp.bfloat16
        )
        there = pl.ds(at, size)
        for j, (held, out) in enumerate(((update_held, update), (error_held, new_error))):
            copies.append(pltpu.make_async_copy(held.at[there], out.at[there], sems.at[j, i]))
            copies[-1].start(priority=j)
    for copy in copies:
        copy.wait()


def last(parts, inverse, arrived, compensated, share, replicas, bucket_tall):
    rows, hidden = compensated.shape
    in_vmem = pl.BlockSpec(memory_space=pltpu.VMEM)
    return pl.pallas_call(
        functools.partial(last_kernel, replicas),
        in_specs=[[in_vmem] * len(parts)] + [in_vmem] * 4,
        out_specs=[pl.BlockSpec(memory_space=pl.ANY)] * 3,
        out_shape=[
            jax.ShapeDtypeStruct((rows, hidden), jnp.float32),
            jax.ShapeDtypeStruct((rows, hidden), jnp.bfloat16),
            jax.ShapeDtypeStruct((bucket_tall, LANES), jnp.float32),
        ],
        scratch_shapes=[
            pltpu.VMEM((rows, hidden), jnp.float32),
            pltpu.VMEM((rows, hidden), jnp.bfloat16),
            pltpu.SemaphoreType.DMA((2, len(pieces(rows)))),
            pltpu.SemaphoreType.DMA(()),
        ],
        compiler_params=pltpu.CompilerParams(vmem_limit_bytes=40 * MIB),
        name="update_and_error",
    )(parts, inverse, arrived, compensated, share)


def on_device(grads, error, q_start, bucket):
    replicas = lax.axis_size("dp")
    rows = grads.shape[1]
    rank = q_start.shape[1]
    bucket = bucket.reshape(replicas, -1, LANES)
    tall = rows // replicas * rank // LANES
    compensated, outgoing = first(grads[0], error[0], q_start.T, replicas)
    for step in range(ITERS):
        share = jnp.sum(exchange(outgoing).astype(jnp.float32), axis=0) / replicas
        factor_p = everywhere(share[:tall].astype(jnp.bfloat16), replicas)
        term, *inverse = right(factor_p, compensated, rank, step + 1 == ITERS)
        parts = addends(term, replicas)
        if step + 1 < ITERS:
            outgoing = left(parts, compensated, bucket)
    update, new_error, bucket_mean = last(
        parts, inverse[0], factor_p, compensated, share, replicas, bucket.shape[1]
    )
    return (update, new_error[None], bucket_mean.reshape(-1))


def solution(mesh):
    return jax.shard_map(
        on_device,
        mesh=mesh,
        in_specs=(
            P("dp", None, "expert"),
            P("dp", None, "expert"),
            P("expert", None),
            P("dp", "expert"),
        ),
        out_specs=(P(None, "expert"), P("dp", None, "expert"), P(("expert", "dp"))),
        check_vma=False,
    )
```

```python
import functools

import jax
import jax.numpy as jnp
from jax import lax
from jax.experimental import pallas as pl
from jax.experimental.pallas import tpu as pltpu
from jax.sharding import PartitionSpec as P

ITERS = 2
LANES = 128
SUBLANES = 8
MIB = 1024 * 1024
CONTRACT_FIRST = (((0,), (0,)), ((), ()))
CONTRACT_LAST = (((1,), (1,)), ((), ()))


def exchange(chunks):
    return lax.all_to_all(chunks, "dp", split_axis=0, concat_axis=0, tiled=True)


def everywhere(share, size):
    return exchange(jnp.broadcast_to(share, (size,) + share.shape))


def three_parts(value):
    high = value.astype(jnp.bfloat16)
    rest = value - high.astype(jnp.float32)
    middle = rest.astype(jnp.bfloat16)
    low = (rest - middle.astype(jnp.float32)).astype(jnp.bfloat16)
    return high, middle, low


def pieces(rows):
    sizes = [LANES, LANES, 2 * LANES] + [4 * LANES] * (rows // (4 * LANES) - 1)
    return [(sum(sizes[:i]), size) for i, size in enumerate(sizes)]


def owner(block, replicas):
    x, j = divmod(block, replicas // 2)
    return 2 * j + x


def store_tiles(chunk, value):
    rank, columns = value.shape
    for tile in range(columns // LANES):
        chunk[tile * rank : (tile + 1) * rank, :] = value[:, tile * LANES : (tile + 1) * LANES]


def first_kernel(replicas, flip, grads, error, q_start, *refs):
    compensated, outgoing, landed, q_landed, total, sems, out_sems, q_sem = refs[-8:]
    fetch_q = pltpu.make_async_copy(q_start, q_landed, q_sem)
    fetch_q.start()
    me = lax.axis_index("dp")
    half = replicas // 2
    block = grads.shape[0] // replicas
    starts, copies = [], []
    for k in range(half):
        start = (((me & 1) ^ flip) * half + ((me >> 1) ^ k)) * block
        starts.append(pl.multiple_of(start, block))
        for j, array in enumerate((grads, error)):
            copies.append(
                pltpu.make_async_copy(
                    array.at[pl.ds(starts[k], block)], landed.at[j, k], sems.at[j, k]
                )
            )
            copies[-1].start(priority=j)
    fetch_q.wait()
    q_half = q_landed[...].astype(jnp.bfloat16)
    for k in range(half):
        copies[2 * k].wait()
        copies[2 * k + 1].wait()
        value = (landed[0, k].astype(jnp.float32) + landed[1, k].astype(jnp.float32)).astype(
            jnp.bfloat16
        )
        total[k] = value
        copies.append(
            pltpu.make_async_copy(
                total.at[k], compensated.at[pl.ds(starts[k], block)], out_sems.at[k]
            )
        )
        copies[-1].start()
        local_p = lax.dot_general(q_half, value, CONTRACT_LAST, preferred_element_type=jnp.float32)
        store_tiles(outgoing.at[k], local_p.astype(jnp.bfloat16))
    for copy in copies[-half:]:
        copy.wait()


def first(grads, error, q_start, replicas, flip, compensated=None):
    rows, hidden = grads.shape
    rank = q_start.shape[0]
    block = rows // replicas
    half = replicas // 2
    in_place = pl.BlockSpec(memory_space=pl.ANY)
    before = [] if compensated is None else [compensated]
    return pl.pallas_call(
        functools.partial(first_kernel, replicas, flip),
        in_specs=[in_place] * (3 + len(before)),
        out_specs=[in_place, pl.BlockSpec(memory_space=pltpu.VMEM)],
        out_shape=[
            pltpu.VMEM((rows, hidden), jnp.bfloat16),
            pltpu.VMEM((half, block // LANES * rank, LANES), jnp.bfloat16),
        ],
        input_output_aliases={3: 0} if before else {},
        scratch_shapes=[
            pltpu.VMEM((2, half, block, hidden), jnp.bfloat16),
            pltpu.VMEM(q_start.shape, jnp.float32),
            pltpu.VMEM((half, block, hidden), jnp.bfloat16),
            pltpu.SemaphoreType.DMA((2, half)),
            pltpu.SemaphoreType.DMA((half,)),
            pltpu.SemaphoreType.DMA(()),
        ],
        compiler_params=pltpu.CompilerParams(vmem_limit_bytes=50 * MIB),
        cost_estimate=pl.CostEstimate(
            flops=rows * hidden * rank, bytes_accessed=2 * rows * hidden, transcendentals=0
        ),
        name="compensate_and_left",
    )(grads, error, q_start, *before)


def first_share(grads, error, q_start, replicas):
    def partner(value, by):
        return lax.ppermute(value, "dp", [(i, i ^ by) for i in range(replicas)])

    compensated, theirs = first(grads, error, q_start, replicas, 1)
    arrived = partner(theirs, 1)
    compensated, mine = first(grads, error, q_start, replicas, 0, compensated)
    pairs = [
        arrived[k].astype(jnp.float32) + mine[k].astype(jnp.float32) for k in range(replicas // 2)
    ]
    total = pairs[0]
    for value in [
        partner(pairs[k].astype(jnp.bfloat16), 2 * k) for k in range(1, replicas // 2)
    ]:
        total = total + value.astype(jnp.float32)
    return compensated, total


def inverse_lower(gram):
    rank = gram.shape[0]
    row = lax.broadcasted_iota(jnp.int32, (SUBLANES, 2 * rank), 0)
    across = lax.broadcasted_iota(jnp.int32, (SUBLANES, 2 * rank), 1)
    both = jnp.concatenate([jnp.zeros((rank, rank), jnp.float32), gram], axis=1)
    starts = range(0, rank, SUBLANES)
    tiles = [
        jnp.where(across == row + at, 1.0, both[at : at + SUBLANES, :]) for at in starts
    ]
    inverse = []
    for top, base in enumerate(starts):
        columns = [
            [
                jnp.broadcast_to(tile[:, rank + k : rank + k + 1], tile.shape)
                for tile in tiles[top:]
            ]
            for k in range(base, base + SUBLANES)
        ]
        for j in range(SUBLANES):
            head = columns[j][0]
            reciprocal = 1.0 / head[j : j + 1, :]
            pivot_row = tiles[top][j : j + 1, :]
            for at in range(len(columns[j])):
                factor = columns[j][at] * reciprocal
                if at == 0:
                    factor = jnp.where(row > j, factor, 0.0)
                for i in range(j + 1, SUBLANES):
                    columns[i][at] = columns[i][at] - factor * head[i : i + 1, :]
                tiles[top + at] = tiles[top + at] - factor * pivot_row
        done = tiles[top]
        pivots = jnp.sum(
            jnp.where(across == row + (rank + base), done, 0.0), axis=1, keepdims=True
        )
        inverse.append(done[:, :rank] * lax.rsqrt(pivots))
    return jnp.concatenate(inverse, axis=0)


def columns_of(arrived, tiles, first_tile, count):
    rank = arrived.shape[1] // tiles
    parts = []
    for at in range(first_tile, first_tile + count):
        block, tile = divmod(at, tiles)
        chunk = owner(block, arrived.shape[0])
        parts.append(arrived[chunk, tile * rank : (tile + 1) * rank, :])
    return jnp.concatenate(parts, axis=1)


def right_kernel(tiles, arrived, compensated, term, inverse_out=None):
    factor_p = columns_of(arrived, tiles, 0, arrived.shape[0] * tiles)
    gram = lax.dot_general(
        factor_p, factor_p, CONTRACT_LAST, preferred_element_type=jnp.float32
    )
    product = jnp.dot(factor_p, compensated[...], preferred_element_type=jnp.float32)
    inverse = inverse_lower(gram)
    if inverse_out is not None:
        inverse_out[...] = inverse
    term[...] = jnp.dot(
        inverse, product, precision=lax.Precision.HIGHEST, preferred_element_type=jnp.float32
    ).astype(jnp.bfloat16)


def right(arrived, compensated, rank, keep):
    out_shape = [pltpu.VMEM((rank, compensated.shape[1]), jnp.bfloat16)]
    if keep:
        out_shape.append(pltpu.VMEM((rank, rank), jnp.float32))
    return pl.pallas_call(
        functools.partial(right_kernel, arrived.shape[1] // rank),
        in_specs=[pl.BlockSpec(memory_space=pltpu.VMEM)] * 2,
        out_specs=[pl.BlockSpec(memory_space=pltpu.VMEM)] * len(out_shape),
        out_shape=out_shape,
        compiler_params=pltpu.CompilerParams(vmem_limit_bytes=24 * MIB),
        name="orthogonalize_and_right",
    )(arrived, compensated)


def addends(term, size):
    def partner(by):
        return lax.ppermute(term, "dp", [(i, i ^ by) for i in range(size)])

    step = 1
    while 4 * step < size:
        term = (term.astype(jnp.float32) + partner(step).astype(jnp.float32)).astype(jnp.bfloat16)
        step *= 2
    return [term] + [partner(by) for by in (step, 2 * step, 3 * step)]


def sum_of(parts):
    one, two, three, four = [part[...].astype(jnp.float32) for part in parts]
    return (one + two) + (three + four)


def left_kernel(parts, compensated, bucket, outgoing, landed, sem):
    replicas = outgoing.shape[0]
    block = compensated.shape[0] // replicas
    fetch = pltpu.make_async_copy(bucket, landed, sem)
    fetch.start()
    factor_q = sum_of(parts) / replicas
    norm = jnp.sqrt(jnp.sum(factor_q * factor_q, axis=1, keepdims=True) + 1e-06)
    q_half = factor_q.astype(jnp.bfloat16)
    for s in range(replicas):
        local_p = lax.dot_general(
            q_half,
            compensated[s * block : (s + 1) * block, :],
            CONTRACT_LAST,
            preferred_element_type=jnp.float32,
        )
        store_tiles(outgoing.at[owner(s, replicas)], (local_p / norm).astype(jnp.bfloat16))
    fetch.wait()
    outgoing[:, -bucket.shape[1] :, :] = landed[...].astype(jnp.bfloat16)


def left(parts, compensated, bucket):
    replicas = bucket.shape[0]
    tall = compensated.shape[0] // replicas * parts[0].shape[0] // LANES + bucket.shape[1]
    in_vmem = pl.BlockSpec(memory_space=pltpu.VMEM)
    return pl.pallas_call(
        left_kernel,
        in_specs=[[in_vmem] * len(parts), in_vmem, pl.BlockSpec(memory_space=pl.ANY)],
        out_specs=in_vmem,
        out_shape=pltpu.VMEM((replicas, tall, LANES), jnp.bfloat16),
        scratch_shapes=[pltpu.VMEM(bucket.shape, jnp.float32), pltpu.SemaphoreType.DMA(())],
        compiler_params=pltpu.CompilerParams(vmem_limit_bytes=24 * MIB),
        name="normalize_and_left",
    )(parts, compensated, bucket)


def last_kernel(
    replicas, parts, inverse, arrived, compensated, share,
    update, new_error, bucket_mean, update_held, error_held, sems, bucket_sem,
):
    tall = bucket_mean.shape[0]
    there = pl.ds(share.shape[0] - tall, tall)
    copies = [pltpu.make_async_copy(share.at[there], bucket_mean, bucket_sem)]
    copies[0].start()
    tiles = compensated.shape[0] // replicas // LANES
    right = lax.dot_general(
        inverse[...],
        sum_of(parts) / replicas,
        CONTRACT_FIRST,
        precision=lax.Precision.HIGHEST,
        preferred_element_type=jnp.float32,
    )
    right = jnp.concatenate(three_parts(right), axis=0)
    for i, (at, size) in enumerate(pieces(compensated.shape[0])):
        where = slice(at, at + size)
        p_block = columns_of(arrived, tiles, at // LANES, size // LANES).T
        block = jnp.dot(
            jnp.concatenate([p_block] * 3, axis=1), right, preferred_element_type=jnp.float32
        )
        update_held[where, :] = block
        error_held[where, :] = (compensated[where, :].astype(jnp.float32) - block).astype(
            jnp.bfloat16
        )
        there = pl.ds(at, size)
        for j, (held, out) in enumerate(((update_held, update), (error_held, new_error))):
            copies.append(pltpu.make_async_copy(held.at[there], out.at[there], sems.at[j, i]))
            copies[-1].start(priority=j)
    for copy in copies:
        copy.wait()


def last(parts, inverse, arrived, compensated, share, replicas, bucket_tall):
    rows, hidden = compensated.shape
    in_vmem = pl.BlockSpec(memory_space=pltpu.VMEM)
    return pl.pallas_call(
        functools.partial(last_kernel, replicas),
        in_specs=[[in_vmem] * len(parts)] + [in_vmem] * 4,
        out_specs=[pl.BlockSpec(memory_space=pl.ANY)] * 3,
        out_shape=[
            jax.ShapeDtypeStruct((rows, hidden), jnp.float32),
            jax.ShapeDtypeStruct((rows, hidden), jnp.bfloat16),
            jax.ShapeDtypeStruct((bucket_tall, LANES), jnp.float32),
        ],
        scratch_shapes=[
            pltpu.VMEM((rows, hidden), jnp.float32),
            pltpu.VMEM((rows, hidden), jnp.bfloat16),
            pltpu.SemaphoreType.DMA((2, len(pieces(rows)))),
            pltpu.SemaphoreType.DMA(()),
        ],
        compiler_params=pltpu.CompilerParams(vmem_limit_bytes=40 * MIB),
        name="update_and_error",
    )(parts, inverse, arrived, compensated, share)


def on_device(grads, error, q_start, bucket):
    replicas = lax.axis_size("dp")
    rows = grads.shape[1]
    rank = q_start.shape[1]
    bucket = bucket.reshape(replicas, -1, LANES)
    tall = rows // replicas * rank // LANES
    compensated, share = first_share(grads[0], error[0], q_start.T, replicas)
    for step in range(ITERS):
        if step > 0:
            share = jnp.sum(exchange(outgoing).astype(jnp.float32), axis=0)
        share = share / replicas
        factor_p = everywhere(share[:tall].astype(jnp.bfloat16), replicas)
        term, *inverse = right(factor_p, compensated, rank, step + 1 == ITERS)
        parts = addends(term, replicas)
        if step + 1 < ITERS:
            outgoing = left(parts, compensated, bucket)
    update, new_error, bucket_mean = last(
        parts, inverse[0], factor_p, compensated, share, replicas, bucket.shape[1]
    )
    return (update, new_error[None], bucket_mean.reshape(-1))


def solution(mesh):
    return jax.shard_map(
        on_device,
        mesh=mesh,
        in_specs=(
            P("dp", None, "expert"),
            P("dp", None, "expert"),
            P("expert", None),
            P("dp", "expert"),
        ),
        out_specs=(P(None, "expert"), P("dp", None, "expert"), P(("expert", "dp"))),
        check_vma=False,
    )
```

```python
import functools

import jax
import jax.numpy as jnp
from jax import lax
from jax.experimental import pallas as pl
from jax.experimental.pallas import tpu as pltpu
from jax.sharding import PartitionSpec as P

ITERS = 2
LANES = 128
SUBLANES = 8
MIB = 1024 * 1024
CONTRACT_FIRST = (((0,), (0,)), ((), ()))
CONTRACT_LAST = (((1,), (1,)), ((), ()))


def exchange(chunks):
    return lax.all_to_all(chunks, "dp", split_axis=0, concat_axis=0, tiled=True)


def everywhere(share, size):
    return exchange(jnp.broadcast_to(share, (size,) + share.shape))


def three_parts(value):
    high = value.astype(jnp.bfloat16)
    rest = value - high.astype(jnp.float32)
    middle = rest.astype(jnp.bfloat16)
    low = (rest - middle.astype(jnp.float32)).astype(jnp.bfloat16)
    return high, middle, low


def pieces(rows, grow):
    sizes = [4 * LANES] * (rows // (4 * LANES))
    if grow:
        sizes[:1] = [LANES, LANES, 2 * LANES]
    return [(sum(sizes[:i]), size) for i, size in enumerate(sizes)]


def store_tiles(chunk, value):
    rank, columns = value.shape
    for tile in range(columns // LANES):
        chunk[tile * rank : (tile + 1) * rank, :] = value[:, tile * LANES : (tile + 1) * LANES]


def first_kernel(replicas, flip, grads, error, q_start, compensated, outgoing, *scratch):
    landed, q_landed, sems, q_sem = scratch
    fetch_q = pltpu.make_async_copy(q_start, q_landed, q_sem)
    fetch_q.start()
    me = lax.axis_index("dp")
    half = replicas // 2
    block = grads.shape[0] // replicas
    starts, copies = [], []
    for k in range(half):
        starts.append(pl.multiple_of(((me >> 1) ^ k) * block, block))
        there = pl.multiple_of(((me & 1) ^ flip) * (half * block) + starts[k], block)
        for j, array in enumerate((grads, error)):
            copies.append(
                pltpu.make_async_copy(
                    array.at[pl.ds(there, block)], landed.at[j, k], sems.at[j, k]
                )
            )
            copies[-1].start(priority=j)
    fetch_q.wait()
    q_half = q_landed[...].astype(jnp.bfloat16)
    for k in range(half):
        copies[2 * k].wait()
        copies[2 * k + 1].wait()
        value = (landed[0, k].astype(jnp.float32) + landed[1, k].astype(jnp.float32)).astype(
            jnp.bfloat16
        )
        compensated[pl.ds(starts[k], block), :] = value
        local_p = lax.dot_general(q_half, value, CONTRACT_LAST, preferred_element_type=jnp.float32)
        store_tiles(outgoing.at[k], local_p.astype(jnp.bfloat16))


def first(grads, error, q_start, replicas, flip):
    rows, hidden = grads.shape
    rank = q_start.shape[0]
    block = rows // replicas
    half = replicas // 2
    return pl.pallas_call(
        functools.partial(first_kernel, replicas, flip),
        in_specs=[pl.BlockSpec(memory_space=pl.ANY)] * 3,
        out_specs=[pl.BlockSpec(memory_space=pltpu.VMEM)] * 2,
        out_shape=[
            pltpu.VMEM((half * block, hidden), jnp.bfloat16),
            pltpu.VMEM((half, block // LANES * rank, LANES), jnp.bfloat16),
        ],
        scratch_shapes=[
            pltpu.VMEM((2, half, block, hidden), jnp.bfloat16),
            pltpu.VMEM(q_start.shape, jnp.float32),
            pltpu.SemaphoreType.DMA((2, half)),
            pltpu.SemaphoreType.DMA(()),
        ],
        compiler_params=pltpu.CompilerParams(vmem_limit_bytes=53 * MIB),
        cost_estimate=pl.CostEstimate(
            flops=rows * hidden * rank, bytes_accessed=2 * rows * hidden, transcendentals=0
        ),
        name="compensate_and_left",
    )(grads, error, q_start)


def partner(value, by, size):
    return lax.ppermute(value, "dp", [(i, i ^ by) for i in range(size)])


def first_share(grads, error, q_start, replicas):
    other, theirs = first(grads, error, q_start, replicas, 1)
    arrived = partner(theirs, 1, replicas)
    own, mine = first(grads, error, q_start, replicas, 0)
    pairs = [
        arrived[k].astype(jnp.float32) + mine[k].astype(jnp.float32) for k in range(replicas // 2)
    ]
    total = pairs[0]
    for value in [
        partner(pairs[k].astype(jnp.bfloat16), 2 * k, replicas) for k in range(1, replicas // 2)
    ]:
        total = total + value.astype(jnp.float32)
    return (own, other), total


def inverse_lower(gram):
    rank = gram.shape[0]
    row = lax.broadcasted_iota(jnp.int32, (SUBLANES, 2 * rank), 0)
    across = lax.broadcasted_iota(jnp.int32, (SUBLANES, 2 * rank), 1)
    both = jnp.concatenate([jnp.zeros((rank, rank), jnp.float32), gram], axis=1)
    starts = range(0, rank, SUBLANES)
    tiles = [
        jnp.where(across == row + at, 1.0, both[at : at + SUBLANES, :]) for at in starts
    ]
    inverse = []
    for top, base in enumerate(starts):
        columns = [
            [
                jnp.broadcast_to(tile[:, rank + k : rank + k + 1], tile.shape)
                for tile in tiles[top:]
            ]
            for k in range(base, base + SUBLANES)
        ]
        for j in range(SUBLANES):
            head = columns[j][0]
            reciprocal = 1.0 / head[j : j + 1, :]
            pivot_row = tiles[top][j : j + 1, :]
            for at in range(len(columns[j])):
                factor = columns[j][at] * reciprocal
                if at == 0:
                    factor = jnp.where(row > j, factor, 0.0)
                for i in range(j + 1, SUBLANES):
                    columns[i][at] = columns[i][at] - factor * head[i : i + 1, :]
                tiles[top + at] = tiles[top + at] - factor * pivot_row
        done = tiles[top]
        pivots = jnp.sum(
            jnp.where(across == row + (rank + base), done, 0.0), axis=1, keepdims=True
        )
        inverse.append(done[:, :rank] * lax.rsqrt(pivots))
    return jnp.concatenate(inverse, axis=0)


def columns_of(arrived, tiles, x, first_tile, count):
    rank = arrived.shape[1] // tiles
    parts = []
    for at in range(first_tile, first_tile + count):
        block, tile = divmod(at, tiles)
        parts.append(arrived[2 * block + x, tile * rank : (tile + 1) * rank, :])
    return jnp.concatenate(parts, axis=1)


def right_kernel(tiles, arrived, halves, term, inverse_out=None):
    x = lax.axis_index("dp") & 1
    count = arrived.shape[0] // 2 * tiles
    factors = [columns_of(arrived, tiles, x ^ flip, 0, count) for flip in range(2)]
    factor_p = jnp.concatenate(factors, axis=1)
    gram = lax.dot_general(
        factor_p, factor_p, CONTRACT_LAST, preferred_element_type=jnp.float32
    )
    product = sum(
        jnp.dot(factor, half[...], preferred_element_type=jnp.float32)
        for factor, half in zip(factors, halves)
    )
    inverse = inverse_lower(gram)
    if inverse_out is not None:
        inverse_out[...] = inverse
    term[...] = jnp.dot(
        inverse, product, precision=lax.Precision.HIGHEST, preferred_element_type=jnp.float32
    ).astype(jnp.bfloat16)


def right(arrived, halves, rank, keep):
    out_shape = [pltpu.VMEM((rank, halves[0].shape[1]), jnp.bfloat16)]
    in_vmem = pl.BlockSpec(memory_space=pltpu.VMEM)
    if keep:
        out_shape.append(pltpu.VMEM((rank, rank), jnp.float32))
    return pl.pallas_call(
        functools.partial(right_kernel, arrived.shape[1] // rank),
        in_specs=[in_vmem, (in_vmem, in_vmem)],
        out_specs=[in_vmem] * len(out_shape),
        out_shape=out_shape,
        compiler_params=pltpu.CompilerParams(vmem_limit_bytes=24 * MIB),
        name="orthogonalize_and_right",
    )(arrived, halves)


def addends(term, size):
    one, two, three, four = [
        part.astype(jnp.float32) for part in [term] + [partner(term, by, size) for by in (1, 2, 3)]
    ]
    term = ((one + two) + (three + four)).astype(jnp.bfloat16)
    step = 4
    while 2 * step < size:
        term = (term.astype(jnp.float32) + partner(term, step, size).astype(jnp.float32)).astype(
            jnp.bfloat16
        )
        step *= 2
    return [term, partner(term, step, size)]


def sum_of(parts):
    one, two = [part[...].astype(jnp.float32) for part in parts]
    return one + two


def left_kernel(parts, halves, bucket, outgoing, landed, sem):
    replicas = outgoing.shape[0]
    block = 2 * halves[0].shape[0] // replicas
    x = lax.axis_index("dp") & 1
    fetch = pltpu.make_async_copy(bucket, landed, sem)
    fetch.start()
    factor_q = sum_of(parts) / replicas
    norm = jnp.sqrt(jnp.sum(factor_q * factor_q, axis=1, keepdims=True) + 1e-06)
    q_half = factor_q.astype(jnp.bfloat16)
    for flip, half in enumerate(halves):
        for j in range(replicas // 2):
            local_p = lax.dot_general(
                q_half,
                half[j * block : (j + 1) * block, :],
                CONTRACT_LAST,
                preferred_element_type=jnp.float32,
            )
            store_tiles(outgoing.at[2 * j + (x ^ flip)], (local_p / norm).astype(jnp.bfloat16))
    fetch.wait()
    outgoing[:, -bucket.shape[1] :, :] = landed[...].astype(jnp.bfloat16)


def left(parts, halves, bucket):
    replicas = bucket.shape[0]
    tall = 2 * halves[0].shape[0] // replicas * parts[0].shape[0] // LANES + bucket.shape[1]
    in_vmem = pl.BlockSpec(memory_space=pltpu.VMEM)
    return pl.pallas_call(
        left_kernel,
        in_specs=[[in_vmem] * len(parts), (in_vmem, in_vmem), pl.BlockSpec(memory_space=pl.ANY)],
        out_specs=in_vmem,
        out_shape=pltpu.VMEM((replicas, tall, LANES), jnp.bfloat16),
        scratch_shapes=[pltpu.VMEM(bucket.shape, jnp.float32), pltpu.SemaphoreType.DMA(())],
        compiler_params=pltpu.CompilerParams(vmem_limit_bytes=24 * MIB),
        name="normalize_and_left",
    )(parts, halves, bucket)


def last_kernel(
    replicas, parts, inverse, arrived, halves, share,
    update, new_error, bucket_mean, update_held, error_held, sems, bucket_sem,
):
    tall = bucket_mean.shape[0]
    there = pl.ds(share.shape[0] - tall, tall)
    copies = [pltpu.make_async_copy(share.at[there], bucket_mean, bucket_sem)]
    copies[0].start()
    rows, hidden = halves[0].shape
    tiles = 2 * rows // replicas // LANES
    x = lax.axis_index("dp") & 1
    right = lax.dot_general(
        inverse[...],
        sum_of(parts) / replicas,
        CONTRACT_FIRST,
        precision=lax.Precision.HIGHEST,
        preferred_element_type=jnp.float32,
    )
    right = jnp.concatenate(three_parts(right), axis=0)
    for flip, half in enumerate(halves):
        for i, (at, size) in enumerate(pieces(rows, flip == 0)):
            where = slice(at, at + size)
            p_block = columns_of(arrived, tiles, x ^ flip, at // LANES, size // LANES).T
            block = jnp.dot(
                jnp.concatenate([p_block] * 3, axis=1), right, preferred_element_type=jnp.float32
            )
            update_held[flip, where, :] = block
            error_held[flip, where, :] = (half[where, :].astype(jnp.float32) - block).astype(
                jnp.bfloat16
            )
            there = pl.ds(pl.multiple_of((x ^ flip) * rows + at, LANES), size)
            for j, (held, out) in enumerate(((update_held, update), (error_held, new_error))):
                copies.append(
                    pltpu.make_async_copy(
                        held.at[flip, pl.ds(at, size)], out.at[there], sems.at[j, flip, i]
                    )
                )
                copies[-1].start(priority=j)
    for copy in copies:
        copy.wait()


def last(parts, inverse, arrived, halves, share, replicas, bucket_tall):
    rows, hidden = halves[0].shape
    in_vmem = pl.BlockSpec(memory_space=pltpu.VMEM)
    return pl.pallas_call(
        functools.partial(last_kernel, replicas),
        in_specs=[[in_vmem] * len(parts), in_vmem, in_vmem, (in_vmem, in_vmem), in_vmem],
        out_specs=[pl.BlockSpec(memory_space=pl.ANY)] * 3,
        out_shape=[
            jax.ShapeDtypeStruct((2 * rows, hidden), jnp.float32),
            jax.ShapeDtypeStruct((2 * rows, hidden), jnp.bfloat16),
            jax.ShapeDtypeStruct((bucket_tall, LANES), jnp.float32),
        ],
        scratch_shapes=[
            pltpu.VMEM((2, rows, hidden), jnp.float32),
            pltpu.VMEM((2, rows, hidden), jnp.bfloat16),
            pltpu.SemaphoreType.DMA((2, 2, len(pieces(rows, True)))),
            pltpu.SemaphoreType.DMA(()),
        ],
        compiler_params=pltpu.CompilerParams(vmem_limit_bytes=40 * MIB),
        name="update_and_error",
    )(parts, inverse, arrived, halves, share)


def on_device(grads, error, q_start, bucket):
    replicas = lax.axis_size("dp")
    rows = grads.shape[1]
    rank = q_start.shape[1]
    bucket = bucket.reshape(replicas, -1, LANES)
    tall = rows // replicas * rank // LANES
    halves, share = first_share(grads[0], error[0], q_start.T, replicas)
    for step in range(ITERS):
        if step > 0:
            share = jnp.sum(exchange(outgoing).astype(jnp.float32), axis=0)
        share = share / replicas
        factor_p = everywhere(share[:tall].astype(jnp.bfloat16), replicas)
        term, *inverse = right(factor_p, halves, rank, step + 1 == ITERS)
        parts = addends(term, replicas)
        if step + 1 < ITERS:
            outgoing = left(parts, halves, bucket)
    update, new_error, bucket_mean = last(
        parts, inverse[0], factor_p, halves, share, replicas, bucket.shape[1]
    )
    return (update, new_error[None], bucket_mean.reshape(-1))


def solution(mesh):
    return jax.shard_map(
        on_device,
        mesh=mesh,
        in_specs=(
            P("dp", None, "expert"),
            P("dp", None, "expert"),
            P("expert", None),
            P("dp", "expert"),
        ),
        out_specs=(P(None, "expert"), P("dp", None, "expert"), P(("expert", "dp"))),
        check_vma=False,
    )
```

```python
import functools

import jax
import jax.numpy as jnp
from jax import lax
from jax.experimental import pallas as pl
from jax.experimental.pallas import tpu as pltpu
from jax.sharding import PartitionSpec as P

ITERS = 2
LANES = 128
SUBLANES = 8
MIB = 1024 * 1024
CONTRACT_FIRST = (((0,), (0,)), ((), ()))
CONTRACT_LAST = (((1,), (1,)), ((), ()))


def exchange(chunks):
    return lax.all_to_all(chunks, "dp", split_axis=0, concat_axis=0, tiled=True)


def pieces(rows, grow):
    sizes = [4 * LANES] * (rows // (4 * LANES))
    if grow:
        sizes[:1] = [LANES, LANES, 2 * LANES]
    return [(sum(sizes[:i]), size) for i, size in enumerate(sizes)]


def store_tiles(chunk, value):
    rank, columns = value.shape
    for tile in range(columns // LANES):
        chunk[tile * rank : (tile + 1) * rank, :] = value[:, tile * LANES : (tile + 1) * LANES]


def three_parts(value):
    high = value.astype(jnp.bfloat16)
    rest = value - high.astype(jnp.float32)
    middle = rest.astype(jnp.bfloat16)
    low = (rest - middle.astype(jnp.float32)).astype(jnp.bfloat16)
    return high, middle, low


def first_kernel(replicas, flip, grads, error, q_start, compensated, outgoing, *scratch):
    landed, q_landed, sems, q_sem = scratch
    fetch_q = pltpu.make_async_copy(q_start, q_landed, q_sem)
    fetch_q.start()
    me = lax.axis_index("dp")
    half = replicas // 2
    block = grads.shape[0] // replicas
    starts, copies = [], []
    for k in range(half):
        starts.append(pl.multiple_of(((me >> 1) ^ k) * block, block))
        there = pl.multiple_of(((me & 1) ^ flip) * (half * block) + starts[k], block)
        for j, array in enumerate((grads, error)):
            copies.append(
                pltpu.make_async_copy(
                    array.at[pl.ds(there, block)], landed.at[j, k], sems.at[j, k]
                )
            )
            copies[-1].start(priority=j)
    fetch_q.wait()
    q_half = q_landed[...].astype(jnp.bfloat16)
    for k in range(half):
        copies[2 * k].wait()
        copies[2 * k + 1].wait()
        value = (landed[0, k].astype(jnp.float32) + landed[1, k].astype(jnp.float32)).astype(
            jnp.bfloat16
        )
        compensated[pl.ds(starts[k], block), :] = value
        local_p = lax.dot_general(q_half, value, CONTRACT_LAST, preferred_element_type=jnp.float32)
        store_tiles(outgoing.at[k], local_p.astype(jnp.bfloat16))


def first(grads, error, q_start, replicas, flip):
    rows, hidden = grads.shape
    rank = q_start.shape[0]
    block = rows // replicas
    half = replicas // 2
    return pl.pallas_call(
        functools.partial(first_kernel, replicas, flip),
        in_specs=[pl.BlockSpec(memory_space=pl.ANY)] * 3,
        out_specs=[pl.BlockSpec(memory_space=pltpu.VMEM)] * 2,
        out_shape=[
            pltpu.VMEM((half * block, hidden), jnp.bfloat16),
            pltpu.VMEM((half, block // LANES * rank, LANES), jnp.bfloat16),
        ],
        scratch_shapes=[
            pltpu.VMEM((2, half, block, hidden), jnp.bfloat16),
            pltpu.VMEM(q_start.shape, jnp.float32),
            pltpu.SemaphoreType.DMA((2, half)),
            pltpu.SemaphoreType.DMA(()),
        ],
        compiler_params=pltpu.CompilerParams(vmem_limit_bytes=53 * MIB),
        cost_estimate=pl.CostEstimate(
            flops=rows * hidden * rank, bytes_accessed=2 * rows * hidden, transcendentals=0
        ),
        name="compensate_and_left",
    )(grads, error, q_start)


def partner(value, by, size):
    return lax.ppermute(value, "dp", [(i, i ^ by) for i in range(size)])


def first_share(grads, error, q_start, replicas):
    other, theirs = first(grads, error, q_start, replicas, 1)
    arrived = partner(theirs, 1, replicas)
    own, mine = first(grads, error, q_start, replicas, 0)
    pairs = [
        arrived[k].astype(jnp.float32) + mine[k].astype(jnp.float32) for k in range(replicas // 2)
    ]
    total = pairs[0]
    for value in [
        partner(pairs[k].astype(jnp.bfloat16), 2 * k, replicas) for k in range(1, replicas // 2)
    ]:
        total = total + value.astype(jnp.float32)
    return (own, other), total


def gather_half(share, replicas):
    return jnp.stack([share] + [partner(share, 2 * k, replicas) for k in range(1, replicas // 2)])


def inverse_lower(gram):
    rank = gram.shape[0]
    row = lax.broadcasted_iota(jnp.int32, (SUBLANES, 2 * rank), 0)
    across = lax.broadcasted_iota(jnp.int32, (SUBLANES, 2 * rank), 1)
    both = jnp.concatenate([jnp.zeros((rank, rank), jnp.float32), gram], axis=1)
    starts = range(0, rank, SUBLANES)
    tiles = [
        jnp.where(across == row + at, 1.0, both[at : at + SUBLANES, :]) for at in starts
    ]
    inverse = []
    for top, base in enumerate(starts):
        columns = [
            [
                jnp.broadcast_to(tile[:, rank + k : rank + k + 1], tile.shape)
                for tile in tiles[top:]
            ]
            for k in range(base, base + SUBLANES)
        ]
        for j in range(SUBLANES):
            head = columns[j][0]
            reciprocal = 1.0 / head[j : j + 1, :]
            pivot_row = tiles[top][j : j + 1, :]
            for at in range(len(columns[j])):
                factor = columns[j][at] * reciprocal
                if at == 0:
                    factor = jnp.where(row > j, factor, 0.0)
                for i in range(j + 1, SUBLANES):
                    columns[i][at] = columns[i][at] - factor * head[i : i + 1, :]
                tiles[top + at] = tiles[top + at] - factor * pivot_row
        done = tiles[top]
        pivots = jnp.sum(
            jnp.where(across == row + (rank + base), done, 0.0), axis=1, keepdims=True
        )
        inverse.append(done[:, :rank] * lax.rsqrt(pivots))
    return jnp.concatenate(inverse, axis=0)


def columns_of(blocks, tiles, first_tile, count):
    rank = blocks.shape[1] // tiles
    me = lax.axis_index("dp") >> 1
    parts = []
    for at in range(first_tile, first_tile + count):
        block, tile = divmod(at, tiles)
        parts.append(blocks[me ^ block, tile * rank : (tile + 1) * rank, :])
    return jnp.concatenate(parts, axis=1)


def products(tiles, blocks, half):
    factor = columns_of(blocks, tiles, 0, blocks.shape[0] * tiles)
    gram = lax.dot_general(factor, factor, CONTRACT_LAST, preferred_element_type=jnp.float32)
    return gram, jnp.dot(factor, half[...], preferred_element_type=jnp.float32)


def products_kernel(tiles, blocks, half, gram, product):
    gram[...], product[...] = products(tiles, blocks, half)


def own_products(blocks, half, rank):
    rows, hidden = half.shape
    in_vmem = pl.BlockSpec(memory_space=pltpu.VMEM)
    return pl.pallas_call(
        functools.partial(products_kernel, blocks.shape[1] // rank),
        in_specs=[in_vmem] * 2,
        out_specs=[in_vmem] * 2,
        out_shape=[
            pltpu.VMEM((rank, rank), jnp.float32),
            pltpu.VMEM((rank, hidden), jnp.float32),
        ],
        compiler_params=pltpu.CompilerParams(vmem_limit_bytes=24 * MIB),
        cost_estimate=pl.CostEstimate(
            flops=2 * rows * hidden * rank, bytes_accessed=2 * rows * hidden, transcendentals=0
        ),
        name="gram_and_right",
    )(blocks, half)


def right_kernel(tiles, blocks, half, own_gram, own_product, term, inverse_out=None):
    gram, product = products(tiles, blocks, half)
    inverse = inverse_lower(own_gram[...] + gram)
    if inverse_out is not None:
        inverse_out[...] = inverse
    term[...] = jnp.dot(
        inverse,
        own_product[...] + product,
        precision=lax.Precision.HIGHEST,
        preferred_element_type=jnp.float32,
    ).astype(jnp.bfloat16)


def right(blocks, half, own_gram, own_product, keep):
    rank, hidden = own_product.shape
    out_shape = [pltpu.VMEM((rank, hidden), jnp.bfloat16)]
    if keep:
        out_shape.append(pltpu.VMEM((rank, rank), jnp.float32))
    in_vmem = pl.BlockSpec(memory_space=pltpu.VMEM)
    return pl.pallas_call(
        functools.partial(right_kernel, blocks.shape[1] // rank),
        in_specs=[in_vmem] * 4,
        out_specs=[in_vmem] * len(out_shape),
        out_shape=out_shape,
        compiler_params=pltpu.CompilerParams(vmem_limit_bytes=24 * MIB),
        name="orthogonalize_and_right",
    )(blocks, half, own_gram, own_product)


def addends(term, size):
    step = 1
    while 4 * step < size:
        term = (term.astype(jnp.float32) + partner(term, step, size).astype(jnp.float32)).astype(
            jnp.bfloat16
        )
        step *= 2
    return [term] + [partner(term, by, size) for by in (step, 2 * step, 3 * step)]


def sum_of(parts):
    one, two, three, four = [part[...].astype(jnp.float32) for part in parts]
    return (one + two) + (three + four)


def left_kernel(parts, halves, bucket, outgoing, landed, sem):
    replicas = outgoing.shape[0]
    block = 2 * halves[0].shape[0] // replicas
    x = lax.axis_index("dp") & 1
    fetch = pltpu.make_async_copy(bucket, landed, sem)
    fetch.start()
    factor_q = sum_of(parts) / replicas
    norm = jnp.sqrt(jnp.sum(factor_q * factor_q, axis=1, keepdims=True) + 1e-06)
    q_half = factor_q.astype(jnp.bfloat16)
    for flip, half in enumerate(halves):
        for j in range(replicas // 2):
            local_p = lax.dot_general(
                q_half,
                half[j * block : (j + 1) * block, :],
                CONTRACT_LAST,
                preferred_element_type=jnp.float32,
            )
            store_tiles(outgoing.at[2 * j + (x ^ flip)], (local_p / norm).astype(jnp.bfloat16))
    fetch.wait()
    outgoing[:, -bucket.shape[1] :, :] = landed[...].astype(jnp.bfloat16)


def left(parts, halves, bucket):
    replicas = bucket.shape[0]
    tall = 2 * halves[0].shape[0] // replicas * parts[0].shape[0] // LANES + bucket.shape[1]
    in_vmem = pl.BlockSpec(memory_space=pltpu.VMEM)
    return pl.pallas_call(
        left_kernel,
        in_specs=[[in_vmem] * len(parts), (in_vmem, in_vmem), pl.BlockSpec(memory_space=pl.ANY)],
        out_specs=in_vmem,
        out_shape=pltpu.VMEM((replicas, tall, LANES), jnp.bfloat16),
        scratch_shapes=[pltpu.VMEM(bucket.shape, jnp.float32), pltpu.SemaphoreType.DMA(())],
        compiler_params=pltpu.CompilerParams(vmem_limit_bytes=24 * MIB),
        name="normalize_and_left",
    )(parts, halves, bucket)


def last_kernel(
    replicas, parts, inverse, blocks, halves, share,
    update, new_error, bucket_mean, update_held, error_held, sems, bucket_sem,
):
    tall = bucket_mean.shape[0]
    there = pl.ds(share.shape[0] - tall, tall)
    copies = [pltpu.make_async_copy(share.at[there], bucket_mean, bucket_sem)]
    copies[0].start()
    rows, hidden = halves[0].shape
    tiles = 2 * rows // replicas // LANES
    x = lax.axis_index("dp") & 1
    right = lax.dot_general(
        inverse[...],
        sum_of(parts) / replicas,
        CONTRACT_FIRST,
        precision=lax.Precision.HIGHEST,
        preferred_element_type=jnp.float32,
    )
    right = jnp.concatenate(three_parts(right), axis=0)
    for flip, half in enumerate(halves):
        for i, (at, size) in enumerate(pieces(rows, flip == 0)):
            where = slice(at, at + size)
            p_block = columns_of(blocks[flip], tiles, at // LANES, size // LANES).T
            block = jnp.dot(
                jnp.concatenate([p_block] * 3, axis=1), right, preferred_element_type=jnp.float32
            )
            update_held[flip, where, :] = block
            error_held[flip, where, :] = (half[where, :].astype(jnp.float32) - block).astype(
                jnp.bfloat16
            )
            there = pl.ds(pl.multiple_of((x ^ flip) * rows + at, LANES), size)
            for j, (held, out) in enumerate(((update_held, update), (error_held, new_error))):
                copies.append(
                    pltpu.make_async_copy(
                        held.at[flip, pl.ds(at, size)], out.at[there], sems.at[j, flip, i]
                    )
                )
                copies[-1].start(priority=j)
    for copy in copies:
        copy.wait()


def last(parts, inverse, blocks, halves, share, replicas, bucket_tall):
    rows, hidden = halves[0].shape
    in_vmem = pl.BlockSpec(memory_space=pltpu.VMEM)
    return pl.pallas_call(
        functools.partial(last_kernel, replicas),
        in_specs=[[in_vmem] * len(parts), in_vmem, (in_vmem, in_vmem), (in_vmem, in_vmem), in_vmem],
        out_specs=[pl.BlockSpec(memory_space=pl.ANY)] * 3,
        out_shape=[
            jax.ShapeDtypeStruct((2 * rows, hidden), jnp.float32),
            jax.ShapeDtypeStruct((2 * rows, hidden), jnp.bfloat16),
            jax.ShapeDtypeStruct((bucket_tall, LANES), jnp.float32),
        ],
        scratch_shapes=[
            pltpu.VMEM((2, rows, hidden), jnp.float32),
            pltpu.VMEM((2, rows, hidden), jnp.bfloat16),
            pltpu.SemaphoreType.DMA((2, 2, len(pieces(rows, True)))),
            pltpu.SemaphoreType.DMA(()),
        ],
        compiler_params=pltpu.CompilerParams(vmem_limit_bytes=40 * MIB),
        name="update_and_error",
    )(parts, inverse, blocks, halves, share)


def on_device(grads, error, q_start, bucket):
    replicas = lax.axis_size("dp")
    rows = grads.shape[1]
    rank = q_start.shape[1]
    bucket = bucket.reshape(replicas, -1, LANES)
    tall = rows // replicas * rank // LANES
    halves, share = first_share(grads[0], error[0], q_start.T, replicas)
    for step in range(ITERS):
        if step > 0:
            share = jnp.sum(exchange(outgoing).astype(jnp.float32), axis=0)
        share = share / replicas
        own_blocks = gather_half(share[:tall].astype(jnp.bfloat16), replicas)
        other_blocks = partner(own_blocks, 1, replicas)
        term, *inverse = right(
            other_blocks, halves[1], *own_products(own_blocks, halves[0], rank), step + 1 == ITERS
        )
        parts = addends(term, replicas)
        if step + 1 < ITERS:
            outgoing = left(parts, halves, bucket)
    update, new_error, bucket_mean = last(
        parts, inverse[0], (own_blocks, other_blocks), halves, share, replicas, bucket.shape[1]
    )
    return (update, new_error[None], bucket_mean.reshape(-1))


def solution(mesh):
    return jax.shard_map(
        on_device,
        mesh=mesh,
        in_specs=(
            P("dp", None, "expert"),
            P("dp", None, "expert"),
            P("expert", None),
            P("dp", "expert"),
        ),
        out_specs=(P(None, "expert"), P("dp", None, "expert"), P(("expert", "dp"))),
        check_vma=False,
    )
```

```python
import functools

import jax
import jax.numpy as jnp
from jax import lax
from jax.experimental import pallas as pl
from jax.experimental.pallas import tpu as pltpu
from jax.sharding import PartitionSpec as P

ITERS = 2
LANES = 128
SUBLANES = 8
MIB = 1024 * 1024
CONTRACT_FIRST = (((0,), (0,)), ((), ()))
CONTRACT_LAST = (((1,), (1,)), ((), ()))


def exchange(chunks):
    return lax.all_to_all(chunks, "dp", split_axis=0, concat_axis=0, tiled=True)


def everywhere(share, size):
    return exchange(jnp.broadcast_to(share, (size,) + share.shape))


def three_parts(value):
    high = value.astype(jnp.bfloat16)
    rest = value - high.astype(jnp.float32)
    middle = rest.astype(jnp.bfloat16)
    low = (rest - middle.astype(jnp.float32)).astype(jnp.bfloat16)
    return high, middle, low


def pieces(rows, grow):
    sizes = [LANES] + [LANES << i for i in range((rows // LANES).bit_length() - 1)]
    sizes = sizes if grow else [rows]
    return [(sum(sizes[:i]), size) for i, size in enumerate(sizes)]


def groups(replicas):
    half = replicas // 2
    return [(0, range(1)), (0, range(1, half)), (1, range(half))]


def place(flip, k):
    me = lax.axis_index("dp")
    return (me & 1) ^ flip, (me >> 1) ^ k


def first_row(replicas, flip, k, block):
    x, j = place(flip, k)
    return pl.multiple_of((x * (replicas // 2) + j) * block, block)


def store_tiles(chunk, value):
    rank, columns = value.shape
    for tile in range(columns // LANES):
        chunk[tile * rank : (tile + 1) * rank, :] = value[:, tile * LANES : (tile + 1) * LANES]


def first_kernel(replicas, flip, ks, grads, error, q_start, compensated, outgoing, *scratch):
    landed, q_landed, sems, q_sem = scratch
    fetch_q = pltpu.make_async_copy(q_start, q_landed, q_sem)
    fetch_q.start()
    block = grads.shape[0] // replicas
    copies = []
    for i, k in enumerate(ks):
        there = pl.ds(first_row(replicas, flip, k, block), block)
        for j, array in enumerate((grads, error)):
            copies.append(
                pltpu.make_async_copy(array.at[there], landed.at[j, i], sems.at[j, i])
            )
            copies[-1].start(priority=j)
    fetch_q.wait()
    q_half = q_landed[...].astype(jnp.bfloat16)
    for i in range(len(ks)):
        copies[2 * i].wait()
        copies[2 * i + 1].wait()
        value = (landed[0, i].astype(jnp.float32) + landed[1, i].astype(jnp.float32)).astype(
            jnp.bfloat16
        )
        compensated[i * block : (i + 1) * block, :] = value
        local_p = lax.dot_general(q_half, value, CONTRACT_LAST, preferred_element_type=jnp.float32)
        store_tiles(outgoing.at[i], local_p.astype(jnp.bfloat16))


def first(grads, error, q_start, replicas, flip, ks):
    rows, hidden = grads.shape
    rank = q_start.shape[0]
    block = rows // replicas
    return pl.pallas_call(
        functools.partial(first_kernel, replicas, flip, ks),
        in_specs=[pl.BlockSpec(memory_space=pl.ANY)] * 3,
        out_specs=[pl.BlockSpec(memory_space=pltpu.VMEM)] * 2,
        out_shape=[
            pltpu.VMEM((len(ks) * block, hidden), jnp.bfloat16),
            pltpu.VMEM((len(ks), block // LANES * rank, LANES), jnp.bfloat16),
        ],
        scratch_shapes=[
            pltpu.VMEM((2, len(ks), block, hidden), jnp.bfloat16),
            pltpu.VMEM(q_start.shape, jnp.float32),
            pltpu.SemaphoreType.DMA((2, len(ks))),
            pltpu.SemaphoreType.DMA(()),
        ],
        compiler_params=pltpu.CompilerParams(vmem_limit_bytes=53 * MIB),
        cost_estimate=pl.CostEstimate(
            flops=2 * len(ks) * block * hidden * rank,
            bytes_accessed=4 * len(ks) * block * hidden,
            transcendentals=0,
        ),
        name="compensate_and_left",
    )(grads, error, q_start)


def partner(value, by, size):
    return lax.ppermute(value, "dp", [(i, i ^ by) for i in range(size)])


def first_share(grads, error, q_start, replicas):
    half = replicas // 2
    other, theirs = first(grads, error, q_start, replicas, 1, range(half))
    arrived = partner(theirs, 1, replicas)
    mates, travelling = first(grads, error, q_start, replicas, 0, range(1, half))
    pairs = [
        (arrived[k].astype(jnp.float32) + travelling[k - 1].astype(jnp.float32)).astype(jnp.bfloat16)
        for k in range(1, half)
    ]
    pairs = [partner(pair, 2 * k, replicas) for k, pair in enumerate(pairs, 1)]
    own, mine = first(grads, error, q_start, replicas, 0, range(1))
    total = arrived[0].astype(jnp.float32) + mine[0].astype(jnp.float32)
    for pair in pairs:
        total = total + pair.astype(jnp.float32)
    return (own, mates, other), total


def inverse_lower(gram):
    rank = gram.shape[0]
    row = lax.broadcasted_iota(jnp.int32, (SUBLANES, 2 * rank), 0)
    across = lax.broadcasted_iota(jnp.int32, (SUBLANES, 2 * rank), 1)
    both = jnp.concatenate([jnp.zeros((rank, rank), jnp.float32), gram], axis=1)
    starts = range(0, rank, SUBLANES)
    tiles = [
        jnp.where(across == row + at, 1.0, both[at : at + SUBLANES, :]) for at in starts
    ]
    inverse = []
    for top, base in enumerate(starts):
        columns = [
            [
                jnp.broadcast_to(tile[:, rank + k : rank + k + 1], tile.shape)
                for tile in tiles[top:]
            ]
            for k in range(base, base + SUBLANES)
        ]
        for j in range(SUBLANES):
            head = columns[j][0]
            reciprocal = 1.0 / head[j : j + 1, :]
            pivot_row = tiles[top][j : j + 1, :]
            for at in range(len(columns[j])):
                factor = columns[j][at] * reciprocal
                if at == 0:
                    factor = jnp.where(row > j, factor, 0.0)
                for i in range(j + 1, SUBLANES):
                    columns[i][at] = columns[i][at] - factor * head[i : i + 1, :]
                tiles[top + at] = tiles[top + at] - factor * pivot_row
        done = tiles[top]
        pivots = jnp.sum(
            jnp.where(across == row + (rank + base), done, 0.0), axis=1, keepdims=True
        )
        inverse.append(done[:, :rank] * lax.rsqrt(pivots))
    return jnp.concatenate(inverse, axis=0)


def columns_of(arrived, tiles, flip, k):
    rank = arrived.shape[1] // tiles
    x, j = place(flip, k)
    return jnp.concatenate(
        [arrived[2 * j + x, t * rank : (t + 1) * rank, :] for t in range(tiles)], axis=1
    )


def right_kernel(tiles, arrived, parts, term, inverse_out=None):
    factors = [
        jnp.concatenate([columns_of(arrived, tiles, flip, k) for k in ks], axis=1)
        for flip, ks in groups(arrived.shape[0])
    ]
    factor_p = jnp.concatenate(factors, axis=1)
    gram = lax.dot_general(
        factor_p, factor_p, CONTRACT_LAST, preferred_element_type=jnp.float32
    )
    product = sum(
        jnp.dot(factor, part[...], preferred_element_type=jnp.float32)
        for factor, part in zip(factors, parts)
    )
    inverse = inverse_lower(gram)
    if inverse_out is not None:
        inverse_out[...] = inverse
    term[...] = jnp.dot(
        inverse, product, precision=lax.Precision.HIGHEST, preferred_element_type=jnp.float32
    ).astype(jnp.bfloat16)


def right(arrived, compensated, rank, keep):
    out_shape = [pltpu.VMEM((rank, compensated[0].shape[1]), jnp.bfloat16)]
    in_vmem = pl.BlockSpec(memory_space=pltpu.VMEM)
    if keep:
        out_shape.append(pltpu.VMEM((rank, rank), jnp.float32))
    return pl.pallas_call(
        functools.partial(right_kernel, arrived.shape[1] // rank),
        in_specs=[in_vmem, (in_vmem,) * len(compensated)],
        out_specs=[in_vmem] * len(out_shape),
        out_shape=out_shape,
        compiler_params=pltpu.CompilerParams(vmem_limit_bytes=24 * MIB),
        name="orthogonalize_and_right",
    )(arrived, compensated)


def addends(term, size):
    step = 1
    while 4 * step < size:
        term = (term.astype(jnp.float32) + partner(term, step, size).astype(jnp.float32)).astype(
            jnp.bfloat16
        )
        step *= 2
    return [term] + [partner(term, by, size) for by in (step, 2 * step, 3 * step)]


def sum_of(parts):
    one, two, three, four = [part[...].astype(jnp.float32) for part in parts]
    return (one + two) + (three + four)


def left_kernel(parts, compensated, bucket, outgoing, landed, sem):
    replicas = outgoing.shape[0]
    block = compensated[0].shape[0]
    fetch = pltpu.make_async_copy(bucket, landed, sem)
    fetch.start()
    factor_q = sum_of(parts) / replicas
    scale = 1.0 / jnp.sqrt(jnp.sum(factor_q * factor_q, axis=1, keepdims=True) + 1e-06)
    q_half = factor_q.astype(jnp.bfloat16)
    for (flip, ks), part in zip(groups(replicas), compensated):
        for i, k in enumerate(ks):
            local_p = lax.dot_general(
                q_half,
                part[i * block : (i + 1) * block, :],
                CONTRACT_LAST,
                preferred_element_type=jnp.float32,
            )
            x, j = place(flip, k)
            store_tiles(outgoing.at[2 * j + x], (local_p * scale).astype(jnp.bfloat16))
    fetch.wait()
    outgoing[:, -bucket.shape[1] :, :] = landed[...].astype(jnp.bfloat16)


def left(parts, compensated, bucket):
    replicas = bucket.shape[0]
    tall = compensated[0].shape[0] * parts[0].shape[0] // LANES + bucket.shape[1]
    in_vmem = pl.BlockSpec(memory_space=pltpu.VMEM)
    return pl.pallas_call(
        left_kernel,
        in_specs=[
            [in_vmem] * len(parts),
            (in_vmem,) * len(compensated),
            pl.BlockSpec(memory_space=pl.ANY),
        ],
        out_specs=in_vmem,
        out_shape=pltpu.VMEM((replicas, tall, LANES), jnp.bfloat16),
        scratch_shapes=[pltpu.VMEM(bucket.shape, jnp.float32), pltpu.SemaphoreType.DMA(())],
        compiler_params=pltpu.CompilerParams(vmem_limit_bytes=24 * MIB),
        name="normalize_and_left",
    )(parts, compensated, bucket)


def last_kernel(
    replicas, parts, inverse, arrived, compensated, share,
    update, new_error, bucket_mean, update_held, error_held, sems, bucket_sem,
):
    tall = bucket_mean.shape[0]
    there = pl.ds(share.shape[0] - tall, tall)
    copies = [pltpu.make_async_copy(share.at[there], bucket_mean, bucket_sem)]
    copies[0].start()
    rows = compensated[0].shape[0]
    right = lax.dot_general(
        inverse[...],
        sum_of(parts) / replicas,
        CONTRACT_FIRST,
        precision=lax.Precision.HIGHEST,
        preferred_element_type=jnp.float32,
    )
    right = jnp.concatenate(three_parts(right), axis=0)
    done = 0
    for (flip, ks), part in zip(groups(replicas), compensated):
        for i, k in enumerate(ks):
            p_block = columns_of(arrived, rows // LANES, flip, k)
            start = first_row(replicas, flip, k, rows)
            for at, size in pieces(rows, done == 0):
                p_piece = p_block[:, at : at + size].T
                value = jnp.dot(
                    jnp.concatenate([p_piece] * 3, axis=1),
                    right,
                    preferred_element_type=jnp.float32,
                )
                held = pl.ds(done, size)
                update_held[held, :] = value
                error_held[held, :] = (
                    part[i * rows + at : i * rows + at + size, :].astype(jnp.float32) - value
                ).astype(jnp.bfloat16)
                there = pl.ds(pl.multiple_of(start + at, LANES), size)
                for j, (source, out) in enumerate(((update_held, update), (error_held, new_error))):
                    copies.append(
                        pltpu.make_async_copy(
                            source.at[held], out.at[there], sems.at[j, done // LANES]
                        )
                    )
                    copies[-1].start(priority=j)
                done += size
    for copy in copies:
        copy.wait()


def last(parts, inverse, arrived, compensated, share, replicas, bucket_tall):
    rows, hidden = compensated[0].shape
    rows *= replicas
    in_vmem = pl.BlockSpec(memory_space=pltpu.VMEM)
    return pl.pallas_call(
        functools.partial(last_kernel, replicas),
        in_specs=[
            [in_vmem] * len(parts), in_vmem, in_vmem, (in_vmem,) * len(compensated), in_vmem
        ],
        out_specs=[pl.BlockSpec(memory_space=pl.ANY)] * 3,
        out_shape=[
            jax.ShapeDtypeStruct((rows, hidden), jnp.float32),
            jax.ShapeDtypeStruct((rows, hidden), jnp.bfloat16),
            jax.ShapeDtypeStruct((bucket_tall, LANES), jnp.float32),
        ],
        scratch_shapes=[
            pltpu.VMEM((rows, hidden), jnp.float32),
            pltpu.VMEM((rows, hidden), jnp.bfloat16),
            pltpu.SemaphoreType.DMA((2, rows // LANES)),
            pltpu.SemaphoreType.DMA(()),
        ],
        compiler_params=pltpu.CompilerParams(vmem_limit_bytes=40 * MIB),
        name="update_and_error",
    )(parts, inverse, arrived, compensated, share)


def on_device(grads, error, q_start, bucket):
    replicas = lax.axis_size("dp")
    rows = grads.shape[1]
    rank = q_start.shape[1]
    bucket = bucket.reshape(replicas, -1, LANES)
    tall = rows // replicas * rank // LANES
    compensated, share = first_share(grads[0], error[0], q_start.T, replicas)
    for step in range(ITERS):
        if step > 0:
            share = jnp.sum(exchange(outgoing).astype(jnp.float32), axis=0)
        share = share / replicas
        factor_p = everywhere(share[:tall].astype(jnp.bfloat16), replicas)
        term, *inverse = right(factor_p, compensated, rank, step + 1 == ITERS)
        parts = addends(term, replicas)
        if step + 1 < ITERS:
            outgoing = left(parts, compensated, bucket)
    update, new_error, bucket_mean = last(
        parts, inverse[0], factor_p, compensated, share, replicas, bucket.shape[1]
    )
    return (update, new_error[None], bucket_mean.reshape(-1))


def solution(mesh):
    return jax.shard_map(
        on_device,
        mesh=mesh,
        in_specs=(
            P("dp", None, "expert"),
            P("dp", None, "expert"),
            P("expert", None),
            P("dp", "expert"),
        ),
        out_specs=(P(None, "expert"), P("dp", None, "expert"), P(("expert", "dp"))),
        check_vma=False,
    )
```

```python
import functools

import jax
import jax.numpy as jnp
from jax import lax
from jax.experimental import pallas as pl
from jax.experimental.pallas import tpu as pltpu
from jax.sharding import PartitionSpec as P

ITERS = 2
LANES = 128
SUBLANES = 8
MIB = 1024 * 1024
CONTRACT_FIRST = (((0,), (0,)), ((), ()))
CONTRACT_LAST = (((1,), (1,)), ((), ()))


def exchange(chunks):
    return lax.all_to_all(chunks, "dp", split_axis=0, concat_axis=0, tiled=True)


def everywhere(share, size):
    return exchange(jnp.broadcast_to(share, (size,) + share.shape))


def three_parts(value):
    high = value.astype(jnp.bfloat16)
    rest = value - high.astype(jnp.float32)
    middle = rest.astype(jnp.bfloat16)
    low = (rest - middle.astype(jnp.float32)).astype(jnp.bfloat16)
    return high, middle, low


def pieces(rows, grow):
    sizes = [4 * LANES] * (rows // (4 * LANES))
    if grow:
        sizes[:1] = [LANES, LANES, 2 * LANES]
    return [(sum(sizes[:i]), size) for i, size in enumerate(sizes)]


def store_tiles(chunk, value):
    rank, columns = value.shape
    for tile in range(columns // LANES):
        chunk[tile * rank : (tile + 1) * rank, :] = value[:, tile * LANES : (tile + 1) * LANES]


def first_kernel(replicas, flip, grads, error, q_start, compensated, outgoing, *scratch):
    landed, q_landed, sems, q_sem = scratch
    fetch_q = pltpu.make_async_copy(q_start, q_landed, q_sem)
    fetch_q.start()
    me = lax.axis_index("dp")
    half = replicas // 2
    block = grads.shape[0] // replicas
    starts, copies = [], []
    for k in range(half):
        starts.append(pl.multiple_of(((me >> 1) ^ k) * block, block))
        there = pl.multiple_of(((me & 1) ^ flip) * (half * block) + starts[k], block)
        for j, array in enumerate((grads, error)):
            copies.append(
                pltpu.make_async_copy(
                    array.at[pl.ds(there, block)], landed.at[j, k], sems.at[j, k]
                )
            )
            copies[-1].start(priority=j)
    fetch_q.wait()
    q_half = q_landed[...].astype(jnp.bfloat16)
    for k in range(half):
        copies[2 * k].wait()
        copies[2 * k + 1].wait()
        value = (landed[0, k].astype(jnp.float32) + landed[1, k].astype(jnp.float32)).astype(
            jnp.bfloat16
        )
        compensated[pl.ds(starts[k], block), :] = value
        local_p = lax.dot_general(q_half, value, CONTRACT_LAST, preferred_element_type=jnp.float32)
        store_tiles(outgoing.at[k], local_p.astype(jnp.bfloat16))


def first(grads, error, q_start, replicas, flip):
    rows, hidden = grads.shape
    rank = q_start.shape[0]
    block = rows // replicas
    half = replicas // 2
    return pl.pallas_call(
        functools.partial(first_kernel, replicas, flip),
        in_specs=[pl.BlockSpec(memory_space=pl.ANY)] * 3,
        out_specs=[pl.BlockSpec(memory_space=pltpu.VMEM)] * 2,
        out_shape=[
            pltpu.VMEM((half * block, hidden), jnp.bfloat16),
            pltpu.VMEM((half, block // LANES * rank, LANES), jnp.bfloat16),
        ],
        scratch_shapes=[
            pltpu.VMEM((2, half, block, hidden), jnp.bfloat16),
            pltpu.VMEM(q_start.shape, jnp.float32),
            pltpu.SemaphoreType.DMA((2, half)),
            pltpu.SemaphoreType.DMA(()),
        ],
        compiler_params=pltpu.CompilerParams(vmem_limit_bytes=53 * MIB),
        cost_estimate=pl.CostEstimate(
            flops=rows * hidden * rank, bytes_accessed=2 * rows * hidden, transcendentals=0
        ),
        name="compensate_and_left",
    )(grads, error, q_start)


def partner(value, by, size):
    return lax.ppermute(value, "dp", [(i, i ^ by) for i in range(size)])


def first_share(grads, error, q_start, replicas):
    other, theirs = first(grads, error, q_start, replicas, 1)
    arrived = partner(theirs, 1, replicas)
    own, mine = first(grads, error, q_start, replicas, 0)
    pairs = [
        arrived[k].astype(jnp.float32) + mine[k].astype(jnp.float32) for k in range(replicas // 2)
    ]
    total = pairs[0]
    for value in [
        partner(pairs[k].astype(jnp.bfloat16), 2 * k, replicas) for k in range(1, replicas // 2)
    ]:
        total = total + value.astype(jnp.float32)
    return (own, other), total


def inverse_lower(gram):
    rank = gram.shape[0]
    on_diagonal = lax.broadcasted_iota(jnp.int32, gram.shape, 0) == lax.broadcasted_iota(
        jnp.int32, gram.shape, 1
    )
    diagonal = jnp.where(on_diagonal, gram, 0.0)
    scale = lax.rsqrt(jnp.sum(diagonal, axis=0, keepdims=True))
    gram = gram * lax.rsqrt(jnp.sum(diagonal, axis=1, keepdims=True)) * scale
    row = lax.broadcasted_iota(jnp.int32, (SUBLANES, 2 * rank), 0)
    across = lax.broadcasted_iota(jnp.int32, (SUBLANES, 2 * rank), 1)
    both = jnp.concatenate([jnp.zeros((rank, rank), jnp.float32), gram], axis=1)
    starts = range(0, rank, SUBLANES)
    tiles = [
        jnp.where(across == row + at, 1.0, both[at : at + SUBLANES, :]) for at in starts
    ]
    inverse = []
    for top, base in enumerate(starts):
        columns = [
            [
                jnp.broadcast_to(tile[:, rank + k : rank + k + 1], tile.shape)
                for tile in tiles[top:]
            ]
            for k in range(base, base + SUBLANES)
        ]
        for j in range(0, SUBLANES, 2):
            first_head, second_head = columns[j][0], columns[j + 1][0]
            a, b = first_head[j : j + 1, :], first_head[j + 1 : j + 2, :]
            c = second_head[j + 1 : j + 2, :]
            first_reciprocal = 1.0 / a
            second_reciprocal = 1.0 / (a * c - b * b)
            ratio = b * first_reciprocal
            first_row = tiles[top][j : j + 1, :]
            second_row = tiles[top][j + 1 : j + 2, :] - ratio * first_row
            for at in range(len(columns[j])):
                first_factor = columns[j][at] * first_reciprocal
                second_factor = (columns[j + 1][at] * a - columns[j][at] * b) * second_reciprocal
                if at == 0:
                    first_factor = jnp.where(row > j, first_factor, 0.0)
                    second_factor = jnp.where(row > j + 1, second_factor, 0.0)
                for i in range(j + 2, SUBLANES):
                    first_at = first_head[i : i + 1, :]
                    second_at = second_head[i : i + 1, :] - ratio * first_at
                    columns[i][at] = (
                        columns[i][at] - first_factor * first_at - second_factor * second_at
                    )
                tiles[top + at] = (
                    tiles[top + at] - first_factor * first_row - second_factor * second_row
                )
        done = tiles[top]
        pivots = jnp.sum(
            jnp.where(across == row + (rank + base), done, 0.0), axis=1, keepdims=True
        )
        inverse.append(done[:, :rank] * lax.rsqrt(pivots))
    return jnp.concatenate(inverse, axis=0) * scale


def columns_of(arrived, tiles, x, first_tile, count):
    rank = arrived.shape[1] // tiles
    parts = []
    for at in range(first_tile, first_tile + count):
        block, tile = divmod(at, tiles)
        parts.append(arrived[2 * block + x, tile * rank : (tile + 1) * rank, :])
    return jnp.concatenate(parts, axis=1)


def right_kernel(tiles, arrived, halves, term, inverse_out=None):
    x = lax.axis_index("dp") & 1
    count = arrived.shape[0] // 2 * tiles
    factors = [columns_of(arrived, tiles, x ^ flip, 0, count) for flip in range(2)]
    factor_p = jnp.concatenate(factors, axis=1)
    gram = lax.dot_general(
        factor_p, factor_p, CONTRACT_LAST, preferred_element_type=jnp.float32
    )
    product = sum(
        jnp.dot(factor, half[...], preferred_element_type=jnp.float32)
        for factor, half in zip(factors, halves)
    )
    inverse = inverse_lower(gram)
    if inverse_out is not None:
        inverse_out[...] = inverse
    term[...] = jnp.dot(
        inverse, product, precision=lax.Precision.HIGHEST, preferred_element_type=jnp.float32
    ).astype(jnp.bfloat16)


def right(arrived, halves, rank, keep):
    out_shape = [pltpu.VMEM((rank, halves[0].shape[1]), jnp.bfloat16)]
    in_vmem = pl.BlockSpec(memory_space=pltpu.VMEM)
    if keep:
        out_shape.append(pltpu.VMEM((rank, rank), jnp.float32))
    return pl.pallas_call(
        functools.partial(right_kernel, arrived.shape[1] // rank),
        in_specs=[in_vmem, (in_vmem, in_vmem)],
        out_specs=[in_vmem] * len(out_shape),
        out_shape=out_shape,
        compiler_params=pltpu.CompilerParams(vmem_limit_bytes=24 * MIB),
        name="orthogonalize_and_right",
    )(arrived, halves)


def addends(term, size):
    one, two, three, four = [
        part.astype(jnp.float32) for part in [term] + [partner(term, by, size) for by in (1, 2, 3)]
    ]
    term = ((one + two) + (three + four)).astype(jnp.bfloat16)
    step = 4
    while 2 * step < size:
        term = (term.astype(jnp.float32) + partner(term, step, size).astype(jnp.float32)).astype(
            jnp.bfloat16
        )
        step *= 2
    return [term, partner(term, step, size)]


def sum_of(parts):
    one, two = [part[...].astype(jnp.float32) for part in parts]
    return one + two


def left_kernel(parts, halves, bucket, outgoing, landed, sem):
    replicas = outgoing.shape[0]
    block = 2 * halves[0].shape[0] // replicas
    x = lax.axis_index("dp") & 1
    fetch = pltpu.make_async_copy(bucket, landed, sem)
    fetch.start()
    factor_q = sum_of(parts) / replicas
    scale = 1.0 / jnp.sqrt(jnp.sum(factor_q * factor_q, axis=1, keepdims=True) + 1e-06)
    q_half = factor_q.astype(jnp.bfloat16)
    for flip, half in enumerate(halves):
        for j in range(replicas // 2):
            local_p = lax.dot_general(
                q_half,
                half[j * block : (j + 1) * block, :],
                CONTRACT_LAST,
                preferred_element_type=jnp.float32,
            )
            store_tiles(outgoing.at[2 * j + (x ^ flip)], (local_p * scale).astype(jnp.bfloat16))
    fetch.wait()
    outgoing[:, -bucket.shape[1] :, :] = landed[...].astype(jnp.bfloat16)


def left(parts, halves, bucket):
    replicas = bucket.shape[0]
    tall = 2 * halves[0].shape[0] // replicas * parts[0].shape[0] // LANES + bucket.shape[1]
    in_vmem = pl.BlockSpec(memory_space=pltpu.VMEM)
    return pl.pallas_call(
        left_kernel,
        in_specs=[[in_vmem] * len(parts), (in_vmem, in_vmem), pl.BlockSpec(memory_space=pl.ANY)],
        out_specs=in_vmem,
        out_shape=pltpu.VMEM((replicas, tall, LANES), jnp.bfloat16),
        scratch_shapes=[pltpu.VMEM(bucket.shape, jnp.float32), pltpu.SemaphoreType.DMA(())],
        compiler_params=pltpu.CompilerParams(vmem_limit_bytes=24 * MIB),
        name="normalize_and_left",
    )(parts, halves, bucket)


def last_kernel(
    replicas, parts, inverse, arrived, halves, share,
    update, new_error, bucket_mean, update_held, error_held, sems, bucket_sem,
):
    tall = bucket_mean.shape[0]
    there = pl.ds(share.shape[0] - tall, tall)
    copies = [pltpu.make_async_copy(share.at[there], bucket_mean, bucket_sem)]
    copies[0].start()
    rows, hidden = halves[0].shape
    tiles = 2 * rows // replicas // LANES
    x = lax.axis_index("dp") & 1
    right = lax.dot_general(
        inverse[...],
        sum_of(parts) / replicas,
        CONTRACT_FIRST,
        precision=lax.Precision.HIGHEST,
        preferred_element_type=jnp.float32,
    )
    right = jnp.concatenate(three_parts(right), axis=0)
    for flip, half in enumerate(halves):
        for i, (at, size) in enumerate(pieces(rows, flip == 0)):
            where = slice(at, at + size)
            p_block = columns_of(arrived, tiles, x ^ flip, at // LANES, size // LANES).T
            block = jnp.dot(
                jnp.concatenate([p_block] * 3, axis=1), right, preferred_element_type=jnp.float32
            )
            update_held[flip, where, :] = block
            error_held[flip, where, :] = (half[where, :].astype(jnp.float32) - block).astype(
                jnp.bfloat16
            )
            there = pl.ds(pl.multiple_of((x ^ flip) * rows + at, LANES), size)
            for j, (held, out) in enumerate(((update_held, update), (error_held, new_error))):
                copies.append(
                    pltpu.make_async_copy(
                        held.at[flip, pl.ds(at, size)], out.at[there], sems.at[j, flip, i]
                    )
                )
                copies[-1].start(priority=j)
    for copy in copies:
        copy.wait()


def last(parts, inverse, arrived, halves, share, replicas, bucket_tall):
    rows, hidden = halves[0].shape
    in_vmem = pl.BlockSpec(memory_space=pltpu.VMEM)
    return pl.pallas_call(
        functools.partial(last_kernel, replicas),
        in_specs=[[in_vmem] * len(parts), in_vmem, in_vmem, (in_vmem, in_vmem), in_vmem],
        out_specs=[pl.BlockSpec(memory_space=pl.ANY)] * 3,
        out_shape=[
            jax.ShapeDtypeStruct((2 * rows, hidden), jnp.float32),
            jax.ShapeDtypeStruct((2 * rows, hidden), jnp.bfloat16),
            jax.ShapeDtypeStruct((bucket_tall, LANES), jnp.float32),
        ],
        scratch_shapes=[
            pltpu.VMEM((2, rows, hidden), jnp.float32),
            pltpu.VMEM((2, rows, hidden), jnp.bfloat16),
            pltpu.SemaphoreType.DMA((2, 2, len(pieces(rows, True)))),
            pltpu.SemaphoreType.DMA(()),
        ],
        compiler_params=pltpu.CompilerParams(vmem_limit_bytes=40 * MIB),
        name="update_and_error",
    )(parts, inverse, arrived, halves, share)


def on_device(grads, error, q_start, bucket):
    replicas = lax.axis_size("dp")
    rows = grads.shape[1]
    rank = q_start.shape[1]
    bucket = bucket.reshape(replicas, -1, LANES)
    tall = rows // replicas * rank // LANES
    halves, share = first_share(grads[0], error[0], q_start.T, replicas)
    for step in range(ITERS):
        if step > 0:
            share = jnp.sum(exchange(outgoing).astype(jnp.float32), axis=0)
        share = share / replicas
        factor_p = everywhere(share[:tall].astype(jnp.bfloat16), replicas)
        term, *inverse = right(factor_p, halves, rank, step + 1 == ITERS)
        parts = addends(term, replicas)
        if step + 1 < ITERS:
            outgoing = left(parts, halves, bucket)
    update, new_error, bucket_mean = last(
        parts, inverse[0], factor_p, halves, share, replicas, bucket.shape[1]
    )
    return (update, new_error[None], bucket_mean.reshape(-1))


def solution(mesh):
    return jax.shard_map(
        on_device,
        mesh=mesh,
        in_specs=(
            P("dp", None, "expert"),
            P("dp", None, "expert"),
            P("expert", None),
            P("dp", "expert"),
        ),
        out_specs=(P(None, "expert"), P("dp", None, "expert"), P(("expert", "dp"))),
        check_vma=False,
    )
```

```python
import functools

import jax
import jax.numpy as jnp
from jax import lax
from jax.experimental import pallas as pl
from jax.experimental.pallas import tpu as pltpu
from jax.sharding import PartitionSpec as P

ITERS = 2
LANES = 128
SUBLANES = 8
MIB = 1024 * 1024
CONTRACT_FIRST = (((0,), (0,)), ((), ()))
CONTRACT_LAST = (((1,), (1,)), ((), ()))


def exchange(chunks):
    return lax.all_to_all(chunks, "dp", split_axis=0, concat_axis=0, tiled=True)


def everywhere(share, size):
    return exchange(jnp.broadcast_to(share, (size,) + share.shape))


def three_parts(value):
    high = value.astype(jnp.bfloat16)
    rest = value - high.astype(jnp.float32)
    middle = rest.astype(jnp.bfloat16)
    low = (rest - middle.astype(jnp.float32)).astype(jnp.bfloat16)
    return high, middle, low


def pieces(rows, grow):
    sizes = [4 * LANES] * (rows // (4 * LANES))
    if grow:
        sizes[:1] = [LANES, LANES, 2 * LANES]
    return [(sum(sizes[:i]), size) for i, size in enumerate(sizes)]


def store_tiles(chunk, value):
    rank, columns = value.shape
    for tile in range(columns // LANES):
        chunk[tile * rank : (tile + 1) * rank, :] = value[:, tile * LANES : (tile + 1) * LANES]


def first_kernel(replicas, flip, grads, error, q_start, compensated, outgoing, *scratch):
    landed, q_landed, sems, q_sem = scratch
    fetch_q = pltpu.make_async_copy(q_start, q_landed, q_sem)
    fetch_q.start()
    me = lax.axis_index("dp")
    half = replicas // 2
    block = grads.shape[0] // replicas
    starts, copies = [], []
    for k in range(half):
        starts.append(pl.multiple_of(((me >> 1) ^ k) * block, block))
        there = pl.multiple_of(((me & 1) ^ flip) * (half * block) + starts[k], block)
        for j, array in enumerate((grads, error)):
            copies.append(
                pltpu.make_async_copy(
                    array.at[pl.ds(there, block)], landed.at[j, k], sems.at[j, k]
                )
            )
            copies[-1].start(priority=j)
    fetch_q.wait()
    q_half = q_landed[...].astype(jnp.bfloat16)
    for k in range(half):
        copies[2 * k].wait()
        copies[2 * k + 1].wait()
        value = (landed[0, k].astype(jnp.float32) + landed[1, k].astype(jnp.float32)).astype(
            jnp.bfloat16
        )
        compensated[pl.ds(starts[k], block), :] = value
        local_p = lax.dot_general(q_half, value, CONTRACT_LAST, preferred_element_type=jnp.float32)
        store_tiles(outgoing.at[k], local_p.astype(jnp.bfloat16))


def first(grads, error, q_start, replicas, flip):
    rows, hidden = grads.shape
    rank = q_start.shape[0]
    block = rows // replicas
    half = replicas // 2
    return pl.pallas_call(
        functools.partial(first_kernel, replicas, flip),
        in_specs=[pl.BlockSpec(memory_space=pl.ANY)] * 3,
        out_specs=[pl.BlockSpec(memory_space=pltpu.VMEM)] * 2,
        out_shape=[
            pltpu.VMEM((half * block, hidden), jnp.bfloat16),
            pltpu.VMEM((half, block // LANES * rank, LANES), jnp.bfloat16),
        ],
        scratch_shapes=[
            pltpu.VMEM((2, half, block, hidden), jnp.bfloat16),
            pltpu.VMEM(q_start.shape, jnp.float32),
            pltpu.SemaphoreType.DMA((2, half)),
            pltpu.SemaphoreType.DMA(()),
        ],
        compiler_params=pltpu.CompilerParams(vmem_limit_bytes=53 * MIB),
        cost_estimate=pl.CostEstimate(
            flops=rows * hidden * rank, bytes_accessed=2 * rows * hidden, transcendentals=0
        ),
        name="compensate_and_left",
    )(grads, error, q_start)


def partner(value, by, size):
    return lax.ppermute(value, "dp", [(i, i ^ by) for i in range(size)])


def first_share(grads, error, q_start, replicas):
    other, theirs = first(grads, error, q_start, replicas, 1)
    arrived = partner(theirs, 1, replicas)
    own, mine = first(grads, error, q_start, replicas, 0)
    pairs = [
        arrived[k].astype(jnp.float32) + mine[k].astype(jnp.float32) for k in range(replicas // 2)
    ]
    total = pairs[0]
    for value in [
        partner(pairs[k].astype(jnp.bfloat16), 2 * k, replicas) for k in range(1, replicas // 2)
    ]:
        total = total + value.astype(jnp.float32)
    return (own, other), total


def inverse_lower(gram):
    rank = gram.shape[0]
    row = lax.broadcasted_iota(jnp.int32, (SUBLANES, 2 * rank), 0)
    across = lax.broadcasted_iota(jnp.int32, (SUBLANES, 2 * rank), 1)
    both = jnp.concatenate([jnp.zeros((rank, rank), jnp.float32), gram], axis=1)
    starts = range(0, rank, SUBLANES)
    tiles = [
        jnp.where(across == row + at, 1.0, both[at : at + SUBLANES, :]) for at in starts
    ]
    inverse = []
    for top, base in enumerate(starts):
        columns = [
            [
                jnp.broadcast_to(tile[:, rank + k : rank + k + 1], tile.shape)
                for tile in tiles[top:]
            ]
            for k in range(base, base + SUBLANES)
        ]
        for j in range(SUBLANES):
            head = columns[j][0]
            reciprocal = 1.0 / head[j : j + 1, :]
            pivot_row = tiles[top][j : j + 1, :]
            for at in range(len(columns[j])):
                factor = columns[j][at] * reciprocal
                if at == 0:
                    factor = jnp.where(row > j, factor, 0.0)
                for i in range(j + 1, SUBLANES):
                    columns[i][at] = columns[i][at] - factor * head[i : i + 1, :]
                tiles[top + at] = tiles[top + at] - factor * pivot_row
        done = tiles[top]
        pivots = jnp.sum(
            jnp.where(across == row + (rank + base), done, 0.0), axis=1, keepdims=True
        )
        inverse.append(done[:, :rank] * lax.rsqrt(pivots))
    return jnp.concatenate(inverse, axis=0)


def columns_of(arrived, tiles, x, first_tile, count):
    rank = arrived.shape[1] // tiles
    parts = []
    for at in range(first_tile, first_tile + count):
        block, tile = divmod(at, tiles)
        parts.append(arrived[2 * block + x, tile * rank : (tile + 1) * rank, :])
    return jnp.concatenate(parts, axis=1)


def right_kernel(tiles, arrived, halves, term, inverse_out=None):
    x = lax.axis_index("dp") & 1
    count = arrived.shape[0] // 2 * tiles
    factors = [columns_of(arrived, tiles, x ^ flip, 0, count) for flip in range(2)]
    factor_p = jnp.concatenate(factors, axis=1)
    gram = lax.dot_general(
        factor_p, factor_p, CONTRACT_LAST, preferred_element_type=jnp.float32
    )
    product = sum(
        jnp.dot(factor, half[...], preferred_element_type=jnp.float32)
        for factor, half in zip(factors, halves)
    )
    inverse = inverse_lower(gram)
    if inverse_out is not None:
        inverse_out[...] = inverse
    term[...] = jnp.dot(
        inverse, product, precision=lax.Precision.HIGHEST, preferred_element_type=jnp.float32
    ).astype(jnp.bfloat16)


def right(arrived, halves, rank, keep):
    out_shape = [pltpu.VMEM((rank, halves[0].shape[1]), jnp.bfloat16)]
    in_vmem = pl.BlockSpec(memory_space=pltpu.VMEM)
    if keep:
        out_shape.append(pltpu.VMEM((rank, rank), jnp.float32))
    return pl.pallas_call(
        functools.partial(right_kernel, arrived.shape[1] // rank),
        in_specs=[in_vmem, (in_vmem, in_vmem)],
        out_specs=[in_vmem] * len(out_shape),
        out_shape=out_shape,
        compiler_params=pltpu.CompilerParams(vmem_limit_bytes=24 * MIB),
        name="orthogonalize_and_right",
    )(arrived, halves)


def addends(term, size):
    step = 1
    while 4 * step < size:
        term = (term.astype(jnp.float32) + partner(term, step, size).astype(jnp.float32)).astype(
            jnp.bfloat16
        )
        step *= 2
    return [term] + [partner(term, by, size) for by in (step, 2 * step, 3 * step)]


def sum_of(parts):
    one, two, three, four = [part[...].astype(jnp.float32) for part in parts]
    return (one + two) + (three + four)


def left_kernel(parts, halves, bucket, outgoing, landed, sem):
    replicas = outgoing.shape[0]
    block = 2 * halves[0].shape[0] // replicas
    x = lax.axis_index("dp") & 1
    fetch = pltpu.make_async_copy(bucket, landed, sem)
    fetch.start()
    factor_q = sum_of(parts) / replicas
    norm = jnp.sqrt(jnp.sum(factor_q * factor_q, axis=1, keepdims=True) + 1e-06)
    q_half = factor_q.astype(jnp.bfloat16)
    for flip, half in enumerate(halves):
        for j in range(replicas // 2):
            local_p = lax.dot_general(
                q_half,
                half[j * block : (j + 1) * block, :],
                CONTRACT_LAST,
                preferred_element_type=jnp.float32,
            )
            store_tiles(outgoing.at[2 * j + (x ^ flip)], (local_p / norm).astype(jnp.bfloat16))
    fetch.wait()
    outgoing[:, -bucket.shape[1] :, :] = landed[...].astype(jnp.bfloat16)


def left(parts, halves, bucket):
    replicas = bucket.shape[0]
    tall = 2 * halves[0].shape[0] // replicas * parts[0].shape[0] // LANES + bucket.shape[1]
    in_vmem = pl.BlockSpec(memory_space=pltpu.VMEM)
    return pl.pallas_call(
        left_kernel,
        in_specs=[[in_vmem] * len(parts), (in_vmem, in_vmem), pl.BlockSpec(memory_space=pl.ANY)],
        out_specs=in_vmem,
        out_shape=pltpu.VMEM((replicas, tall, LANES), jnp.bfloat16),
        scratch_shapes=[pltpu.VMEM(bucket.shape, jnp.float32), pltpu.SemaphoreType.DMA(())],
        compiler_params=pltpu.CompilerParams(vmem_limit_bytes=24 * MIB),
        name="normalize_and_left",
    )(parts, halves, bucket)


def last_kernel(
    replicas, parts, inverse, arrived, halves, share,
    update, new_error, bucket_mean, update_held, error_held, sems, bucket_sem,
):
    tall = bucket_mean.shape[0]
    there = pl.ds(share.shape[0] - tall, tall)
    copies = [pltpu.make_async_copy(share.at[there], bucket_mean, bucket_sem)]
    copies[0].start()
    rows, hidden = halves[0].shape
    tiles = 2 * rows // replicas // LANES
    x = lax.axis_index("dp") & 1
    right = lax.dot_general(
        inverse[...],
        sum_of(parts) / replicas,
        CONTRACT_FIRST,
        precision=lax.Precision.HIGHEST,
        preferred_element_type=jnp.float32,
    )
    right = jnp.concatenate(three_parts(right), axis=0)
    for flip, half in enumerate(halves):
        for i, (at, size) in enumerate(pieces(rows, flip == 0)):
            where = slice(at, at + size)
            p_block = columns_of(arrived, tiles, x ^ flip, at // LANES, size // LANES).T
            block = jnp.dot(
                jnp.concatenate([p_block] * 3, axis=1), right, preferred_element_type=jnp.float32
            )
            update_held[flip, where, :] = block
            error_held[flip, where, :] = (half[where, :].astype(jnp.float32) - block).astype(
                jnp.bfloat16
            )
            there = pl.ds(pl.multiple_of((x ^ flip) * rows + at, LANES), size)
            for j, (held, out) in enumerate(((update_held, update), (error_held, new_error))):
                copies.append(
                    pltpu.make_async_copy(
                        held.at[flip, pl.ds(at, size)], out.at[there], sems.at[j, flip, i]
                    )
                )
                copies[-1].start(priority=j)
    for copy in copies:
        copy.wait()


def last(parts, inverse, arrived, halves, share, replicas, bucket_tall):
    rows, hidden = halves[0].shape
    in_vmem = pl.BlockSpec(memory_space=pltpu.VMEM)
    return pl.pallas_call(
        functools.partial(last_kernel, replicas),
        in_specs=[[in_vmem] * len(parts), in_vmem, in_vmem, (in_vmem, in_vmem), in_vmem],
        out_specs=[pl.BlockSpec(memory_space=pl.ANY)] * 3,
        out_shape=[
            jax.ShapeDtypeStruct((2 * rows, hidden), jnp.float32),
            jax.ShapeDtypeStruct((2 * rows, hidden), jnp.bfloat16),
            jax.ShapeDtypeStruct((bucket_tall, LANES), jnp.float32),
        ],
        scratch_shapes=[
            pltpu.VMEM((2, rows, hidden), jnp.float32),
            pltpu.VMEM((2, rows, hidden), jnp.bfloat16),
            pltpu.SemaphoreType.DMA((2, 2, len(pieces(rows, True)))),
            pltpu.SemaphoreType.DMA(()),
        ],
        compiler_params=pltpu.CompilerParams(vmem_limit_bytes=40 * MIB),
        name="update_and_error",
    )(parts, inverse, arrived, halves, share)


def on_device(grads, error, q_start, bucket):
    replicas = lax.axis_size("dp")
    rows = grads.shape[1]
    rank = q_start.shape[1]
    bucket = bucket.reshape(replicas, -1, LANES)
    tall = rows // replicas * rank // LANES
    halves, share = first_share(grads[0], error[0], q_start.T, replicas)
    for step in range(ITERS):
        if step > 0:
            share = jnp.sum(exchange(outgoing).astype(jnp.float32), axis=0)
        share = share / replicas
        factor_p = everywhere(share[:tall].astype(jnp.bfloat16), replicas)
        term, *inverse = right(factor_p, halves, rank, step + 1 == ITERS)
        parts = addends(term, replicas)
        if step + 1 < ITERS:
            outgoing = left(parts, halves, bucket)
    update, new_error, bucket_mean = last(
        parts, inverse[0], factor_p, halves, share, replicas, bucket.shape[1]
    )
    return (update, new_error[None], bucket_mean.reshape(-1))


def solution(mesh):
    return jax.shard_map(
        on_device,
        mesh=mesh,
        in_specs=(
            P("dp", None, "expert"),
            P("dp", None, "expert"),
            P("expert", None),
            P("dp", "expert"),
        ),
        out_specs=(P(None, "expert"), P("dp", None, "expert"), P(("expert", "dp"))),
        check_vma=False,
    )
```

```python
import functools

import jax
import jax.numpy as jnp
from jax import lax
from jax.experimental import pallas as pl
from jax.experimental.pallas import tpu as pltpu
from jax.sharding import PartitionSpec as P

ITERS = 2
LANES = 128
SUBLANES = 8
MIB = 1024 * 1024
CONTRACT_FIRST = (((0,), (0,)), ((), ()))
CONTRACT_LAST = (((1,), (1,)), ((), ()))


def exchange(chunks):
    return lax.all_to_all(chunks, "dp", split_axis=0, concat_axis=0, tiled=True)


def everywhere(share, size):
    return exchange(jnp.broadcast_to(share, (size,) + share.shape))


def three_parts(value):
    high = value.astype(jnp.bfloat16)
    rest = value - high.astype(jnp.float32)
    middle = rest.astype(jnp.bfloat16)
    low = (rest - middle.astype(jnp.float32)).astype(jnp.bfloat16)
    return high, middle, low


def pieces(rows, grow):
    sizes = [4 * LANES] * (rows // (4 * LANES))
    if grow:
        sizes[:1] = [LANES, LANES, 2 * LANES]
    return [(sum(sizes[:i]), size) for i, size in enumerate(sizes)]


def store_tiles(chunk, value):
    rank, columns = value.shape
    for tile in range(columns // LANES):
        chunk[tile * rank : (tile + 1) * rank, :] = value[:, tile * LANES : (tile + 1) * LANES]


def first_kernel(replicas, flip, grads, error, q_start, bucket, compensated, outgoing, *scratch):
    landed, q_landed, bucket_landed, sems, q_sem, bucket_sems = scratch
    fetch_q = pltpu.make_async_copy(q_start, q_landed, q_sem)
    fetch_q.start()
    me = lax.axis_index("dp")
    half = replicas // 2
    block = grads.shape[0] // replicas
    starts, copies = [], []
    for k in range(half):
        starts.append(pl.multiple_of(((me >> 1) ^ k) * block, block))
        there = pl.multiple_of(((me & 1) ^ flip) * (half * block) + starts[k], block)
        for j, array in enumerate((grads, error)):
            copies.append(
                pltpu.make_async_copy(
                    array.at[pl.ds(there, block)], landed.at[j, k], sems.at[j, k]
                )
            )
            copies[-1].start(priority=j)
    bucket_copies = []
    for k in range(half):
        chunk = 2 * ((me >> 1) ^ k) + ((me & 1) ^ flip)
        bucket_copies.append(
            pltpu.make_async_copy(bucket.at[chunk], bucket_landed.at[k], bucket_sems.at[k])
        )
        bucket_copies[-1].start()
    fetch_q.wait()
    q_half = q_landed[...].astype(jnp.bfloat16)
    for k in range(half):
        copies[2 * k].wait()
        copies[2 * k + 1].wait()
        value = (landed[0, k].astype(jnp.float32) + landed[1, k].astype(jnp.float32)).astype(
            jnp.bfloat16
        )
        compensated[pl.ds(starts[k], block), :] = value
        local_p = lax.dot_general(q_half, value, CONTRACT_LAST, preferred_element_type=jnp.float32)
        store_tiles(outgoing.at[k], local_p.astype(jnp.bfloat16))
    for copy in bucket_copies:
        copy.wait()
    outgoing[:, -bucket.shape[1] :, :] = bucket_landed[...].astype(jnp.bfloat16)


def first(grads, error, q_start, bucket, flip):
    rows, hidden = grads.shape
    rank = q_start.shape[0]
    replicas = bucket.shape[0]
    block = rows // replicas
    half = replicas // 2
    tall = block // LANES * rank + bucket.shape[1]
    return pl.pallas_call(
        functools.partial(first_kernel, replicas, flip),
        in_specs=[pl.BlockSpec(memory_space=pl.ANY)] * 4,
        out_specs=[pl.BlockSpec(memory_space=pltpu.VMEM)] * 2,
        out_shape=[
            pltpu.VMEM((half * block, hidden), jnp.bfloat16),
            pltpu.VMEM((half, tall, LANES), jnp.bfloat16),
        ],
        scratch_shapes=[
            pltpu.VMEM((2, half, block, hidden), jnp.bfloat16),
            pltpu.VMEM(q_start.shape, jnp.float32),
            pltpu.VMEM((half,) + bucket.shape[1:], jnp.float32),
            pltpu.SemaphoreType.DMA((2, half)),
            pltpu.SemaphoreType.DMA(()),
            pltpu.SemaphoreType.DMA((half,)),
        ],
        compiler_params=pltpu.CompilerParams(vmem_limit_bytes=(53 + 3 * flip) * MIB),
        cost_estimate=pl.CostEstimate(
            flops=rows * hidden * rank, bytes_accessed=2 * rows * hidden, transcendentals=0
        ),
        name="compensate_and_left",
    )(grads, error, q_start, bucket)


def partner(value, by, size):
    return lax.ppermute(value, "dp", [(i, i ^ by) for i in range(size)])


def first_share(grads, error, q_start, bucket):
    replicas = bucket.shape[0]
    other, theirs = first(grads, error, q_start, bucket, 1)
    arrived = partner(theirs, 1, replicas)
    own, mine = first(grads, error, q_start, bucket, 0)
    pairs = [
        arrived[k].astype(jnp.float32) + mine[k].astype(jnp.float32) for k in range(replicas // 2)
    ]
    total = pairs[0]
    for value in [
        partner(pairs[k].astype(jnp.bfloat16), 2 * k, replicas) for k in range(1, replicas // 2)
    ]:
        total = total + value.astype(jnp.float32)
    return (own, other), total


def inverse_lower(gram):
    rank = gram.shape[0]
    row = lax.broadcasted_iota(jnp.int32, (SUBLANES, 2 * rank), 0)
    across = lax.broadcasted_iota(jnp.int32, (SUBLANES, 2 * rank), 1)
    both = jnp.concatenate([jnp.zeros((rank, rank), jnp.float32), gram], axis=1)
    starts = range(0, rank, SUBLANES)
    tiles = [
        jnp.where(across == row + at, 1.0, both[at : at + SUBLANES, :]) for at in starts
    ]
    inverse = []
    for top, base in enumerate(starts):
        columns = [
            [
                jnp.broadcast_to(tile[:, rank + k : rank + k + 1], tile.shape)
                for tile in tiles[top:]
            ]
            for k in range(base, base + SUBLANES)
        ]
        for j in range(SUBLANES):
            head = columns[j][0]
            reciprocal = 1.0 / head[j : j + 1, :]
            pivot_row = tiles[top][j : j + 1, :]
            for at in range(len(columns[j])):
                factor = columns[j][at] * reciprocal
                if at == 0:
                    factor = jnp.where(row > j, factor, 0.0)
                for i in range(j + 1, SUBLANES):
                    columns[i][at] = columns[i][at] - factor * head[i : i + 1, :]
                tiles[top + at] = tiles[top + at] - factor * pivot_row
        done = tiles[top]
        pivots = jnp.sum(
            jnp.where(across == row + (rank + base), done, 0.0), axis=1, keepdims=True
        )
        inverse.append(done[:, :rank] * lax.rsqrt(pivots))
    return jnp.concatenate(inverse, axis=0)


def columns_of(arrived, tiles, x, first_tile, count):
    rank = arrived.shape[1] // tiles
    parts = []
    for at in range(first_tile, first_tile + count):
        block, tile = divmod(at, tiles)
        parts.append(arrived[2 * block + x, tile * rank : (tile + 1) * rank, :])
    return jnp.concatenate(parts, axis=1)


def right_kernel(tiles, arrived, halves, term, inverse_out=None):
    x = lax.axis_index("dp") & 1
    count = arrived.shape[0] // 2 * tiles
    factors = [columns_of(arrived, tiles, x ^ flip, 0, count) for flip in range(2)]
    factor_p = jnp.concatenate(factors, axis=1)
    gram = lax.dot_general(
        factor_p, factor_p, CONTRACT_LAST, preferred_element_type=jnp.float32
    )
    product = sum(
        jnp.dot(factor, half[...], preferred_element_type=jnp.float32)
        for factor, half in zip(factors, halves)
    )
    inverse = inverse_lower(gram)
    if inverse_out is not None:
        inverse_out[...] = inverse
    term[...] = jnp.dot(
        inverse, product, precision=lax.Precision.HIGHEST, preferred_element_type=jnp.float32
    ).astype(jnp.bfloat16)


def right(arrived, halves, rank, keep):
    out_shape = [pltpu.VMEM((rank, halves[0].shape[1]), jnp.bfloat16)]
    in_vmem = pl.BlockSpec(memory_space=pltpu.VMEM)
    if keep:
        out_shape.append(pltpu.VMEM((rank, rank), jnp.float32))
    return pl.pallas_call(
        functools.partial(right_kernel, arrived.shape[1] // rank),
        in_specs=[in_vmem, (in_vmem, in_vmem)],
        out_specs=[in_vmem] * len(out_shape),
        out_shape=out_shape,
        compiler_params=pltpu.CompilerParams(vmem_limit_bytes=24 * MIB),
        name="orthogonalize_and_right",
    )(arrived, halves)


def addends(term, size):
    one, two, three, four = [
        part.astype(jnp.float32) for part in [term] + [partner(term, by, size) for by in (1, 2, 3)]
    ]
    term = ((one + two) + (three + four)).astype(jnp.bfloat16)
    step = 4
    while 2 * step < size:
        term = (term.astype(jnp.float32) + partner(term, step, size).astype(jnp.float32)).astype(
            jnp.bfloat16
        )
        step *= 2
    return [term, partner(term, step, size)]


def sum_of(parts):
    one, two = [part[...].astype(jnp.float32) for part in parts]
    return one + two


def left_kernel(parts, halves, outgoing):
    replicas = outgoing.shape[0]
    block = 2 * halves[0].shape[0] // replicas
    x = lax.axis_index("dp") & 1
    factor_q = sum_of(parts) / replicas
    norm = jnp.sqrt(jnp.sum(factor_q * factor_q, axis=1, keepdims=True) + 1e-06)
    q_half = factor_q.astype(jnp.bfloat16)
    for flip, half in enumerate(halves):
        for j in range(replicas // 2):
            local_p = lax.dot_general(
                q_half,
                half[j * block : (j + 1) * block, :],
                CONTRACT_LAST,
                preferred_element_type=jnp.float32,
            )
            store_tiles(outgoing.at[2 * j + (x ^ flip)], (local_p / norm).astype(jnp.bfloat16))


def left(parts, halves, replicas):
    tall = 2 * halves[0].shape[0] // replicas * parts[0].shape[0] // LANES
    in_vmem = pl.BlockSpec(memory_space=pltpu.VMEM)
    return pl.pallas_call(
        left_kernel,
        in_specs=[[in_vmem] * len(parts), (in_vmem, in_vmem)],
        out_specs=in_vmem,
        out_shape=pltpu.VMEM((replicas, tall, LANES), jnp.bfloat16),
        compiler_params=pltpu.CompilerParams(vmem_limit_bytes=24 * MIB),
        name="normalize_and_left",
    )(parts, halves)


def last_kernel(
    replicas, parts, inverse, arrived, halves, share,
    update, new_error, bucket_mean, update_held, error_held, sems, bucket_sem,
):
    tall = bucket_mean.shape[0]
    there = pl.ds(share.shape[0] - tall, tall)
    copies = [pltpu.make_async_copy(share.at[there], bucket_mean, bucket_sem)]
    copies[0].start()
    rows, hidden = halves[0].shape
    tiles = 2 * rows // replicas // LANES
    x = lax.axis_index("dp") & 1
    right = lax.dot_general(
        inverse[...],
        sum_of(parts) / replicas,
        CONTRACT_FIRST,
        precision=lax.Precision.HIGHEST,
        preferred_element_type=jnp.float32,
    )
    right = jnp.concatenate(three_parts(right), axis=0)
    for flip, half in enumerate(halves):
        for i, (at, size) in enumerate(pieces(rows, flip == 0)):
            where = slice(at, at + size)
            p_block = columns_of(arrived, tiles, x ^ flip, at // LANES, size // LANES).T
            block = jnp.dot(
                jnp.concatenate([p_block] * 3, axis=1), right, preferred_element_type=jnp.float32
            )
            update_held[flip, where, :] = block
            error_held[flip, where, :] = (half[where, :].astype(jnp.float32) - block).astype(
                jnp.bfloat16
            )
            there = pl.ds(pl.multiple_of((x ^ flip) * rows + at, LANES), size)
            for j, (held, out) in enumerate(((update_held, update), (error_held, new_error))):
                copies.append(
                    pltpu.make_async_copy(
                        held.at[flip, pl.ds(at, size)], out.at[there], sems.at[j, flip, i]
                    )
                )
                copies[-1].start(priority=j)
    for copy in copies:
        copy.wait()


def last(parts, inverse, arrived, halves, share, replicas, bucket_tall):
    rows, hidden = halves[0].shape
    in_vmem = pl.BlockSpec(memory_space=pltpu.VMEM)
    return pl.pallas_call(
        functools.partial(last_kernel, replicas),
        in_specs=[[in_vmem] * len(parts), in_vmem, in_vmem, (in_vmem, in_vmem), in_vmem],
        out_specs=[pl.BlockSpec(memory_space=pl.ANY)] * 3,
        out_shape=[
            jax.ShapeDtypeStruct((2 * rows, hidden), jnp.float32),
            jax.ShapeDtypeStruct((2 * rows, hidden), jnp.bfloat16),
            jax.ShapeDtypeStruct((bucket_tall, LANES), jnp.float32),
        ],
        scratch_shapes=[
            pltpu.VMEM((2, rows, hidden), jnp.float32),
            pltpu.VMEM((2, rows, hidden), jnp.bfloat16),
            pltpu.SemaphoreType.DMA((2, 2, len(pieces(rows, True)))),
            pltpu.SemaphoreType.DMA(()),
        ],
        compiler_params=pltpu.CompilerParams(vmem_limit_bytes=40 * MIB),
        name="update_and_error",
    )(parts, inverse, arrived, halves, share)


def on_device(grads, error, q_start, bucket):
    replicas = lax.axis_size("dp")
    rows = grads.shape[1]
    rank = q_start.shape[1]
    bucket = bucket.reshape(replicas, -1, LANES)
    tall = rows // replicas * rank // LANES
    halves, share = first_share(grads[0], error[0], q_start.T, bucket)
    first_sums = share / replicas
    for step in range(ITERS):
        if step > 0:
            share = jnp.sum(exchange(outgoing).astype(jnp.float32), axis=0)
        share = share / replicas
        factor_p = everywhere(share[:tall].astype(jnp.bfloat16), replicas)
        term, *inverse = right(factor_p, halves, rank, step + 1 == ITERS)
        parts = addends(term, replicas)
        if step + 1 < ITERS:
            outgoing = left(parts, halves, replicas)
    update, new_error, bucket_mean = last(
        parts, inverse[0], factor_p, halves, first_sums, replicas, bucket.shape[1]
    )
    return (update, new_error[None], bucket_mean.reshape(-1))


def solution(mesh):
    return jax.shard_map(
        on_device,
        mesh=mesh,
        in_specs=(
            P("dp", None, "expert"),
            P("dp", None, "expert"),
            P("expert", None),
            P("dp", "expert"),
        ),
        out_specs=(P(None, "expert"), P("dp", None, "expert"), P(("expert", "dp"))),
        check_vma=False,
    )
```

```python
import functools

import jax
import jax.numpy as jnp
from jax import lax
from jax.experimental import pallas as pl
from jax.experimental.pallas import tpu as pltpu
from jax.sharding import PartitionSpec as P

ITERS = 2
LANES = 128
SUBLANES = 8
MIB = 1024 * 1024
CONTRACT_FIRST = (((0,), (0,)), ((), ()))
CONTRACT_LAST = (((1,), (1,)), ((), ()))


def exchange(chunks):
    return lax.all_to_all(chunks, "dp", split_axis=0, concat_axis=0, tiled=True)


def everywhere(share, size):
    return exchange(jnp.broadcast_to(share, (size,) + share.shape))


def three_parts(value):
    high = value.astype(jnp.bfloat16)
    rest = value - high.astype(jnp.float32)
    middle = rest.astype(jnp.bfloat16)
    low = (rest - middle.astype(jnp.float32)).astype(jnp.bfloat16)
    return high, middle, low


def pieces(rows, grow):
    sizes = [4 * LANES] * (rows // (4 * LANES))
    if grow:
        sizes[:1] = [LANES, LANES, 2 * LANES]
    return [(sum(sizes[:i]), size) for i, size in enumerate(sizes)]


def store_tiles(chunk, value):
    rank, columns = value.shape
    for tile in range(columns // LANES):
        chunk[tile * rank : (tile + 1) * rank, :] = value[:, tile * LANES : (tile + 1) * LANES]


def first_kernel(replicas, flip, grads, error, q_start, compensated, outgoing, *scratch):
    landed, q_landed, sems, q_sem = scratch
    fetch_q = pltpu.make_async_copy(q_start, q_landed, q_sem)
    fetch_q.start()
    me = lax.axis_index("dp")
    half = replicas // 2
    block = grads.shape[0] // replicas
    starts, copies = [], []
    for k in range(half):
        starts.append(pl.multiple_of(((me >> 1) ^ k) * block, block))
        there = pl.multiple_of(((me & 1) ^ flip) * (half * block) + starts[k], block)
        for j, array in enumerate((grads, error)):
            copies.append(
                pltpu.make_async_copy(
                    array.at[pl.ds(there, block)], landed.at[j, k], sems.at[j, k]
                )
            )
            copies[-1].start(priority=j)
    fetch_q.wait()
    q_half = q_landed[...].astype(jnp.bfloat16)
    for k in range(half):
        copies[2 * k].wait()
        copies[2 * k + 1].wait()
        value = (landed[0, k].astype(jnp.float32) + landed[1, k].astype(jnp.float32)).astype(
            jnp.bfloat16
        )
        compensated[pl.ds(starts[k], block), :] = value
        local_p = lax.dot_general(q_half, value, CONTRACT_LAST, preferred_element_type=jnp.float32)
        store_tiles(outgoing.at[k], local_p.astype(jnp.bfloat16))


def first(grads, error, q_start, replicas, flip):
    rows, hidden = grads.shape
    rank = q_start.shape[0]
    block = rows // replicas
    half = replicas // 2
    return pl.pallas_call(
        functools.partial(first_kernel, replicas, flip),
        in_specs=[pl.BlockSpec(memory_space=pl.ANY)] * 3,
        out_specs=[pl.BlockSpec(memory_space=pltpu.VMEM)] * 2,
        out_shape=[
            pltpu.VMEM((half * block, hidden), jnp.bfloat16),
            pltpu.VMEM((half, block // LANES * rank, LANES), jnp.bfloat16),
        ],
        scratch_shapes=[
            pltpu.VMEM((2, half, block, hidden), jnp.bfloat16),
            pltpu.VMEM(q_start.shape, jnp.float32),
            pltpu.SemaphoreType.DMA((2, half)),
            pltpu.SemaphoreType.DMA(()),
        ],
        compiler_params=pltpu.CompilerParams(vmem_limit_bytes=53 * MIB),
        cost_estimate=pl.CostEstimate(
            flops=rows * hidden * rank, bytes_accessed=2 * rows * hidden, transcendentals=0
        ),
        name="compensate_and_left",
    )(grads, error, q_start)


def partner(value, by, size):
    return lax.ppermute(value, "dp", [(i, i ^ by) for i in range(size)])


def first_share(grads, error, q_start, replicas):
    other, theirs = first(grads, error, q_start, replicas, 1)
    arrived = partner(theirs, 1, replicas)
    own, mine = first(grads, error, q_start, replicas, 0)
    pairs = [
        arrived[k].astype(jnp.float32) + mine[k].astype(jnp.float32) for k in range(replicas // 2)
    ]
    total = pairs[0]
    for value in [
        partner(pairs[k].astype(jnp.bfloat16), 2 * k, replicas) for k in range(1, replicas // 2)
    ]:
        total = total + value.astype(jnp.float32)
    return (own, other), total


def inverse_lower(gram):
    rank = gram.shape[0]
    row = lax.broadcasted_iota(jnp.int32, (SUBLANES, 2 * rank), 0)
    across = lax.broadcasted_iota(jnp.int32, (SUBLANES, 2 * rank), 1)
    both = jnp.concatenate([jnp.zeros((rank, rank), jnp.float32), gram], axis=1)
    starts = range(0, rank, SUBLANES)
    tiles = [
        jnp.where(across == row + at, 1.0, both[at : at + SUBLANES, :]) for at in starts
    ]
    inverse = []
    for top, base in enumerate(starts):
        columns = [
            [
                jnp.broadcast_to(tile[:, rank + k : rank + k + 1], tile.shape)
                for tile in tiles[top:]
            ]
            for k in range(base, base + SUBLANES)
        ]
        for j in range(SUBLANES):
            head = columns[j][0]
            reciprocal = 1.0 / head[j : j + 1, :]
            pivot_row = tiles[top][j : j + 1, :]
            for at in range(len(columns[j])):
                factor = columns[j][at] * reciprocal
                if at == 0:
                    factor = jnp.where(row > j, factor, 0.0)
                for i in range(j + 1, SUBLANES):
                    columns[i][at] = columns[i][at] - factor * head[i : i + 1, :]
                tiles[top + at] = tiles[top + at] - factor * pivot_row
        done = tiles[top]
        pivots = jnp.sum(
            jnp.where(across == row + (rank + base), done, 0.0), axis=1, keepdims=True
        )
        inverse.append(done[:, :rank] * lax.rsqrt(pivots))
    return jnp.concatenate(inverse, axis=0)


def columns_of(arrived, tiles, x, first_tile, count):
    rank = arrived.shape[1] // tiles
    parts = []
    for at in range(first_tile, first_tile + count):
        block, tile = divmod(at, tiles)
        parts.append(arrived[2 * block + x, tile * rank : (tile + 1) * rank, :])
    return jnp.concatenate(parts, axis=1)


def right_kernel(tiles, arrived, halves, term, inverse_out=None):
    x = lax.axis_index("dp") & 1
    count = arrived.shape[0] // 2 * tiles
    factors = [columns_of(arrived, tiles, x ^ flip, 0, count) for flip in range(2)]
    factor_p = jnp.concatenate(factors, axis=1)
    gram = lax.dot_general(
        factor_p, factor_p, CONTRACT_LAST, preferred_element_type=jnp.float32
    )
    product = sum(
        jnp.dot(factor, half[...], preferred_element_type=jnp.float32)
        for factor, half in zip(factors, halves)
    )
    inverse = inverse_lower(gram)
    if inverse_out is not None:
        inverse_out[...] = inverse
    term[...] = jnp.dot(
        inverse, product, precision=lax.Precision.HIGHEST, preferred_element_type=jnp.float32
    ).astype(jnp.bfloat16)


def right(arrived, halves, rank, keep):
    out_shape = [pltpu.VMEM((rank, halves[0].shape[1]), jnp.bfloat16)]
    in_vmem = pl.BlockSpec(memory_space=pltpu.VMEM)
    if keep:
        out_shape.append(pltpu.VMEM((rank, rank), jnp.float32))
    return pl.pallas_call(
        functools.partial(right_kernel, arrived.shape[1] // rank),
        in_specs=[in_vmem, (in_vmem, in_vmem)],
        out_specs=[in_vmem] * len(out_shape),
        out_shape=out_shape,
        compiler_params=pltpu.CompilerParams(vmem_limit_bytes=24 * MIB),
        name="orthogonalize_and_right",
    )(arrived, halves)


def addends(term, size):
    one, two, three, four = [
        part.astype(jnp.float32) for part in [term] + [partner(term, by, size) for by in (1, 2, 3)]
    ]
    term = ((one + two) + (three + four)).astype(jnp.bfloat16)
    step = 4
    while 2 * step < size:
        term = (term.astype(jnp.float32) + partner(term, step, size).astype(jnp.float32)).astype(
            jnp.bfloat16
        )
        step *= 2
    return [term, partner(term, step, size)]


def turn(term):
    size = lax.axis_size("dp") * lax.axis_size("expert")
    return lax.ppermute(
        term[:16, :LANES], ("dp", "expert"), [(i, i + 1) for i in range(0, size, 2)]
    )


def sum_of(parts):
    one, two = [part[...].astype(jnp.float32) for part in parts]
    return one + two


def left_kernel(parts, halves, bucket, token, outgoing, landed, sem):
    replicas = outgoing.shape[0]
    block = 2 * halves[0].shape[0] // replicas
    x = lax.axis_index("dp") & 1
    fetch = pltpu.make_async_copy(bucket, landed, sem)
    fetch.start()
    factor_q = sum_of(parts) / replicas
    norm = jnp.sqrt(jnp.sum(factor_q * factor_q, axis=1, keepdims=True) + 1e-06)
    q_half = factor_q.astype(jnp.bfloat16)
    for flip, half in enumerate(halves):
        for j in range(replicas // 2):
            local_p = lax.dot_general(
                q_half,
                half[j * block : (j + 1) * block, :],
                CONTRACT_LAST,
                preferred_element_type=jnp.float32,
            )
            store_tiles(outgoing.at[2 * j + (x ^ flip)], (local_p / norm).astype(jnp.bfloat16))
    fetch.wait()
    outgoing[:, -bucket.shape[1] :, :] = landed[...].astype(jnp.bfloat16)


def left(parts, halves, bucket, token):
    replicas = bucket.shape[0]
    tall = 2 * halves[0].shape[0] // replicas * parts[0].shape[0] // LANES + bucket.shape[1]
    in_vmem = pl.BlockSpec(memory_space=pltpu.VMEM)
    return pl.pallas_call(
        left_kernel,
        in_specs=[
            [in_vmem] * len(parts),
            (in_vmem, in_vmem),
            pl.BlockSpec(memory_space=pl.ANY),
            in_vmem,
        ],
        out_specs=in_vmem,
        out_shape=pltpu.VMEM((replicas, tall, LANES), jnp.bfloat16),
        scratch_shapes=[pltpu.VMEM(bucket.shape, jnp.float32), pltpu.SemaphoreType.DMA(())],
        compiler_params=pltpu.CompilerParams(vmem_limit_bytes=24 * MIB),
        name="normalize_and_left",
    )(parts, halves, bucket, token)


def last_kernel(
    replicas, parts, inverse, arrived, halves, share,
    update, new_error, bucket_mean, update_held, error_held, sems, bucket_sem,
):
    tall = bucket_mean.shape[0]
    there = pl.ds(share.shape[0] - tall, tall)
    copies = [pltpu.make_async_copy(share.at[there], bucket_mean, bucket_sem)]
    copies[0].start()
    rows, hidden = halves[0].shape
    tiles = 2 * rows // replicas // LANES
    x = lax.axis_index("dp") & 1
    right = lax.dot_general(
        inverse[...],
        sum_of(parts) / replicas,
        CONTRACT_FIRST,
        precision=lax.Precision.HIGHEST,
        preferred_element_type=jnp.float32,
    )
    right = jnp.concatenate(three_parts(right), axis=0)
    for flip, half in enumerate(halves):
        for i, (at, size) in enumerate(pieces(rows, flip == 0)):
            where = slice(at, at + size)
            p_block = columns_of(arrived, tiles, x ^ flip, at // LANES, size // LANES).T
            block = jnp.dot(
                jnp.concatenate([p_block] * 3, axis=1), right, preferred_element_type=jnp.float32
            )
            update_held[flip, where, :] = block
            error_held[flip, where, :] = (half[where, :].astype(jnp.float32) - block).astype(
                jnp.bfloat16
            )
            there = pl.ds(pl.multiple_of((x ^ flip) * rows + at, LANES), size)
            for j, (held, out) in enumerate(((update_held, update), (error_held, new_error))):
                copies.append(
                    pltpu.make_async_copy(
                        held.at[flip, pl.ds(at, size)], out.at[there], sems.at[j, flip, i]
                    )
                )
                copies[-1].start(priority=j)
    for copy in copies:
        copy.wait()


def last(parts, inverse, arrived, halves, share, replicas, bucket_tall):
    rows, hidden = halves[0].shape
    in_vmem = pl.BlockSpec(memory_space=pltpu.VMEM)
    return pl.pallas_call(
        functools.partial(last_kernel, replicas),
        in_specs=[[in_vmem] * len(parts), in_vmem, in_vmem, (in_vmem, in_vmem), in_vmem],
        out_specs=[pl.BlockSpec(memory_space=pl.ANY)] * 3,
        out_shape=[
            jax.ShapeDtypeStruct((2 * rows, hidden), jnp.float32),
            jax.ShapeDtypeStruct((2 * rows, hidden), jnp.bfloat16),
            jax.ShapeDtypeStruct((bucket_tall, LANES), jnp.float32),
        ],
        scratch_shapes=[
            pltpu.VMEM((2, rows, hidden), jnp.float32),
            pltpu.VMEM((2, rows, hidden), jnp.bfloat16),
            pltpu.SemaphoreType.DMA((2, 2, len(pieces(rows, True)))),
            pltpu.SemaphoreType.DMA(()),
        ],
        compiler_params=pltpu.CompilerParams(vmem_limit_bytes=40 * MIB),
        name="update_and_error",
    )(parts, inverse, arrived, halves, share)


def on_device(grads, error, q_start, bucket):
    replicas = lax.axis_size("dp")
    rows = grads.shape[1]
    rank = q_start.shape[1]
    bucket = bucket.reshape(replicas, -1, LANES)
    tall = rows // replicas * rank // LANES
    halves, share = first_share(grads[0], error[0], q_start.T, replicas)
    for step in range(ITERS):
        if step > 0:
            share = jnp.sum(exchange(outgoing).astype(jnp.float32), axis=0)
        share = share / replicas
        factor_p = everywhere(share[:tall].astype(jnp.bfloat16), replicas)
        term, *inverse = right(factor_p, halves, rank, step + 1 == ITERS)
        parts = addends(term, replicas)
        if step + 1 < ITERS:
            outgoing = left(parts, halves, bucket, turn(parts[0]))
    update, new_error, bucket_mean = last(
        parts, inverse[0], factor_p, halves, share, replicas, bucket.shape[1]
    )
    return (update, new_error[None], bucket_mean.reshape(-1))


def solution(mesh):
    return jax.shard_map(
        on_device,
        mesh=mesh,
        in_specs=(
            P("dp", None, "expert"),
            P("dp", None, "expert"),
            P("expert", None),
            P("dp", "expert"),
        ),
        out_specs=(P(None, "expert"), P("dp", None, "expert"), P(("expert", "dp"))),
        check_vma=False,
    )
```

```python
import functools

import jax
import jax.numpy as jnp
from jax import lax
from jax.experimental import pallas as pl
from jax.experimental.pallas import tpu as pltpu
from jax.sharding import PartitionSpec as P

ITERS = 2
LANES = 128
SUBLANES = 8
MIB = 1024 * 1024
CONTRACT_FIRST = (((0,), (0,)), ((), ()))
CONTRACT_LAST = (((1,), (1,)), ((), ()))


def exchange(chunks):
    return lax.all_to_all(chunks, "dp", split_axis=0, concat_axis=0, tiled=True)


def everywhere(share, size):
    return exchange(jnp.broadcast_to(share, (size,) + share.shape))


def three_parts(value):
    high = value.astype(jnp.bfloat16)
    rest = value - high.astype(jnp.float32)
    middle = rest.astype(jnp.bfloat16)
    low = (rest - middle.astype(jnp.float32)).astype(jnp.bfloat16)
    return high, middle, low


def pieces(rows, grow):
    sizes = [4 * LANES] * (rows // (4 * LANES))
    if grow:
        sizes[:1] = [LANES, LANES, 2 * LANES]
    return [(sum(sizes[:i]), size) for i, size in enumerate(sizes)]


def store_tiles(chunk, value):
    rank, columns = value.shape
    for tile in range(columns // LANES):
        chunk[tile * rank : (tile + 1) * rank, :] = value[:, tile * LANES : (tile + 1) * LANES]


def first_kernel(replicas, flip, grads, error, q_start, compensated, outgoing, *scratch):
    landed, q_landed, sems, q_sem = scratch
    fetch_q = pltpu.make_async_copy(q_start, q_landed, q_sem)
    fetch_q.start()
    me = lax.axis_index("dp")
    half = replicas // 2
    block = grads.shape[0] // replicas
    starts, copies = [], []
    for k in range(half):
        starts.append(pl.multiple_of(((me >> 1) ^ k) * block, block))
        there = pl.multiple_of(((me & 1) ^ flip) * (half * block) + starts[k], block)
        for j, array in enumerate((grads, error)):
            copies.append(
                pltpu.make_async_copy(
                    array.at[pl.ds(there, block)], landed.at[j, k], sems.at[j, k]
                )
            )
            copies[-1].start(priority=j)
    fetch_q.wait()
    q_half = q_landed[...].astype(jnp.bfloat16)
    for k in range(half):
        copies[2 * k].wait()
        copies[2 * k + 1].wait()
        value = (landed[0, k].astype(jnp.float32) + landed[1, k].astype(jnp.float32)).astype(
            jnp.bfloat16
        )
        compensated[pl.ds(starts[k], block), :] = value
        local_p = lax.dot_general(q_half, value, CONTRACT_LAST, preferred_element_type=jnp.float32)
        store_tiles(outgoing.at[k], local_p.astype(jnp.bfloat16))


def first(grads, error, q_start, replicas, flip):
    rows, hidden = grads.shape
    rank = q_start.shape[0]
    block = rows // replicas
    half = replicas // 2
    return pl.pallas_call(
        functools.partial(first_kernel, replicas, flip),
        in_specs=[pl.BlockSpec(memory_space=pl.ANY)] * 3,
        out_specs=[pl.BlockSpec(memory_space=pltpu.VMEM)] * 2,
        out_shape=[
            pltpu.VMEM((half * block, hidden), jnp.bfloat16),
            pltpu.VMEM((half, block // LANES * rank, LANES), jnp.bfloat16),
        ],
        scratch_shapes=[
            pltpu.VMEM((2, half, block, hidden), jnp.bfloat16),
            pltpu.VMEM(q_start.shape, jnp.float32),
            pltpu.SemaphoreType.DMA((2, half)),
            pltpu.SemaphoreType.DMA(()),
        ],
        compiler_params=pltpu.CompilerParams(vmem_limit_bytes=53 * MIB),
        cost_estimate=pl.CostEstimate(
            flops=rows * hidden * rank, bytes_accessed=2 * rows * hidden, transcendentals=0
        ),
        name="compensate_and_left",
    )(grads, error, q_start)


def partner(value, by, size):
    return lax.ppermute(value, "dp", [(i, i ^ by) for i in range(size)])


def first_share(grads, error, q_start, replicas):
    other, theirs = first(grads, error, q_start, replicas, 1)
    arrived = partner(theirs, 1, replicas)
    own, mine = first(grads, error, q_start, replicas, 0)
    pairs = [
        arrived[k].astype(jnp.float32) + mine[k].astype(jnp.float32) for k in range(replicas // 2)
    ]
    total = pairs[0]
    for value in [
        partner(pairs[k].astype(jnp.bfloat16), 2 * k, replicas) for k in range(1, replicas // 2)
    ]:
        total = total + value.astype(jnp.float32)
    return (own, other), total


def inverse_lower(gram):
    rank = gram.shape[0]
    row = lax.broadcasted_iota(jnp.int32, (SUBLANES, 2 * rank), 0)
    across = lax.broadcasted_iota(jnp.int32, (SUBLANES, 2 * rank), 1)
    both = jnp.concatenate([jnp.zeros((rank, rank), jnp.float32), gram], axis=1)
    starts = range(0, rank, SUBLANES)
    tiles = [
        jnp.where(across == row + at, 1.0, both[at : at + SUBLANES, :]) for at in starts
    ]
    inverse = []
    for top, base in enumerate(starts):
        columns = [
            [
                jnp.broadcast_to(tile[:, rank + k : rank + k + 1], tile.shape)
                for tile in tiles[top:]
            ]
            for k in range(base, base + SUBLANES)
        ]
        for j in range(SUBLANES):
            head = columns[j][0]
            reciprocal = 1.0 / head[j : j + 1, :]
            pivot_row = tiles[top][j : j + 1, :]
            for at in range(len(columns[j])):
                factor = columns[j][at] * reciprocal
                if at == 0:
                    factor = jnp.where(row > j, factor, 0.0)
                for i in range(j + 1, SUBLANES):
                    columns[i][at] = columns[i][at] - factor * head[i : i + 1, :]
                tiles[top + at] = tiles[top + at] - factor * pivot_row
        done = tiles[top]
        pivots = jnp.sum(
            jnp.where(across == row + (rank + base), done, 0.0), axis=1, keepdims=True
        )
        inverse.append(done[:, :rank] * lax.rsqrt(pivots))
    return jnp.concatenate(inverse, axis=0)


def columns_of(arrived, tiles, x, first_tile, count):
    rank = arrived.shape[1] // tiles
    parts = []
    for at in range(first_tile, first_tile + count):
        block, tile = divmod(at, tiles)
        parts.append(arrived[2 * block + x, tile * rank : (tile + 1) * rank, :])
    return jnp.concatenate(parts, axis=1)


def right_kernel(tiles, arrived, halves, term, inverse_out=None):
    x = lax.axis_index("dp") & 1
    count = arrived.shape[0] // 2 * tiles
    factors = [columns_of(arrived, tiles, x ^ flip, 0, count) for flip in range(2)]
    factor_p = jnp.concatenate(factors, axis=1)
    gram = lax.dot_general(
        factor_p, factor_p, CONTRACT_LAST, preferred_element_type=jnp.float32
    )
    product = sum(
        jnp.dot(factor, half[...], preferred_element_type=jnp.float32)
        for factor, half in zip(factors, halves)
    )
    inverse = inverse_lower(gram)
    if inverse_out is not None:
        inverse_out[...] = inverse
    term[...] = jnp.dot(
        inverse, product, precision=lax.Precision.HIGHEST, preferred_element_type=jnp.float32
    ).astype(jnp.bfloat16)


def right(arrived, halves, rank, keep):
    out_shape = [pltpu.VMEM((rank, halves[0].shape[1]), jnp.bfloat16)]
    in_vmem = pl.BlockSpec(memory_space=pltpu.VMEM)
    if keep:
        out_shape.append(pltpu.VMEM((rank, rank), jnp.float32))
    return pl.pallas_call(
        functools.partial(right_kernel, arrived.shape[1] // rank),
        in_specs=[in_vmem, (in_vmem, in_vmem)],
        out_specs=[in_vmem] * len(out_shape),
        out_shape=out_shape,
        compiler_params=pltpu.CompilerParams(vmem_limit_bytes=24 * MIB),
        name="orthogonalize_and_right",
    )(arrived, halves)


def addends(term, size):
    one, two, three, four = [
        part.astype(jnp.float32) for part in [term] + [partner(term, by, size) for by in (1, 2, 3)]
    ]
    term = ((one + two) + (three + four)).astype(jnp.bfloat16)
    step = 4
    while 2 * step < size:
        term = (term.astype(jnp.float32) + partner(term, step, size).astype(jnp.float32)).astype(
            jnp.bfloat16
        )
        step *= 2
    return [term, partner(term, step, size)]


def turn(term):
    experts = lax.axis_size("expert")
    size = lax.axis_size("dp") * experts
    return lax.ppermute(
        term[:16, :LANES], ("dp", "expert"), [(i, i ^ experts) for i in range(1, size, 2)]
    )


def sum_of(parts):
    one, two = [part[...].astype(jnp.float32) for part in parts]
    return one + two


def left_kernel(parts, halves, bucket, token, outgoing, landed, sem):
    replicas = outgoing.shape[0]
    block = 2 * halves[0].shape[0] // replicas
    x = lax.axis_index("dp") & 1
    fetch = pltpu.make_async_copy(bucket, landed, sem)
    fetch.start()
    factor_q = sum_of(parts) / replicas
    norm = jnp.sqrt(jnp.sum(factor_q * factor_q, axis=1, keepdims=True) + 1e-06)
    q_half = factor_q.astype(jnp.bfloat16)
    for flip, half in enumerate(halves):
        for j in range(replicas // 2):
            local_p = lax.dot_general(
                q_half,
                half[j * block : (j + 1) * block, :],
                CONTRACT_LAST,
                preferred_element_type=jnp.float32,
            )
            store_tiles(outgoing.at[2 * j + (x ^ flip)], (local_p / norm).astype(jnp.bfloat16))
    fetch.wait()
    outgoing[:, -bucket.shape[1] :, :] = landed[...].astype(jnp.bfloat16)


def left(parts, halves, bucket, token):
    replicas = bucket.shape[0]
    tall = 2 * halves[0].shape[0] // replicas * parts[0].shape[0] // LANES + bucket.shape[1]
    in_vmem = pl.BlockSpec(memory_space=pltpu.VMEM)
    return pl.pallas_call(
        left_kernel,
        in_specs=[
            [in_vmem] * len(parts),
            (in_vmem, in_vmem),
            pl.BlockSpec(memory_space=pl.ANY),
            in_vmem,
        ],
        out_specs=in_vmem,
        out_shape=pltpu.VMEM((replicas, tall, LANES), jnp.bfloat16),
        scratch_shapes=[pltpu.VMEM(bucket.shape, jnp.float32), pltpu.SemaphoreType.DMA(())],
        compiler_params=pltpu.CompilerParams(vmem_limit_bytes=24 * MIB),
        name="normalize_and_left",
    )(parts, halves, bucket, token)


def last_kernel(
    replicas, parts, inverse, arrived, halves, share,
    update, new_error, bucket_mean, update_held, error_held, sems, bucket_sem,
):
    tall = bucket_mean.shape[0]
    there = pl.ds(share.shape[0] - tall, tall)
    copies = [pltpu.make_async_copy(share.at[there], bucket_mean, bucket_sem)]
    copies[0].start()
    rows, hidden = halves[0].shape
    tiles = 2 * rows // replicas // LANES
    x = lax.axis_index("dp") & 1
    right = lax.dot_general(
        inverse[...],
        sum_of(parts) / replicas,
        CONTRACT_FIRST,
        precision=lax.Precision.HIGHEST,
        preferred_element_type=jnp.float32,
    )
    right = jnp.concatenate(three_parts(right), axis=0)
    for flip, half in enumerate(halves):
        for i, (at, size) in enumerate(pieces(rows, flip == 0)):
            where = slice(at, at + size)
            p_block = columns_of(arrived, tiles, x ^ flip, at // LANES, size // LANES).T
            block = jnp.dot(
                jnp.concatenate([p_block] * 3, axis=1), right, preferred_element_type=jnp.float32
            )
            update_held[flip, where, :] = block
            error_held[flip, where, :] = (half[where, :].astype(jnp.float32) - block).astype(
                jnp.bfloat16
            )
            there = pl.ds(pl.multiple_of((x ^ flip) * rows + at, LANES), size)
            for j, (held, out) in enumerate(((update_held, update), (error_held, new_error))):
                copies.append(
                    pltpu.make_async_copy(
                        held.at[flip, pl.ds(at, size)], out.at[there], sems.at[j, flip, i]
                    )
                )
                copies[-1].start(priority=j)
    for copy in copies:
        copy.wait()


def last(parts, inverse, arrived, halves, share, replicas, bucket_tall):
    rows, hidden = halves[0].shape
    in_vmem = pl.BlockSpec(memory_space=pltpu.VMEM)
    return pl.pallas_call(
        functools.partial(last_kernel, replicas),
        in_specs=[[in_vmem] * len(parts), in_vmem, in_vmem, (in_vmem, in_vmem), in_vmem],
        out_specs=[pl.BlockSpec(memory_space=pl.ANY)] * 3,
        out_shape=[
            jax.ShapeDtypeStruct((2 * rows, hidden), jnp.float32),
            jax.ShapeDtypeStruct((2 * rows, hidden), jnp.bfloat16),
            jax.ShapeDtypeStruct((bucket_tall, LANES), jnp.float32),
        ],
        scratch_shapes=[
            pltpu.VMEM((2, rows, hidden), jnp.float32),
            pltpu.VMEM((2, rows, hidden), jnp.bfloat16),
            pltpu.SemaphoreType.DMA((2, 2, len(pieces(rows, True)))),
            pltpu.SemaphoreType.DMA(()),
        ],
        compiler_params=pltpu.CompilerParams(vmem_limit_bytes=40 * MIB),
        name="update_and_error",
    )(parts, inverse, arrived, halves, share)


def on_device(grads, error, q_start, bucket):
    replicas = lax.axis_size("dp")
    rows = grads.shape[1]
    rank = q_start.shape[1]
    bucket = bucket.reshape(replicas, -1, LANES)
    tall = rows // replicas * rank // LANES
    halves, share = first_share(grads[0], error[0], q_start.T, replicas)
    for step in range(ITERS):
        if step > 0:
            share = jnp.sum(exchange(outgoing).astype(jnp.float32), axis=0)
        share = share / replicas
        factor_p = everywhere(share[:tall].astype(jnp.bfloat16), replicas)
        term, *inverse = right(factor_p, halves, rank, step + 1 == ITERS)
        parts = addends(term, replicas)
        if step + 1 < ITERS:
            outgoing = left(parts, halves, bucket, turn(parts[1]))
    update, new_error, bucket_mean = last(
        parts, inverse[0], factor_p, halves, share, replicas, bucket.shape[1]
    )
    return (update, new_error[None], bucket_mean.reshape(-1))


def solution(mesh):
    return jax.shard_map(
        on_device,
        mesh=mesh,
        in_specs=(
            P("dp", None, "expert"),
            P("dp", None, "expert"),
            P("expert", None),
            P("dp", "expert"),
        ),
        out_specs=(P(None, "expert"), P("dp", None, "expert"), P(("expert", "dp"))),
        check_vma=False,
    )
```

```python
import functools

import jax
import jax.numpy as jnp
from jax import lax
from jax.experimental import pallas as pl
from jax.experimental.pallas import tpu as pltpu
from jax.sharding import PartitionSpec as P

ITERS = 2
LANES = 128
SUBLANES = 8
MIB = 1024 * 1024
CONTRACT_FIRST = (((0,), (0,)), ((), ()))
CONTRACT_LAST = (((1,), (1,)), ((), ()))


def exchange(chunks):
    return lax.all_to_all(chunks, "dp", split_axis=0, concat_axis=0, tiled=True)


def everywhere(share, size):
    return exchange(jnp.broadcast_to(share, (size,) + share.shape))


def three_parts(value):
    high = value.astype(jnp.bfloat16)
    rest = value - high.astype(jnp.float32)
    middle = rest.astype(jnp.bfloat16)
    low = (rest - middle.astype(jnp.float32)).astype(jnp.bfloat16)
    return high, middle, low


def pieces(rows, grow):
    sizes = [4 * LANES] * (rows // (4 * LANES))
    if grow:
        sizes[:1] = [LANES, LANES, 2 * LANES]
    return [(sum(sizes[:i]), size) for i, size in enumerate(sizes)]


def store_tiles(chunk, value):
    rank, columns = value.shape
    for tile in range(columns // LANES):
        chunk[tile * rank : (tile + 1) * rank, :] = value[:, tile * LANES : (tile + 1) * LANES]


def first_kernel(replicas, flip, grads, error, q_start, compensated, outgoing, *scratch):
    landed, q_landed, sems, q_sem = scratch
    fetch_q = pltpu.make_async_copy(q_start, q_landed, q_sem)
    fetch_q.start()
    me = lax.axis_index("dp")
    half = replicas // 2
    block = grads.shape[0] // replicas
    starts, copies = [], []
    for k in range(half):
        starts.append(pl.multiple_of(((me >> 1) ^ k) * block, block))
        there = pl.multiple_of(((me & 1) ^ flip) * (half * block) + starts[k], block)
        for j, array in enumerate((grads, error)):
            copies.append(
                pltpu.make_async_copy(
                    array.at[pl.ds(there, block)], landed.at[j, k], sems.at[j, k]
                )
            )
            copies[-1].start(priority=j)
    fetch_q.wait()
    q_half = q_landed[...].astype(jnp.bfloat16)
    for k in range(half):
        copies[2 * k].wait()
        copies[2 * k + 1].wait()
        value = (landed[0, k].astype(jnp.float32) + landed[1, k].astype(jnp.float32)).astype(
            jnp.bfloat16
        )
        compensated[pl.ds(starts[k], block), :] = value
        local_p = lax.dot_general(q_half, value, CONTRACT_LAST, preferred_element_type=jnp.float32)
        store_tiles(outgoing.at[k], local_p.astype(jnp.bfloat16))


def first(grads, error, q_start, replicas, flip):
    rows, hidden = grads.shape
    rank = q_start.shape[0]
    block = rows // replicas
    half = replicas // 2
    return pl.pallas_call(
        functools.partial(first_kernel, replicas, flip),
        in_specs=[pl.BlockSpec(memory_space=pl.ANY)] * 3,
        out_specs=[pl.BlockSpec(memory_space=pltpu.VMEM)] * 2,
        out_shape=[
            pltpu.VMEM((half * block, hidden), jnp.bfloat16),
            pltpu.VMEM((half, block // LANES * rank, LANES), jnp.bfloat16),
        ],
        scratch_shapes=[
            pltpu.VMEM((2, half, block, hidden), jnp.bfloat16),
            pltpu.VMEM(q_start.shape, jnp.float32),
            pltpu.SemaphoreType.DMA((2, half)),
            pltpu.SemaphoreType.DMA(()),
        ],
        compiler_params=pltpu.CompilerParams(vmem_limit_bytes=53 * MIB),
        cost_estimate=pl.CostEstimate(
            flops=rows * hidden * rank, bytes_accessed=2 * rows * hidden, transcendentals=0
        ),
        name="compensate_and_left",
    )(grads, error, q_start)


def partner(value, by, size):
    return lax.ppermute(value, "dp", [(i, i ^ by) for i in range(size)])


def first_share(grads, error, q_start, replicas):
    other, theirs = first(grads, error, q_start, replicas, 1)
    arrived = partner(theirs, 1, replicas)
    own, mine = first(grads, error, q_start, replicas, 0)
    pairs = [
        arrived[k].astype(jnp.float32) + mine[k].astype(jnp.float32) for k in range(replicas // 2)
    ]
    total = pairs[0]
    for value in [
        partner(pairs[k].astype(jnp.bfloat16), 2 * k, replicas) for k in range(1, replicas // 2)
    ]:
        total = total + value.astype(jnp.float32)
    return (own, other), total


def inverse_lower(gram):
    rank = gram.shape[0]
    row = lax.broadcasted_iota(jnp.int32, (SUBLANES, 2 * rank), 0)
    across = lax.broadcasted_iota(jnp.int32, (SUBLANES, 2 * rank), 1)
    both = jnp.concatenate([jnp.zeros((rank, rank), jnp.float32), gram], axis=1)
    starts = range(0, rank, SUBLANES)
    tiles = [
        jnp.where(across == row + at, 1.0, both[at : at + SUBLANES, :]) for at in starts
    ]
    inverse = []
    for top, base in enumerate(starts):
        columns = [
            [
                jnp.broadcast_to(tile[:, rank + k : rank + k + 1], tile.shape)
                for tile in tiles[top:]
            ]
            for k in range(base, base + SUBLANES)
        ]
        for j in range(SUBLANES):
            head = columns[j][0]
            reciprocal = 1.0 / head[j : j + 1, :]
            pivot_row = tiles[top][j : j + 1, :]
            for at in range(len(columns[j])):
                factor = columns[j][at] * reciprocal
                if at == 0:
                    factor = jnp.where(row > j, factor, 0.0)
                for i in range(j + 1, SUBLANES):
                    columns[i][at] = columns[i][at] - factor * head[i : i + 1, :]
                tiles[top + at] = tiles[top + at] - factor * pivot_row
        done = tiles[top]
        pivots = jnp.sum(
            jnp.where(across == row + (rank + base), done, 0.0), axis=1, keepdims=True
        )
        inverse.append(done[:, :rank] * lax.rsqrt(pivots))
    return jnp.concatenate(inverse, axis=0)


def columns_of(arrived, tiles, x, first_tile, count):
    rank = arrived.shape[1] // tiles
    parts = []
    for at in range(first_tile, first_tile + count):
        block, tile = divmod(at, tiles)
        parts.append(arrived[2 * block + x, tile * rank : (tile + 1) * rank, :])
    return jnp.concatenate(parts, axis=1)


def right_kernel(tiles, arrived, halves, term, inverse_out=None):
    x = lax.axis_index("dp") & 1
    count = arrived.shape[0] // 2 * tiles
    factors = [columns_of(arrived, tiles, x ^ flip, 0, count) for flip in range(2)]
    factor_p = jnp.concatenate(factors, axis=1)
    gram = lax.dot_general(
        factor_p, factor_p, CONTRACT_LAST, preferred_element_type=jnp.float32
    )
    product = sum(
        jnp.dot(factor, half[...], preferred_element_type=jnp.float32)
        for factor, half in zip(factors, halves)
    )
    inverse = inverse_lower(gram)
    if inverse_out is not None:
        inverse_out[...] = inverse
    term[...] = jnp.dot(
        inverse, product, precision=lax.Precision.HIGHEST, preferred_element_type=jnp.float32
    ).astype(jnp.bfloat16)


def right(arrived, halves, rank, keep):
    out_shape = [pltpu.VMEM((rank, halves[0].shape[1]), jnp.bfloat16)]
    in_vmem = pl.BlockSpec(memory_space=pltpu.VMEM)
    if keep:
        out_shape.append(pltpu.VMEM((rank, rank), jnp.float32))
    return pl.pallas_call(
        functools.partial(right_kernel, arrived.shape[1] // rank),
        in_specs=[in_vmem, (in_vmem, in_vmem)],
        out_specs=[in_vmem] * len(out_shape),
        out_shape=out_shape,
        compiler_params=pltpu.CompilerParams(vmem_limit_bytes=24 * MIB),
        name="orthogonalize_and_right",
    )(arrived, halves)


def last_partner(value, step, size, detour):
    experts = lax.axis_size("expert")
    pairs = []
    for i in range(size):
        for e in range(experts):
            other = i ^ (step ^ 2 if detour and e % 2 else step)
            pairs.append((i * experts + e, other * experts + e))
    return lax.ppermute(value, ("dp", "expert"), pairs)


def addends(term, size, detour):
    one, two, three, four = [
        part.astype(jnp.float32) for part in [term] + [partner(term, by, size) for by in (1, 2, 3)]
    ]
    term = ((one + two) + (three + four)).astype(jnp.bfloat16)
    step = 4
    while 2 * step < size:
        term = (term.astype(jnp.float32) + partner(term, step, size).astype(jnp.float32)).astype(
            jnp.bfloat16
        )
        step *= 2
    return [term, last_partner(term, step, size, detour)]


def sum_of(parts):
    one, two = [part[...].astype(jnp.float32) for part in parts]
    return one + two


def left_kernel(parts, halves, bucket, outgoing, landed, sem):
    replicas = outgoing.shape[0]
    block = 2 * halves[0].shape[0] // replicas
    x = lax.axis_index("dp") & 1
    fetch = pltpu.make_async_copy(bucket, landed, sem)
    fetch.start()
    factor_q = sum_of(parts) / replicas
    norm = jnp.sqrt(jnp.sum(factor_q * factor_q, axis=1, keepdims=True) + 1e-06)
    q_half = factor_q.astype(jnp.bfloat16)
    for flip, half in enumerate(halves):
        for j in range(replicas // 2):
            local_p = lax.dot_general(
                q_half,
                half[j * block : (j + 1) * block, :],
                CONTRACT_LAST,
                preferred_element_type=jnp.float32,
            )
            store_tiles(outgoing.at[2 * j + (x ^ flip)], (local_p / norm).astype(jnp.bfloat16))
    fetch.wait()
    outgoing[:, -bucket.shape[1] :, :] = landed[...].astype(jnp.bfloat16)


def left(parts, halves, bucket):
    replicas = bucket.shape[0]
    tall = 2 * halves[0].shape[0] // replicas * parts[0].shape[0] // LANES + bucket.shape[1]
    in_vmem = pl.BlockSpec(memory_space=pltpu.VMEM)
    return pl.pallas_call(
        left_kernel,
        in_specs=[[in_vmem] * len(parts), (in_vmem, in_vmem), pl.BlockSpec(memory_space=pl.ANY)],
        out_specs=in_vmem,
        out_shape=pltpu.VMEM((replicas, tall, LANES), jnp.bfloat16),
        scratch_shapes=[pltpu.VMEM(bucket.shape, jnp.float32), pltpu.SemaphoreType.DMA(())],
        compiler_params=pltpu.CompilerParams(vmem_limit_bytes=24 * MIB),
        name="normalize_and_left",
    )(parts, halves, bucket)


def last_kernel(
    replicas, parts, inverse, arrived, halves, share,
    update, new_error, bucket_mean, update_held, error_held, sems, bucket_sem,
):
    tall = bucket_mean.shape[0]
    there = pl.ds(share.shape[0] - tall, tall)
    copies = [pltpu.make_async_copy(share.at[there], bucket_mean, bucket_sem)]
    copies[0].start()
    rows, hidden = halves[0].shape
    tiles = 2 * rows // replicas // LANES
    x = lax.axis_index("dp") & 1
    right = lax.dot_general(
        inverse[...],
        sum_of(parts) / replicas,
        CONTRACT_FIRST,
        precision=lax.Precision.HIGHEST,
        preferred_element_type=jnp.float32,
    )
    right = jnp.concatenate(three_parts(right), axis=0)
    for flip, half in enumerate(halves):
        for i, (at, size) in enumerate(pieces(rows, flip == 0)):
            where = slice(at, at + size)
            p_block = columns_of(arrived, tiles, x ^ flip, at // LANES, size // LANES).T
            block = jnp.dot(
                jnp.concatenate([p_block] * 3, axis=1), right, preferred_element_type=jnp.float32
            )
            update_held[flip, where, :] = block
            error_held[flip, where, :] = (half[where, :].astype(jnp.float32) - block).astype(
                jnp.bfloat16
            )
            there = pl.ds(pl.multiple_of((x ^ flip) * rows + at, LANES), size)
            for j, (held, out) in enumerate(((update_held, update), (error_held, new_error))):
                copies.append(
                    pltpu.make_async_copy(
                        held.at[flip, pl.ds(at, size)], out.at[there], sems.at[j, flip, i]
                    )
                )
                copies[-1].start(priority=j)
    for copy in copies:
        copy.wait()


def last(parts, inverse, arrived, halves, share, replicas, bucket_tall):
    rows, hidden = halves[0].shape
    in_vmem = pl.BlockSpec(memory_space=pltpu.VMEM)
    return pl.pallas_call(
        functools.partial(last_kernel, replicas),
        in_specs=[[in_vmem] * len(parts), in_vmem, in_vmem, (in_vmem, in_vmem), in_vmem],
        out_specs=[pl.BlockSpec(memory_space=pl.ANY)] * 3,
        out_shape=[
            jax.ShapeDtypeStruct((2 * rows, hidden), jnp.float32),
            jax.ShapeDtypeStruct((2 * rows, hidden), jnp.bfloat16),
            jax.ShapeDtypeStruct((bucket_tall, LANES), jnp.float32),
        ],
        scratch_shapes=[
            pltpu.VMEM((2, rows, hidden), jnp.float32),
            pltpu.VMEM((2, rows, hidden), jnp.bfloat16),
            pltpu.SemaphoreType.DMA((2, 2, len(pieces(rows, True)))),
            pltpu.SemaphoreType.DMA(()),
        ],
        compiler_params=pltpu.CompilerParams(vmem_limit_bytes=40 * MIB),
        name="update_and_error",
    )(parts, inverse, arrived, halves, share)


def on_device(grads, error, q_start, bucket):
    replicas = lax.axis_size("dp")
    rows = grads.shape[1]
    rank = q_start.shape[1]
    bucket = bucket.reshape(replicas, -1, LANES)
    tall = rows // replicas * rank // LANES
    halves, share = first_share(grads[0], error[0], q_start.T, replicas)
    for step in range(ITERS):
        if step > 0:
            share = jnp.sum(exchange(outgoing).astype(jnp.float32), axis=0)
        share = share / replicas
        factor_p = everywhere(share[:tall].astype(jnp.bfloat16), replicas)
        term, *inverse = right(factor_p, halves, rank, step + 1 == ITERS)
        parts = addends(term, replicas, step + 1 < ITERS)
        if step + 1 < ITERS:
            outgoing = left(parts, halves, bucket)
    update, new_error, bucket_mean = last(
        parts, inverse[0], factor_p, halves, share, replicas, bucket.shape[1]
    )
    return (update, new_error[None], bucket_mean.reshape(-1))


def solution(mesh):
    return jax.shard_map(
        on_device,
        mesh=mesh,
        in_specs=(
            P("dp", None, "expert"),
            P("dp", None, "expert"),
            P("expert", None),
            P("dp", "expert"),
        ),
        out_specs=(P(None, "expert"), P("dp", None, "expert"), P(("expert", "dp"))),
        check_vma=False,
    )
```

```python
import functools

import jax
import jax.numpy as jnp
from jax import lax
from jax.experimental import pallas as pl
from jax.experimental.pallas import tpu as pltpu
from jax.sharding import PartitionSpec as P

ITERS = 2
LANES = 128
SUBLANES = 8
MIB = 1024 * 1024
CONTRACT_LAST = (((1,), (1,)), ((), ()))


def exchange(chunks):
    return lax.all_to_all(chunks, "dp", split_axis=0, concat_axis=0, tiled=True)


def everywhere(share, size):
    return exchange(jnp.broadcast_to(share, (size,) + share.shape))


def three_parts(value):
    high = value.astype(jnp.bfloat16)
    rest = value - high.astype(jnp.float32)
    middle = rest.astype(jnp.bfloat16)
    low = (rest - middle.astype(jnp.float32)).astype(jnp.bfloat16)
    return high, middle, low


def pieces(rows, grow):
    sizes = [4 * LANES] * (rows // (4 * LANES))
    if grow:
        sizes[:1] = [LANES, LANES, 2 * LANES]
    return [(sum(sizes[:i]), size) for i, size in enumerate(sizes)]


def store_tiles(chunk, value):
    rank, columns = value.shape
    for tile in range(columns // LANES):
        chunk[tile * rank : (tile + 1) * rank, :] = value[:, tile * LANES : (tile + 1) * LANES]


def fine_product(left, right, axis):
    lh, lm, ll = three_parts(left)
    rh, rm, rl = three_parts(right)
    return lax.dot_general(
        jnp.concatenate([lh, lm, ll, lh, lm, lh], axis=axis),
        jnp.concatenate([rh, rh, rh, rm, rm, rl], axis=0),
        (((axis,), (0,)), ((), ())),
        preferred_element_type=jnp.float32,
    )


def first_kernel(replicas, flip, grads, error, q_start, compensated, outgoing, *scratch):
    landed, q_landed, sems, q_sem = scratch
    fetch_q = pltpu.make_async_copy(q_start, q_landed, q_sem)
    fetch_q.start()
    me = lax.axis_index("dp")
    half = replicas // 2
    block = grads.shape[0] // replicas
    starts, copies = [], []
    for k in range(half):
        starts.append(pl.multiple_of(((me >> 1) ^ k) * block, block))
        there = pl.multiple_of(((me & 1) ^ flip) * (half * block) + starts[k], block)
        for j, array in enumerate((grads, error)):
            copies.append(
                pltpu.make_async_copy(
                    array.at[pl.ds(there, block)], landed.at[j, k], sems.at[j, k]
                )
            )
            copies[-1].start(priority=j)
    fetch_q.wait()
    q_half = q_landed[...].astype(jnp.bfloat16)
    for k in range(half):
        copies[2 * k].wait()
        copies[2 * k + 1].wait()
        value = (landed[0, k].astype(jnp.float32) + landed[1, k].astype(jnp.float32)).astype(
            jnp.bfloat16
        )
        compensated[pl.ds(starts[k], block), :] = value
        local_p = lax.dot_general(q_half, value, CONTRACT_LAST, preferred_element_type=jnp.float32)
        store_tiles(outgoing.at[k], local_p.astype(jnp.bfloat16))


def first(grads, error, q_start, replicas, flip):
    rows, hidden = grads.shape
    rank = q_start.shape[0]
    block = rows // replicas
    half = replicas // 2
    return pl.pallas_call(
        functools.partial(first_kernel, replicas, flip),
        in_specs=[pl.BlockSpec(memory_space=pl.ANY)] * 3,
        out_specs=[pl.BlockSpec(memory_space=pltpu.VMEM)] * 2,
        out_shape=[
            pltpu.VMEM((half * block, hidden), jnp.bfloat16),
            pltpu.VMEM((half, block // LANES * rank, LANES), jnp.bfloat16),
        ],
        scratch_shapes=[
            pltpu.VMEM((2, half, block, hidden), jnp.bfloat16),
            pltpu.VMEM(q_start.shape, jnp.float32),
            pltpu.SemaphoreType.DMA((2, half)),
            pltpu.SemaphoreType.DMA(()),
        ],
        compiler_params=pltpu.CompilerParams(vmem_limit_bytes=53 * MIB),
        cost_estimate=pl.CostEstimate(
            flops=rows * hidden * rank, bytes_accessed=2 * rows * hidden, transcendentals=0
        ),
        name="compensate_and_left",
    )(grads, error, q_start)


def partner(value, by, size):
    return lax.ppermute(value, "dp", [(i, i ^ by) for i in range(size)])


def first_share(grads, error, q_start, replicas):
    other, theirs = first(grads, error, q_start, replicas, 1)
    arrived = partner(theirs, 1, replicas)
    own, mine = first(grads, error, q_start, replicas, 0)
    pairs = [
        arrived[k].astype(jnp.float32) + mine[k].astype(jnp.float32) for k in range(replicas // 2)
    ]
    total = pairs[0]
    for value in [
        partner(pairs[k].astype(jnp.bfloat16), 2 * k, replicas) for k in range(1, replicas // 2)
    ]:
        total = total + value.astype(jnp.float32)
    return (own, other), total


def inverse_lower(gram):
    rank = gram.shape[0]
    row = lax.broadcasted_iota(jnp.int32, (SUBLANES, 2 * rank), 0)
    across = lax.broadcasted_iota(jnp.int32, (SUBLANES, 2 * rank), 1)
    both = jnp.concatenate([jnp.zeros((rank, rank), jnp.float32), gram], axis=1)
    starts = range(0, rank, SUBLANES)
    tiles = [
        jnp.where(across == row + at, 1.0, both[at : at + SUBLANES, :]) for at in starts
    ]
    inverse = []
    for top, base in enumerate(starts):
        columns = [
            [
                jnp.broadcast_to(tile[:, rank + k : rank + k + 1], tile.shape)
                for tile in tiles[top:]
            ]
            for k in range(base, base + SUBLANES)
        ]
        for j in range(SUBLANES):
            head = columns[j][0]
            reciprocal = 1.0 / head[j : j + 1, :]
            pivot_row = tiles[top][j : j + 1, :]
            for at in range(len(columns[j])):
                factor = columns[j][at] * reciprocal
                if at == 0:
                    factor = jnp.where(row > j, factor, 0.0)
                for i in range(j + 1, SUBLANES):
                    columns[i][at] = columns[i][at] - factor * head[i : i + 1, :]
                tiles[top + at] = tiles[top + at] - factor * pivot_row
        done = tiles[top]
        pivots = jnp.sum(
            jnp.where(across == row + (rank + base), done, 0.0), axis=1, keepdims=True
        )
        inverse.append(done[:, :rank] * lax.rsqrt(pivots))
    return jnp.concatenate(inverse, axis=0)


def columns_of(arrived, tiles, x, first_tile, count):
    rank = arrived.shape[1] // tiles
    parts = []
    for at in range(first_tile, first_tile + count):
        block, tile = divmod(at, tiles)
        parts.append(arrived[2 * block + x, tile * rank : (tile + 1) * rank, :])
    return jnp.concatenate(parts, axis=1)


def right_kernel(tiles, arrived, halves, term, inverse_out=None):
    x = lax.axis_index("dp") & 1
    count = arrived.shape[0] // 2 * tiles
    factors = [columns_of(arrived, tiles, x ^ flip, 0, count) for flip in range(2)]
    factor_p = jnp.concatenate(factors, axis=1)
    gram = lax.dot_general(
        factor_p, factor_p, CONTRACT_LAST, preferred_element_type=jnp.float32
    )
    product = sum(
        jnp.dot(factor, half[...], preferred_element_type=jnp.float32)
        for factor, half in zip(factors, halves)
    )
    inverse = inverse_lower(gram)
    if inverse_out is not None:
        inverse_out[...] = inverse
    term[...] = fine_product(inverse, product, 1).astype(jnp.bfloat16)


def right(arrived, halves, rank, keep):
    out_shape = [pltpu.VMEM((rank, halves[0].shape[1]), jnp.bfloat16)]
    in_vmem = pl.BlockSpec(memory_space=pltpu.VMEM)
    if keep:
        out_shape.append(pltpu.VMEM((rank, rank), jnp.float32))
    return pl.pallas_call(
        functools.partial(right_kernel, arrived.shape[1] // rank),
        in_specs=[in_vmem, (in_vmem, in_vmem)],
        out_specs=[in_vmem] * len(out_shape),
        out_shape=out_shape,
        compiler_params=pltpu.CompilerParams(vmem_limit_bytes=24 * MIB),
        name="orthogonalize_and_right",
    )(arrived, halves)


def last_partner(value, step, size, detour):
    experts = lax.axis_size("expert")
    pairs = []
    for i in range(size):
        for e in range(experts):
            other = i ^ (step ^ 2 if detour and e % 2 else step)
            pairs.append((i * experts + e, other * experts + e))
    return lax.ppermute(value, ("dp", "expert"), pairs)


def addends(term, size, detour):
    one, two, three, four = [
        part.astype(jnp.float32) for part in [term] + [partner(term, by, size) for by in (1, 2, 3)]
    ]
    term = ((one + two) + (three + four)).astype(jnp.bfloat16)
    step = 4
    while 2 * step < size:
        term = (term.astype(jnp.float32) + partner(term, step, size).astype(jnp.float32)).astype(
            jnp.bfloat16
        )
        step *= 2
    return [term, last_partner(term, step, size, detour)]


def sum_of(parts):
    one, two = [part[...].astype(jnp.float32) for part in parts]
    return one + two


def left_kernel(parts, halves, bucket, outgoing, landed, sem):
    replicas = outgoing.shape[0]
    block = 2 * halves[0].shape[0] // replicas
    x = lax.axis_index("dp") & 1
    fetch = pltpu.make_async_copy(bucket, landed, sem)
    fetch.start()
    factor_q = sum_of(parts) / replicas
    scale = 1.0 / jnp.sqrt(jnp.sum(factor_q * factor_q, axis=1, keepdims=True) + 1e-06)
    q_half = factor_q.astype(jnp.bfloat16)
    for flip, half in enumerate(halves):
        for j in range(replicas // 2):
            local_p = lax.dot_general(
                q_half,
                half[j * block : (j + 1) * block, :],
                CONTRACT_LAST,
                preferred_element_type=jnp.float32,
            )
            store_tiles(outgoing.at[2 * j + (x ^ flip)], (local_p * scale).astype(jnp.bfloat16))
    fetch.wait()
    outgoing[:, -bucket.shape[1] :, :] = landed[...].astype(jnp.bfloat16)


def left(parts, halves, bucket):
    replicas = bucket.shape[0]
    tall = 2 * halves[0].shape[0] // replicas * parts[0].shape[0] // LANES + bucket.shape[1]
    in_vmem = pl.BlockSpec(memory_space=pltpu.VMEM)
    return pl.pallas_call(
        left_kernel,
        in_specs=[[in_vmem] * len(parts), (in_vmem, in_vmem), pl.BlockSpec(memory_space=pl.ANY)],
        out_specs=in_vmem,
        out_shape=pltpu.VMEM((replicas, tall, LANES), jnp.bfloat16),
        scratch_shapes=[pltpu.VMEM(bucket.shape, jnp.float32), pltpu.SemaphoreType.DMA(())],
        compiler_params=pltpu.CompilerParams(vmem_limit_bytes=24 * MIB),
        name="normalize_and_left",
    )(parts, halves, bucket)


def last_kernel(
    replicas, parts, inverse, arrived, halves, share,
    update, new_error, bucket_mean, update_held, error_held, sems, bucket_sem,
):
    tall = bucket_mean.shape[0]
    there = pl.ds(share.shape[0] - tall, tall)
    copies = [pltpu.make_async_copy(share.at[there], bucket_mean, bucket_sem)]
    copies[0].start()
    rows, hidden = halves[0].shape
    tiles = 2 * rows // replicas // LANES
    x = lax.axis_index("dp") & 1
    right = fine_product(inverse[...], sum_of(parts) / replicas, 0)
    right = jnp.concatenate(three_parts(right), axis=0)
    for flip, half in enumerate(halves):
        for i, (at, size) in enumerate(pieces(rows, flip == 0)):
            where = slice(at, at + size)
            p_block = columns_of(arrived, tiles, x ^ flip, at // LANES, size // LANES).T
            block = jnp.dot(
                jnp.concatenate([p_block] * 3, axis=1), right, preferred_element_type=jnp.float32
            )
            update_held[flip, where, :] = block
            error_held[flip, where, :] = (half[where, :].astype(jnp.float32) - block).astype(
                jnp.bfloat16
            )
            there = pl.ds(pl.multiple_of((x ^ flip) * rows + at, LANES), size)
            for j, (held, out) in enumerate(((update_held, update), (error_held, new_error))):
                copies.append(
                    pltpu.make_async_copy(
                        held.at[flip, pl.ds(at, size)], out.at[there], sems.at[j, flip, i]
                    )
                )
                copies[-1].start(priority=j)
    for copy in copies:
        copy.wait()


def last(parts, inverse, arrived, halves, share, replicas, bucket_tall):
    rows, hidden = halves[0].shape
    in_vmem = pl.BlockSpec(memory_space=pltpu.VMEM)
    return pl.pallas_call(
        functools.partial(last_kernel, replicas),
        in_specs=[[in_vmem] * len(parts), in_vmem, in_vmem, (in_vmem, in_vmem), in_vmem],
        out_specs=[pl.BlockSpec(memory_space=pl.ANY)] * 3,
        out_shape=[
            jax.ShapeDtypeStruct((2 * rows, hidden), jnp.float32),
            jax.ShapeDtypeStruct((2 * rows, hidden), jnp.bfloat16),
            jax.ShapeDtypeStruct((bucket_tall, LANES), jnp.float32),
        ],
        scratch_shapes=[
            pltpu.VMEM((2, rows, hidden), jnp.float32),
            pltpu.VMEM((2, rows, hidden), jnp.bfloat16),
            pltpu.SemaphoreType.DMA((2, 2, len(pieces(rows, True)))),
            pltpu.SemaphoreType.DMA(()),
        ],
        compiler_params=pltpu.CompilerParams(vmem_limit_bytes=40 * MIB),
        name="update_and_error",
    )(parts, inverse, arrived, halves, share)


def on_device(grads, error, q_start, bucket):
    replicas = lax.axis_size("dp")
    rows = grads.shape[1]
    rank = q_start.shape[1]
    bucket = bucket.reshape(replicas, -1, LANES)
    tall = rows // replicas * rank // LANES
    halves, share = first_share(grads[0], error[0], q_start.T, replicas)
    for step in range(ITERS):
        if step > 0:
            share = jnp.sum(exchange(outgoing).astype(jnp.float32), axis=0)
        share = share / replicas
        factor_p = everywhere(share[:tall].astype(jnp.bfloat16), replicas)
        term, *inverse = right(factor_p, halves, rank, step + 1 == ITERS)
        parts = addends(term, replicas, step + 1 < ITERS)
        if step + 1 < ITERS:
            outgoing = left(parts, halves, bucket)
    update, new_error, bucket_mean = last(
        parts, inverse[0], factor_p, halves, share, replicas, bucket.shape[1]
    )
    return (update, new_error[None], bucket_mean.reshape(-1))


def solution(mesh):
    return jax.shard_map(
        on_device,
        mesh=mesh,
        in_specs=(
            P("dp", None, "expert"),
            P("dp", None, "expert"),
            P("expert", None),
            P("dp", "expert"),
        ),
        out_specs=(P(None, "expert"), P("dp", None, "expert"), P(("expert", "dp"))),
        check_vma=False,
    )
```

```python
import functools

import jax
import jax.numpy as jnp
from jax import lax
from jax.experimental import pallas as pl
from jax.experimental.pallas import tpu as pltpu
from jax.sharding import PartitionSpec as P

ITERS = 2
LANES = 128
SUBLANES = 8
MIB = 1024 * 1024
CONTRACT_LAST = (((1,), (1,)), ((), ()))


def exchange(chunks):
    return lax.all_to_all(chunks, "dp", split_axis=0, concat_axis=0, tiled=True)


def everywhere(share, size):
    return exchange(jnp.broadcast_to(share, (size,) + share.shape))


def three_parts(value):
    high = value.astype(jnp.bfloat16)
    rest = value - high.astype(jnp.float32)
    middle = rest.astype(jnp.bfloat16)
    low = (rest - middle.astype(jnp.float32)).astype(jnp.bfloat16)
    return high, middle, low


def pieces(rows, grow):
    sizes = [4 * LANES] * (rows // (4 * LANES))
    if grow:
        sizes[:1] = [LANES, LANES, 2 * LANES]
    return [(sum(sizes[:i]), size) for i, size in enumerate(sizes)]


def store_tiles(chunk, value):
    rank, columns = value.shape
    for tile in range(columns // LANES):
        chunk[tile * rank : (tile + 1) * rank, :] = value[:, tile * LANES : (tile + 1) * LANES]


def fine_product(left, right, axis):
    lh, lm, ll = three_parts(left)
    rh, rm, rl = three_parts(right)
    return lax.dot_general(
        jnp.concatenate([lh, lm, ll, lh, lm, lh], axis=axis),
        jnp.concatenate([rh, rh, rh, rm, rm, rl], axis=0),
        (((axis,), (0,)), ((), ())),
        preferred_element_type=jnp.float32,
    )


def first_kernel(replicas, flip, grads, error, q_start, compensated, outgoing, *scratch):
    landed, q_landed, sems, q_sem = scratch
    fetch_q = pltpu.make_async_copy(q_start, q_landed, q_sem)
    fetch_q.start()
    me = lax.axis_index("dp")
    half = replicas // 2
    block = grads.shape[0] // replicas
    starts, copies = [], []
    for k in range(half):
        starts.append(pl.multiple_of(((me >> 1) ^ k) * block, block))
        there = pl.multiple_of(((me & 1) ^ flip) * (half * block) + starts[k], block)
        for j, array in enumerate((grads, error)):
            copies.append(
                pltpu.make_async_copy(
                    array.at[pl.ds(there, block)], landed.at[j, k], sems.at[j, k]
                )
            )
            copies[-1].start(priority=j)
    fetch_q.wait()
    q_half = q_landed[...].astype(jnp.bfloat16)
    for k in range(half):
        copies[2 * k].wait()
        copies[2 * k + 1].wait()
        value = (landed[0, k].astype(jnp.float32) + landed[1, k].astype(jnp.float32)).astype(
            jnp.bfloat16
        )
        compensated[pl.ds(starts[k], block), :] = value
        local_p = lax.dot_general(q_half, value, CONTRACT_LAST, preferred_element_type=jnp.float32)
        store_tiles(outgoing.at[k], local_p.astype(jnp.bfloat16))


def first(grads, error, q_start, replicas, flip):
    rows, hidden = grads.shape
    rank = q_start.shape[0]
    block = rows // replicas
    half = replicas // 2
    return pl.pallas_call(
        functools.partial(first_kernel, replicas, flip),
        in_specs=[pl.BlockSpec(memory_space=pl.ANY)] * 3,
        out_specs=[pl.BlockSpec(memory_space=pltpu.VMEM)] * 2,
        out_shape=[
            pltpu.VMEM((half * block, hidden), jnp.bfloat16),
            pltpu.VMEM((half, block // LANES * rank, LANES), jnp.bfloat16),
        ],
        scratch_shapes=[
            pltpu.VMEM((2, half, block, hidden), jnp.bfloat16),
            pltpu.VMEM(q_start.shape, jnp.float32),
            pltpu.SemaphoreType.DMA((2, half)),
            pltpu.SemaphoreType.DMA(()),
        ],
        compiler_params=pltpu.CompilerParams(vmem_limit_bytes=53 * MIB),
        cost_estimate=pl.CostEstimate(
            flops=rows * hidden * rank, bytes_accessed=2 * rows * hidden, transcendentals=0
        ),
        name="compensate_and_left",
    )(grads, error, q_start)


def partner(value, by, size):
    return lax.ppermute(value, "dp", [(i, i ^ by) for i in range(size)])


def first_share(grads, error, q_start, replicas):
    other, theirs = first(grads, error, q_start, replicas, 1)
    arrived = partner(theirs, 1, replicas)
    own, mine = first(grads, error, q_start, replicas, 0)
    pairs = [
        arrived[k].astype(jnp.float32) + mine[k].astype(jnp.float32) for k in range(replicas // 2)
    ]
    total = pairs[0]
    for value in [
        partner(pairs[k].astype(jnp.bfloat16), 2 * k, replicas) for k in range(1, replicas // 2)
    ]:
        total = total + value.astype(jnp.float32)
    return (own, other), total


def inverse_lower(gram):
    rank = gram.shape[0]
    row = lax.broadcasted_iota(jnp.int32, (SUBLANES, 2 * rank), 0)
    across = lax.broadcasted_iota(jnp.int32, (SUBLANES, 2 * rank), 1)
    both = jnp.concatenate([jnp.zeros((rank, rank), jnp.float32), gram], axis=1)
    starts = range(0, rank, SUBLANES)
    tiles = [
        jnp.where(across == row + at, 1.0, both[at : at + SUBLANES, :]) for at in starts
    ]
    inverse = []
    for top, base in enumerate(starts):
        columns = [
            [
                jnp.broadcast_to(tile[:, rank + k : rank + k + 1], tile.shape)
                for tile in tiles[top:]
            ]
            for k in range(base, base + SUBLANES)
        ]
        for j in range(SUBLANES):
            head = columns[j][0]
            reciprocal = 1.0 / head[j : j + 1, :]
            pivot_row = tiles[top][j : j + 1, :]
            for at in range(len(columns[j])):
                factor = columns[j][at] * reciprocal
                if at == 0:
                    factor = jnp.where(row > j, factor, 0.0)
                for i in range(j + 1, SUBLANES):
                    columns[i][at] = columns[i][at] - factor * head[i : i + 1, :]
                tiles[top + at] = tiles[top + at] - factor * pivot_row
        done = tiles[top]
        pivots = jnp.sum(
            jnp.where(across == row + (rank + base), done, 0.0), axis=1, keepdims=True
        )
        inverse.append(done[:, :rank] * lax.rsqrt(pivots))
    return jnp.concatenate(inverse, axis=0)


def columns_of(arrived, tiles, x, first_tile, count):
    rank = arrived.shape[1] // tiles
    parts = []
    for at in range(first_tile, first_tile + count):
        block, tile = divmod(at, tiles)
        parts.append(arrived[2 * block + x, tile * rank : (tile + 1) * rank, :])
    return jnp.concatenate(parts, axis=1)


def right_kernel(tiles, arrived, halves, term, inverse_out=None):
    x = lax.axis_index("dp") & 1
    count = arrived.shape[0] // 2 * tiles
    factors = [columns_of(arrived, tiles, x ^ flip, 0, count) for flip in range(2)]
    factor_p = jnp.concatenate(factors, axis=1)
    gram = lax.dot_general(
        factor_p, factor_p, CONTRACT_LAST, preferred_element_type=jnp.float32
    )
    product = sum(
        jnp.dot(factor, half[...], preferred_element_type=jnp.float32)
        for factor, half in zip(factors, halves)
    )
    inverse = inverse_lower(gram)
    if inverse_out is not None:
        inverse_out[...] = inverse
    term[...] = fine_product(inverse, product, 1).astype(jnp.bfloat16)


def right(arrived, halves, rank, keep):
    out_shape = [pltpu.VMEM((rank, halves[0].shape[1]), jnp.bfloat16)]
    in_vmem = pl.BlockSpec(memory_space=pltpu.VMEM)
    if keep:
        out_shape.append(pltpu.VMEM((rank, rank), jnp.float32))
    return pl.pallas_call(
        functools.partial(right_kernel, arrived.shape[1] // rank),
        in_specs=[in_vmem, (in_vmem, in_vmem)],
        out_specs=[in_vmem] * len(out_shape),
        out_shape=out_shape,
        compiler_params=pltpu.CompilerParams(vmem_limit_bytes=24 * MIB),
        name="orthogonalize_and_right",
    )(arrived, halves)


def last_partner(value, step, size, detour):
    experts = lax.axis_size("expert")
    pairs = []
    for i in range(size):
        for e in range(experts):
            other = i ^ (step ^ 2 if detour and e % 2 else step)
            pairs.append((i * experts + e, other * experts + e))
    return lax.ppermute(value, ("dp", "expert"), pairs)


def addends(term, size, detour):
    one, two, three, four = [
        part.astype(jnp.float32) for part in [term] + [partner(term, by, size) for by in (1, 2, 3)]
    ]
    term = ((one + two) + (three + four)).astype(jnp.bfloat16)
    step = 4
    while 2 * step < size:
        term = (term.astype(jnp.float32) + partner(term, step, size).astype(jnp.float32)).astype(
            jnp.bfloat16
        )
        step *= 2
    return [term, last_partner(term, step, size, detour)]


def sum_of(parts):
    one, two = [part[...].astype(jnp.float32) for part in parts]
    return one + two


def left_kernel(parts, halves, bucket, outgoing):
    replicas = outgoing.shape[0]
    block = 2 * halves[0].shape[0] // replicas
    x = lax.axis_index("dp") & 1
    outgoing[:, -bucket.shape[1] :, :] = bucket[...].astype(jnp.bfloat16)
    factor_q = sum_of(parts) / replicas
    scale = 1.0 / jnp.sqrt(jnp.sum(factor_q * factor_q, axis=1, keepdims=True) + 1e-06)
    q_half = factor_q.astype(jnp.bfloat16)
    for flip, half in enumerate(halves):
        for j in range(replicas // 2):
            local_p = lax.dot_general(
                q_half,
                half[j * block : (j + 1) * block, :],
                CONTRACT_LAST,
                preferred_element_type=jnp.float32,
            )
            store_tiles(outgoing.at[2 * j + (x ^ flip)], (local_p * scale).astype(jnp.bfloat16))


def left(parts, halves, bucket):
    replicas = bucket.shape[0]
    tall = 2 * halves[0].shape[0] // replicas * parts[0].shape[0] // LANES + bucket.shape[1]
    in_vmem = pl.BlockSpec(memory_space=pltpu.VMEM)
    return pl.pallas_call(
        left_kernel,
        in_specs=[[in_vmem] * len(parts), (in_vmem, in_vmem), in_vmem],
        out_specs=in_vmem,
        out_shape=pltpu.VMEM((replicas, tall, LANES), jnp.bfloat16),
        compiler_params=pltpu.CompilerParams(vmem_limit_bytes=24 * MIB),
        name="normalize_and_left",
    )(parts, halves, bucket)


def last_kernel(
    replicas, parts, inverse, arrived, halves, share,
    update, new_error, bucket_mean, update_held, error_held, sems, bucket_sem,
):
    tall = bucket_mean.shape[0]
    there = pl.ds(share.shape[0] - tall, tall)
    copies = [pltpu.make_async_copy(share.at[there], bucket_mean, bucket_sem)]
    copies[0].start()
    rows, hidden = halves[0].shape
    tiles = 2 * rows // replicas // LANES
    x = lax.axis_index("dp") & 1
    right = fine_product(inverse[...], sum_of(parts) / replicas, 0)
    right = jnp.concatenate(three_parts(right), axis=0)
    for flip, half in enumerate(halves):
        for i, (at, size) in enumerate(pieces(rows, flip == 0)):
            where = slice(at, at + size)
            p_block = columns_of(arrived, tiles, x ^ flip, at // LANES, size // LANES).T
            block = jnp.dot(
                jnp.concatenate([p_block] * 3, axis=1), right, preferred_element_type=jnp.float32
            )
            update_held[flip, where, :] = block
            error_held[flip, where, :] = (half[where, :].astype(jnp.float32) - block).astype(
                jnp.bfloat16
            )
            there = pl.ds(pl.multiple_of((x ^ flip) * rows + at, LANES), size)
            for j, (held, out) in enumerate(((update_held, update), (error_held, new_error))):
                copies.append(
                    pltpu.make_async_copy(
                        held.at[flip, pl.ds(at, size)], out.at[there], sems.at[j, flip, i]
                    )
                )
                copies[-1].start(priority=j)
    for copy in copies:
        copy.wait()


def last(parts, inverse, arrived, halves, share, replicas, bucket_tall):
    rows, hidden = halves[0].shape
    in_vmem = pl.BlockSpec(memory_space=pltpu.VMEM)
    return pl.pallas_call(
        functools.partial(last_kernel, replicas),
        in_specs=[[in_vmem] * len(parts), in_vmem, in_vmem, (in_vmem, in_vmem), in_vmem],
        out_specs=[pl.BlockSpec(memory_space=pl.ANY)] * 3,
        out_shape=[
            jax.ShapeDtypeStruct((2 * rows, hidden), jnp.float32),
            jax.ShapeDtypeStruct((2 * rows, hidden), jnp.bfloat16),
            jax.ShapeDtypeStruct((bucket_tall, LANES), jnp.float32),
        ],
        scratch_shapes=[
            pltpu.VMEM((2, rows, hidden), jnp.float32),
            pltpu.VMEM((2, rows, hidden), jnp.bfloat16),
            pltpu.SemaphoreType.DMA((2, 2, len(pieces(rows, True)))),
            pltpu.SemaphoreType.DMA(()),
        ],
        compiler_params=pltpu.CompilerParams(vmem_limit_bytes=40 * MIB),
        name="update_and_error",
    )(parts, inverse, arrived, halves, share)


def on_device(grads, error, q_start, bucket):
    replicas = lax.axis_size("dp")
    rows = grads.shape[1]
    rank = q_start.shape[1]
    bucket = bucket.reshape(replicas, -1, LANES)
    tall = rows // replicas * rank // LANES
    halves, share = first_share(grads[0], error[0], q_start.T, replicas)
    for step in range(ITERS):
        if step > 0:
            share = jnp.sum(exchange(outgoing).astype(jnp.float32), axis=0)
        share = share / replicas
        factor_p = everywhere(share[:tall].astype(jnp.bfloat16), replicas)
        term, *inverse = right(factor_p, halves, rank, step + 1 == ITERS)
        parts = addends(term, replicas, step + 1 < ITERS)
        if step + 1 < ITERS:
            outgoing = left(parts, halves, bucket)
    update, new_error, bucket_mean = last(
        parts, inverse[0], factor_p, halves, share, replicas, bucket.shape[1]
    )
    return (update, new_error[None], bucket_mean.reshape(-1))


def solution(mesh):
    return jax.shard_map(
        on_device,
        mesh=mesh,
        in_specs=(
            P("dp", None, "expert"),
            P("dp", None, "expert"),
            P("expert", None),
            P("dp", "expert"),
        ),
        out_specs=(P(None, "expert"), P("dp", None, "expert"), P(("expert", "dp"))),
        check_vma=False,
    )
```

```python
import functools

import jax
import jax.numpy as jnp
from jax import lax
from jax.experimental import pallas as pl
from jax.experimental.pallas import tpu as pltpu
from jax.sharding import PartitionSpec as P

ITERS = 2
LANES = 128
SUBLANES = 8
MIB = 1024 * 1024
CONTRACT_LAST = (((1,), (1,)), ((), ()))


def exchange(chunks):
    return lax.all_to_all(chunks, "dp", split_axis=0, concat_axis=0, tiled=True)


def everywhere(share, size):
    return exchange(jnp.broadcast_to(share, (size,) + share.shape))


def three_parts(value):
    high = value.astype(jnp.bfloat16)
    rest = value - high.astype(jnp.float32)
    middle = rest.astype(jnp.bfloat16)
    low = (rest - middle.astype(jnp.float32)).astype(jnp.bfloat16)
    return high, middle, low


def pieces(rows, grow):
    sizes = [4 * LANES] * (rows // (4 * LANES))
    if grow:
        sizes[:1] = [LANES, LANES, 2 * LANES]
    return [(sum(sizes[:i]), size) for i, size in enumerate(sizes)]


def store_tiles(chunk, value):
    rank, columns = value.shape
    for tile in range(columns // LANES):
        chunk[tile * rank : (tile + 1) * rank, :] = value[:, tile * LANES : (tile + 1) * LANES]


def fine_product(left, right, axis):
    lh, lm, ll = three_parts(left)
    rh, rm, rl = three_parts(right)
    return lax.dot_general(
        jnp.concatenate([lh, lm, ll, lh, lm, lh], axis=axis),
        jnp.concatenate([rh, rh, rh, rm, rm, rl], axis=0),
        (((axis,), (0,)), ((), ())),
        preferred_element_type=jnp.float32,
    )


def first_kernel(replicas, flip, grads, error, q_start, compensated, outgoing, *scratch):
    landed, q_landed, sems, q_sem = scratch
    fetch_q = pltpu.make_async_copy(q_start, q_landed, q_sem)
    fetch_q.start()
    me = lax.axis_index("dp")
    half = replicas // 2
    block = grads.shape[0] // replicas
    starts, copies = [], []
    for k in range(half):
        starts.append(pl.multiple_of(((me >> 1) ^ k) * block, block))
        there = pl.multiple_of(((me & 1) ^ flip) * (half * block) + starts[k], block)
        for j, array in enumerate((grads, error)):
            copies.append(
                pltpu.make_async_copy(
                    array.at[pl.ds(there, block)], landed.at[j, k], sems.at[j, k]
                )
            )
            copies[-1].start(priority=j)
    fetch_q.wait()
    q_half = q_landed[...].astype(jnp.bfloat16)
    for k in range(half):
        copies[2 * k].wait()
        copies[2 * k + 1].wait()
        value = (landed[0, k].astype(jnp.float32) + landed[1, k].astype(jnp.float32)).astype(
            jnp.bfloat16
        )
        compensated[pl.ds(starts[k], block), :] = value
        local_p = lax.dot_general(q_half, value, CONTRACT_LAST, preferred_element_type=jnp.float32)
        store_tiles(outgoing.at[k], local_p.astype(jnp.bfloat16))


def first(grads, error, q_start, replicas, flip):
    rows, hidden = grads.shape
    rank = q_start.shape[0]
    block = rows // replicas
    half = replicas // 2
    return pl.pallas_call(
        functools.partial(first_kernel, replicas, flip),
        in_specs=[pl.BlockSpec(memory_space=pl.ANY)] * 3,
        out_specs=[pl.BlockSpec(memory_space=pltpu.VMEM)] * 2,
        out_shape=[
            pltpu.VMEM((half * block, hidden), jnp.bfloat16),
            pltpu.VMEM((half, block // LANES * rank, LANES), jnp.bfloat16),
        ],
        scratch_shapes=[
            pltpu.VMEM((2, half, block, hidden), jnp.bfloat16),
            pltpu.VMEM(q_start.shape, jnp.float32),
            pltpu.SemaphoreType.DMA((2, half)),
            pltpu.SemaphoreType.DMA(()),
        ],
        compiler_params=pltpu.CompilerParams(vmem_limit_bytes=53 * MIB),
        cost_estimate=pl.CostEstimate(
            flops=rows * hidden * rank, bytes_accessed=2 * rows * hidden, transcendentals=0
        ),
        name="compensate_and_left",
    )(grads, error, q_start)


def partner(value, by, size):
    return lax.ppermute(value, "dp", [(i, i ^ by) for i in range(size)])


def first_share(grads, error, q_start, replicas):
    other, theirs = first(grads, error, q_start, replicas, 1)
    arrived = partner(theirs, 1, replicas)
    own, mine = first(grads, error, q_start, replicas, 0)
    pairs = [
        arrived[k].astype(jnp.float32) + mine[k].astype(jnp.float32) for k in range(replicas // 2)
    ]
    total = pairs[0]
    for value in [
        partner(pairs[k].astype(jnp.bfloat16), 2 * k, replicas) for k in range(1, replicas // 2)
    ]:
        total = total + value.astype(jnp.float32)
    return (own, other), total


def inverse_lower(gram):
    rank = gram.shape[0]
    row = lax.broadcasted_iota(jnp.int32, (SUBLANES, 2 * rank), 0)
    across = lax.broadcasted_iota(jnp.int32, (SUBLANES, 2 * rank), 1)
    both = jnp.concatenate([jnp.zeros((rank, rank), jnp.float32), gram], axis=1)
    starts = range(0, rank, SUBLANES)
    tiles = [
        jnp.where(across == row + at, 1.0, both[at : at + SUBLANES, :]) for at in starts
    ]
    inverse = []
    for top, base in enumerate(starts):
        columns = [
            [
                jnp.broadcast_to(tile[:, rank + k : rank + k + 1], tile.shape)
                for tile in tiles[top:]
            ]
            for k in range(base, base + SUBLANES)
        ]
        for j in range(SUBLANES):
            head = columns[j][0]
            reciprocal = 1.0 / head[j : j + 1, :]
            pivot_row = tiles[top][j : j + 1, :]
            for at in range(len(columns[j])):
                factor = columns[j][at] * reciprocal
                if at == 0:
                    factor = jnp.where(row > j, factor, 0.0)
                for i in range(j + 1, SUBLANES):
                    columns[i][at] = columns[i][at] - factor * head[i : i + 1, :]
                tiles[top + at] = tiles[top + at] - factor * pivot_row
        done = tiles[top]
        pivots = jnp.sum(
            jnp.where(across == row + (rank + base), done, 0.0), axis=1, keepdims=True
        )
        inverse.append(done[:, :rank] * lax.rsqrt(pivots))
    return jnp.concatenate(inverse, axis=0)


def columns_of(arrived, tiles, x, first_tile, count):
    rank = arrived.shape[1] // tiles
    parts = []
    for at in range(first_tile, first_tile + count):
        block, tile = divmod(at, tiles)
        parts.append(arrived[2 * block + x, tile * rank : (tile + 1) * rank, :])
    return jnp.concatenate(parts, axis=1)


def right_kernel(tiles, arrived, halves, term, inverse_out=None):
    x = lax.axis_index("dp") & 1
    count = arrived.shape[0] // 2 * tiles
    factors = [columns_of(arrived, tiles, x ^ flip, 0, count) for flip in range(2)]
    factor_p = jnp.concatenate(factors, axis=1)
    gram = lax.dot_general(
        factor_p, factor_p, CONTRACT_LAST, preferred_element_type=jnp.float32
    )
    product = sum(
        jnp.dot(factor, half[...], preferred_element_type=jnp.float32)
        for factor, half in zip(factors, halves)
    )
    inverse = inverse_lower(gram)
    if inverse_out is not None:
        inverse_out[...] = inverse
    term[...] = fine_product(inverse, product, 1).astype(jnp.bfloat16)


def right(arrived, halves, rank, keep):
    out_shape = [pltpu.VMEM((rank, halves[0].shape[1]), jnp.bfloat16)]
    in_vmem = pl.BlockSpec(memory_space=pltpu.VMEM)
    if keep:
        out_shape.append(pltpu.VMEM((rank, rank), jnp.float32))
    return pl.pallas_call(
        functools.partial(right_kernel, arrived.shape[1] // rank),
        in_specs=[in_vmem, (in_vmem, in_vmem)],
        out_specs=[in_vmem] * len(out_shape),
        out_shape=out_shape,
        compiler_params=pltpu.CompilerParams(vmem_limit_bytes=24 * MIB),
        name="orthogonalize_and_right",
    )(arrived, halves)


def last_partner(value, step, size):
    experts = lax.axis_size("expert")
    pairs = []
    for i in range(size):
        for e in range(experts):
            other = i ^ (step ^ 2 if e % 2 else step)
            pairs.append((i * experts + e, other * experts + e))
    return lax.ppermute(value, ("dp", "expert"), pairs)


def addends(term, size):
    one, two, three, four = [
        part.astype(jnp.float32) for part in [term] + [partner(term, by, size) for by in (1, 2, 3)]
    ]
    term = ((one + two) + (three + four)).astype(jnp.bfloat16)
    step = 4
    while 2 * step < size:
        term = (term.astype(jnp.float32) + partner(term, step, size).astype(jnp.float32)).astype(
            jnp.bfloat16
        )
        step *= 2
    return [term, last_partner(term, step, size)]


def sum_of(parts):
    one, two = [part[...].astype(jnp.float32) for part in parts]
    return one + two


def left_kernel(parts, halves, bucket, outgoing):
    replicas = outgoing.shape[0]
    block = 2 * halves[0].shape[0] // replicas
    x = lax.axis_index("dp") & 1
    outgoing[:, -bucket.shape[1] :, :] = bucket[...].astype(jnp.bfloat16)
    factor_q = sum_of(parts) / replicas
    scale = 1.0 / jnp.sqrt(jnp.sum(factor_q * factor_q, axis=1, keepdims=True) + 1e-06)
    q_half = factor_q.astype(jnp.bfloat16)
    for flip, half in enumerate(halves):
        for j in range(replicas // 2):
            local_p = lax.dot_general(
                q_half,
                half[j * block : (j + 1) * block, :],
                CONTRACT_LAST,
                preferred_element_type=jnp.float32,
            )
            store_tiles(outgoing.at[2 * j + (x ^ flip)], (local_p * scale).astype(jnp.bfloat16))


def left(parts, halves, bucket):
    replicas = bucket.shape[0]
    tall = 2 * halves[0].shape[0] // replicas * parts[0].shape[0] // LANES + bucket.shape[1]
    in_vmem = pl.BlockSpec(memory_space=pltpu.VMEM)
    return pl.pallas_call(
        left_kernel,
        in_specs=[[in_vmem] * len(parts), (in_vmem, in_vmem), in_vmem],
        out_specs=in_vmem,
        out_shape=pltpu.VMEM((replicas, tall, LANES), jnp.bfloat16),
        compiler_params=pltpu.CompilerParams(vmem_limit_bytes=24 * MIB),
        name="normalize_and_left",
    )(parts, halves, bucket)


def last_kernel(
    replicas, parts, inverse, arrived, halves, share,
    update, new_error, bucket_mean, update_held, error_held, sems, bucket_sem,
):
    tall = bucket_mean.shape[0]
    there = pl.ds(share.shape[0] - tall, tall)
    copies = [pltpu.make_async_copy(share.at[there], bucket_mean, bucket_sem)]
    copies[0].start()
    rows, hidden = halves[0].shape
    tiles = 2 * rows // replicas // LANES
    x = lax.axis_index("dp") & 1
    right = fine_product(inverse[...], sum_of(parts) / replicas, 0)
    right = jnp.concatenate(three_parts(right), axis=0)
    for flip, half in enumerate(halves):
        for i, (at, size) in enumerate(pieces(rows, flip == 0)):
            where = slice(at, at + size)
            p_block = columns_of(arrived, tiles, x ^ flip, at // LANES, size // LANES).T
            block = jnp.dot(
                jnp.concatenate([p_block] * 3, axis=1), right, preferred_element_type=jnp.float32
            )
            update_held[flip, where, :] = block
            error_held[flip, where, :] = (half[where, :].astype(jnp.float32) - block).astype(
                jnp.bfloat16
            )
            there = pl.ds(pl.multiple_of((x ^ flip) * rows + at, LANES), size)
            for j, (held, out) in enumerate(((update_held, update), (error_held, new_error))):
                copies.append(
                    pltpu.make_async_copy(
                        held.at[flip, pl.ds(at, size)], out.at[there], sems.at[j, flip, i]
                    )
                )
                copies[-1].start(priority=j)
    for copy in copies:
        copy.wait()


def last(parts, inverse, arrived, halves, share, replicas, bucket_tall):
    rows, hidden = halves[0].shape
    in_vmem = pl.BlockSpec(memory_space=pltpu.VMEM)
    return pl.pallas_call(
        functools.partial(last_kernel, replicas),
        in_specs=[[in_vmem] * len(parts), in_vmem, in_vmem, (in_vmem, in_vmem), in_vmem],
        out_specs=[pl.BlockSpec(memory_space=pl.ANY)] * 3,
        out_shape=[
            jax.ShapeDtypeStruct((2 * rows, hidden), jnp.float32),
            jax.ShapeDtypeStruct((2 * rows, hidden), jnp.bfloat16),
            jax.ShapeDtypeStruct((bucket_tall, LANES), jnp.float32),
        ],
        scratch_shapes=[
            pltpu.VMEM((2, rows, hidden), jnp.float32),
            pltpu.VMEM((2, rows, hidden), jnp.bfloat16),
            pltpu.SemaphoreType.DMA((2, 2, len(pieces(rows, True)))),
            pltpu.SemaphoreType.DMA(()),
        ],
        compiler_params=pltpu.CompilerParams(vmem_limit_bytes=40 * MIB),
        name="update_and_error",
    )(parts, inverse, arrived, halves, share)


def on_device(grads, error, q_start, bucket):
    replicas = lax.axis_size("dp")
    rows = grads.shape[1]
    rank = q_start.shape[1]
    bucket = bucket.reshape(replicas, -1, LANES)
    tall = rows // replicas * rank // LANES
    halves, share = first_share(grads[0], error[0], q_start.T, replicas)
    for step in range(ITERS):
        if step > 0:
            share = jnp.sum(exchange(outgoing).astype(jnp.float32), axis=0)
        share = share / replicas
        factor_p = everywhere(share[:tall].astype(jnp.bfloat16), replicas)
        term, *inverse = right(factor_p, halves, rank, step + 1 == ITERS)
        parts = addends(term, replicas)
        if step + 1 < ITERS:
            outgoing = left(parts, halves, bucket)
    update, new_error, bucket_mean = last(
        parts, inverse[0], factor_p, halves, share, replicas, bucket.shape[1]
    )
    return (update, new_error[None], bucket_mean.reshape(-1))


def solution(mesh):
    return jax.shard_map(
        on_device,
        mesh=mesh,
        in_specs=(
            P("dp", None, "expert"),
            P("dp", None, "expert"),
            P("expert", None),
            P("dp", "expert"),
        ),
        out_specs=(P(None, "expert"), P("dp", None, "expert"), P(("expert", "dp"))),
        check_vma=False,
    )
```
